32 devices in a mesh: wide: 8 (over z, y), narrow: 4 (over x, core).
Axes of the slice: x: 2, y: 2, z: 4, core: 2. Of those that a mesh axis runs over, the one named last changes fastest.
Arguments:
- tokens: bfloat16 [32768, 768], P(('wide', 'narrow')), may hold values from -6 to 6
- cotangent: bfloat16 [32768, 768], P(('wide', 'narrow')), may hold values from -6 to 6
- lengths: int32 [64], P(('wide', 'narrow')), may hold values from 1 to 512, as said below
- buckets: int32 [32], P(('wide', 'narrow')), may hold values from 0 to 2, as said below
- w_query: bfloat16 [768, 768], P(('wide', 'narrow')), may hold values from -0.21875 to 0.21875
- w_key: bfloat16 [768, 768], P(('wide', 'narrow')), may hold values from -0.21875 to 0.21875
- w_value: bfloat16 [768, 768], P(('wide', 'narrow')), may hold values from -0.21875 to 0.21875
- w_output: bfloat16 [768, 768], P(('wide', 'narrow')), may hold values from -0.875 to 0.875
- b_query: bfloat16 [768], P(('wide', 'narrow')), may hold values from -3 to 3
- b_value: bfloat16 [768], P(('wide', 'narrow')), may hold values from -3 to 3
- b_output: bfloat16 [768], P(('wide', 'narrow')), may hold values from -3 to 3
- gain_attn: bfloat16 [768], P(('wide', 'narrow')), may hold values from 0.5 to 1.5
- shift_attn: bfloat16 [768], P(('wide', 'narrow')), may hold values from -2 to 2
- w_inner: bfloat16 [768, 3072], P(('wide', 'narrow')), may hold values from -0.21875 to 0.21875
- b_inner: bfloat16 [3072], P(('wide', 'narrow')), may hold values from -3 to 3
- w_outer: bfloat16 [3072, 768], P(('wide', 'narrow')), may hold values from -0.109375 to 0.109375
- b_outer: bfloat16 [768], P(('wide', 'narrow')), may hold values from -3 to 3
- gain_ffn: bfloat16 [768], P(('wide', 'narrow')), may hold values from 0.5 to 1.5
- shift_ffn: bfloat16 [768], P(('wide', 'narrow')), may hold values from -2 to 2
Outputs:
- layer_out: bfloat16 [32768, 768], P(('wide', 'narrow'))
- grad_tokens: bfloat16 [32768, 768], P(('wide', 'narrow'))
- grad_w_query: float32 [768, 768], P(('wide', 'narrow'))
- grad_w_key: float32 [768, 768], P(('wide', 'narrow'))
- grad_w_value: float32 [768, 768], P(('wide', 'narrow'))
- grad_w_output: float32 [768, 768], P(('wide', 'narrow'))
- grad_b_query: float32 [768], P(('wide', 'narrow'))
- grad_b_value: float32 [768], P(('wide', 'narrow'))
- grad_b_output: float32 [768], P(('wide', 'narrow'))
- grad_gain_attn: float32 [768], P(('wide', 'narrow'))
- grad_shift_attn: float32 [768], P(('wide', 'narrow'))
- grad_w_inner: float32 [768, 3072], P(('wide', 'narrow'))
- grad_b_inner: float32 [3072], P(('wide', 'narrow'))
- grad_w_outer: float32 [3072, 768], P(('wide', 'narrow'))
- grad_b_outer: float32 [768], P(('wide', 'narrow'))
- grad_gain_ffn: float32 [768], P(('wide', 'narrow'))
- grad_shift_ffn: float32 [768], P(('wide', 'narrow'))
The draws below stay inside these ranges and needn't reach their ends.
Inputs may be any that keep to these rules, and one draw needn't show every extreme that they name: `lengths`: some sequence has length 512 in every draw. `buckets`: some device has bucket 2 in every draw.
All inputs are finite; a program needn't handle non-finite values.
Results may differ from the reference program's by a relative error of at most 0.014.
Values may be sent and summed in bfloat16 or wider, within the bound.
No kernel may reach another device: no remote copies, remote signals or barrier semaphores. Data moves between devices by JAX's collectives and lax.ppermute only.
A program may use at most 192 MiB of HBM per device.

```python
import math
import jax
import jax.numpy as jnp
from jax import lax

D = 768
H = 12
HD = 64
FF = 3072
BLEN = 128
MAXLEN = 512
SEQ_DEV = 2
SEQS = 64
TOKENS = 32768
DEVICES = 32


def draw_lengths(key, part):
    key = jax.random.fold_in(key, 5)
    samples = jax.random.randint(jax.random.fold_in(key, 1), (2, SEQS), 1, MAXLEN + 1)
    longest = jax.random.randint(jax.random.fold_in(key, 2), (), 0, SEQS)
    shortest = jnp.min(samples, axis=0)
    return jnp.where(jnp.arange(SEQS) == longest, MAXLEN, shortest).astype(jnp.int32)


def draw_buckets(key, part):
    key = jax.random.fold_in(key, 9)
    samples = jax.random.randint(jax.random.fold_in(key, 1), (DEVICES,), 0, 3)
    widest = jax.random.randint(jax.random.fold_in(key, 2), (), 0, DEVICES)
    return jnp.where(jnp.arange(DEVICES) == widest, 2, samples).astype(jnp.int32)


def spiked(result, rng, source, target, parts, factor):
    owner, partner = [(jnp.arange(result.shape[dim]) // (result.shape[dim] // parts)).reshape([-1 if axis == dim else 1 for axis in range(result.ndim)]) for dim in (source, target)]
    chosen = jax.random.permutation(rng, parts)[partner]
    strong = (owner == chosen) | (owner == (partner + parts // 2) % parts)
    return jnp.where(strong, factor * result, result)


def block_scale(stream_key, shape, cuts, least, largest):
    level, own = 1.0, jax.random.fold_in(stream_key, 6)
    for axis_at, blocks in cuts:
        draws = jnp.exp(jax.random.uniform(jax.random.fold_in(own, axis_at), (blocks,), jnp.float32, least / len(cuts), largest / len(cuts)))
        level = level * jnp.repeat(draws, shape[axis_at] // blocks).reshape([-1 if axis == axis_at else 1 for axis in range(len(shape))])
    return level


def normal_values(key, extent, scale, most, split=(), kind=jnp.bfloat16):
    values = scale * jax.random.normal(key, extent, jnp.float32)
    if split:
        values = values * block_scale(key, extent, split, -0.22, 0.18)
    return jnp.clip(values, -most, most).astype(kind)


def gaussian_with(stream_key, extent, scale, bound, pieces, heavy, kind=jnp.bfloat16):
    result = scale * jax.random.normal(stream_key, extent, jnp.float32)
    if pieces:
        result = result * block_scale(stream_key, extent, pieces, -0.22, 0.18)
    return jnp.clip(spiked(result, jax.random.fold_in(stream_key, 3), *heavy), -bound, bound).astype(kind)


def setup_inputs(seed: int = 0) -> dict:
    keys = jax.random.split(jax.random.key(seed), 20)
    tokens = gaussian_with(keys[0], (TOKENS, D), 1.0, 6.0, ((0, 32),), (0, 1, 32, 2.75))
    cotangent = normal_values(keys[1], (TOKENS, D), 1.0, 6.0, ((0, 32),))
    lengths = draw_lengths(jax.random.fold_in(keys[19], 71), 0)
    buckets = draw_buckets(jax.random.fold_in(keys[19], 71), 0)
    w_query = normal_values(keys[4], (D, D), D ** -0.5, 0.21875, ((0, 32),))
    w_key = normal_values(keys[5], (D, D), D ** -0.5, 0.21875, ((0, 32),))
    w_value = normal_values(keys[6], (D, D), D ** -0.5, 0.21875, ((0, 32),))
    w_output = normal_values(keys[7], (D, D), (D // 16) ** -0.5, 0.875, ((0, 32),))
    b_query = normal_values(keys[8], (D,), 0.5, 3.0, ((0, 32),))
    b_value = normal_values(keys[9], (D,), 0.5, 3.0, ((0, 32),))
    b_output = normal_values(keys[10], (D,), 0.5, 3.0, ((0, 32),))
    gain_attn = jnp.clip(1.0 + 0.1 * jax.random.normal(keys[11], (D,), jnp.float32), 0.5, 1.5).astype(jnp.bfloat16)
    shift_attn = normal_values(keys[12], (D,), 0.3, 2.0, ((0, 32),))
    w_inner = normal_values(keys[13], (D, FF), D ** -0.5, 0.21875, ((0, 32),))
    b_inner = normal_values(keys[14], (FF,), 0.5, 3.0, ((0, 32),))
    w_outer = normal_values(keys[15], (FF, D), FF ** -0.5, 0.109375, ((0, 32),))
    b_outer = normal_values(keys[16], (D,), 0.5, 3.0, ((0, 32),))
    gain_ffn = jnp.clip(1.0 + 0.1 * jax.random.normal(keys[17], (D,), jnp.float32), 0.5, 1.5).astype(jnp.bfloat16)
    shift_ffn = normal_values(keys[18], (D,), 0.3, 2.0, ((0, 32),))
    return dict(tokens=tokens, cotangent=cotangent, lengths=lengths, buckets=buckets, w_query=w_query, w_key=w_key, w_value=w_value, w_output=w_output, b_query=b_query, b_value=b_value, b_output=b_output, gain_attn=gain_attn, shift_attn=shift_attn, w_inner=w_inner, b_inner=b_inner, w_outer=w_outer, b_outer=b_outer, gain_ffn=gain_ffn, shift_ffn=shift_ffn)


HIGH = lax.Precision.HIGHEST
EPSILON = 1e-12

@jax.custom_vjp
def low(v):
    return lax.optimization_barrier(v.astype(jnp.bfloat16)).astype(jnp.float32)

@jax.custom_vjp
def low_back(v):
    return v

def low_keep(v):
    return (low(v), None)

def low_pass(kept, grad):
    return (grad,)

def back_keep(v):
    return (v, None)

def back_low(kept, grad):
    return (low(grad),)
low.defvjp(low_keep, low_pass)
low_back.defvjp(back_keep, back_low)

def matmul(left_side, right_side):
    return jnp.dot(left_side, right_side, precision=HIGH, preferred_element_type=jnp.float32)

def layer_norm(hidden, gain, shift):
    center = hidden - lax.optimization_barrier(jnp.mean(hidden, axis=-1, keepdims=True))
    variance = lax.optimization_barrier(jnp.mean(center * center, axis=-1, keepdims=True))
    return center * lax.rsqrt(variance + EPSILON) * gain + shift

def one_sequence(params, inputs, key_limit):
    w_query, w_key, w_value, w_output, b_query, b_value, b_output, gain_attn, shift_attn, w_inner, b_inner, w_outer, b_outer, gain_ffn, shift_ffn = params
    queries = low(low_back(matmul(inputs, w_query) + b_query))
    key_rows = low(low_back(matmul(inputs, w_key)))
    value_rows = low(low_back(matmul(inputs, w_value) + b_value))
    query_heads = queries.reshape(MAXLEN, H, HD)
    key_heads = key_rows.reshape(MAXLEN, H, HD)
    value_heads = value_rows.reshape(MAXLEN, H, HD)
    scores = low_back(jnp.einsum('qhd,khd->hqk', query_heads, key_heads, precision=HIGH) * HD ** (-0.5))
    places = jnp.arange(MAXLEN, dtype=jnp.int32)
    scores = jnp.where((places < key_limit)[None, None, :], scores, -1e+30)
    row_max = lax.optimization_barrier(jnp.max(scores, axis=-1, keepdims=True))
    powers = jnp.exp(scores - row_max)
    attention = low(powers / lax.optimization_barrier(jnp.sum(powers, axis=-1, keepdims=True)))
    attended = jnp.einsum('hqk,khd->qhd', attention, value_heads, precision=HIGH).reshape(MAXLEN, D)
    attended = low(low_back(attended))
    first_sum = inputs + low_back(matmul(attended, w_output) + b_output)
    normed = layer_norm(first_sum, gain_attn, shift_attn)
    hidden = low_back(matmul(low(normed), w_inner) + b_inner)
    active = low(jax.nn.gelu(hidden, approximate=False))
    second_sum = normed + low_back(matmul(active, w_outer) + b_outer)
    return layer_norm(second_sum, gain_ffn, shift_ffn)

def reference(tokens, cotangent, lengths, buckets, w_query, w_key, w_value, w_output, b_query, b_value, b_output, gain_attn, shift_attn, w_inner, b_inner, w_outer, b_outer, gain_ffn, shift_ffn):
    params = tuple((weight_arg.astype(jnp.float32) for weight_arg in (w_query, w_key, w_value, w_output, b_query, b_value, b_output, gain_attn, shift_attn, w_inner, b_inner, w_outer, b_outer, gain_ffn, shift_ffn)))
    factor = jnp.where(buckets == 0, 1, jnp.where(buckets == 1, 2, 4)).astype(jnp.int32)
    key_spans = jnp.repeat(BLEN * factor, SEQ_DEV, total_repeat_length=SEQS).astype(jnp.int32)
    limits = jnp.minimum(lengths.astype(jnp.int32), key_spans).astype(jnp.int32)
    group_size = math.gcd(SEQS, 8)

    def forward(inputs, weights):
        blocks = inputs.reshape(SEQS // group_size, group_size, MAXLEN, D)

        def run_group(block, block_limits):
            return jax.vmap(lambda seq_in, seq_limit: one_sequence(weights, seq_in, seq_limit))(block, block_limits)
        kept_group = jax.checkpoint(run_group)

        def scan_step(carry_over, block_pair):
            return (carry_over, kept_group(block_pair[0], block_pair[1]))
        _, outputs = lax.scan(scan_step, jnp.zeros((), jnp.float32), (blocks, limits.reshape(SEQS // group_size, group_size)))
        return outputs.reshape(TOKENS, D)
    layer_out, pullback = jax.vjp(forward, tokens.astype(jnp.float32), params)
    grad_tokens, grads = pullback(cotangent.astype(jnp.float32))
    return (layer_out.astype(jnp.bfloat16), grad_tokens.astype(jnp.bfloat16), grads[0], grads[1], grads[2], grads[3], grads[4], grads[5], grads[6], grads[7], grads[8], grads[9], grads[10], grads[11], grads[12], grads[13], grads[14])
```

```python
from functools import partial

import jax
import jax.numpy as jnp
from jax import lax
from jax.experimental import pallas as pl
from jax.experimental.pallas import tpu as pltpu
from jax.sharding import PartitionSpec as P

D = 768
H = 12
HD = 64
FF = 3072
BLEN = 128
MAXLEN = 512
SEQ_DEV = 2
PAIR = 2 * HD
PAIRS = H // 2
CHUNKS = FF // D

EPSILON = 1e-12
DENSITY = 0.3989422804014327
LOG2E = 1.4426950408889634
SCORE_SCALE = LOG2E * HD ** (-0.5)
VMEM = 60 * 1024 * 1024
BF = jnp.bfloat16
F32 = jnp.float32


def params(**kw):
    return pltpu.CompilerParams(vmem_limit_bytes=VMEM, **kw)


def dot_nn(a, b):
    return lax.dot_general(a, b, (((1,), (0,)), ((), ())), preferred_element_type=F32)


def dot_nt(a, b):
    return lax.dot_general(a, b, (((1,), (1,)), ((), ())), preferred_element_type=F32)


def dot_tn(a, b):
    return lax.dot_general(a, b, (((0,), (0,)), ((), ())), preferred_element_type=F32)


def whole(shape):
    return pl.BlockSpec(shape, lambda *_: (0,) * len(shape), pipeline_mode=pl.Buffered(1))


def qkv_kernel(x_ref, w_ref, b_ref, out_ref):
    x = x_ref[...]
    for part in range(3):
        rows = dot_nn(x, w_ref[:, part * D : (part + 1) * D])
        out_ref[part] = (rows + b_ref[part : part + 1, :]).astype(BF)


def project_qkv(tokens, w_qkv, biases, rows=256):
    count = tokens.shape[0]
    return pl.pallas_call(
        qkv_kernel,
        grid=(count // rows,),
        in_specs=[
            pl.BlockSpec((rows, D), lambda i: (i, 0)),
            whole((D, 3 * D)),
            whole((8, D)),
        ],
        out_specs=pl.BlockSpec((3, rows, D), lambda i: (0, i, 0)),
        out_shape=jax.ShapeDtypeStruct((3, count, D), BF),
        compiler_params=params(),
        cost_estimate=pl.CostEstimate(
            flops=2 * count * D * 3 * D, bytes_accessed=8 * count * D + 6 * D * D, transcendentals=0
        ),
        name="project_qkv",
    )(tokens, w_qkv, biases)


def lane_half(shape):
    return lax.broadcasted_iota(jnp.int32, shape, 1) < HD


def live_rows(keys, limit):
    return lax.broadcasted_iota(jnp.int32, (keys, 1), 0) < limit


def pick_half(matrix, low, head):
    zero = jnp.zeros_like(matrix)
    return jnp.where(low, matrix, zero) if head == 0 else jnp.where(low, zero, matrix)


def forward_block(keys, limit, qkv_ref, out_ref, lse_ref):
    queries = qkv_ref[0]
    key_part = qkv_ref[1, :keys]
    value_t = qkv_ref[2, :keys].T
    low = lane_half((keys, PAIR))
    live = live_rows(keys, limit)
    outs = []
    for head in range(2):
        scores = dot_nt(pick_half(key_part, low, head), queries)
        scores = jnp.where(live, scores, -1e30)
        top = jnp.max(scores, axis=0, keepdims=True) * SCORE_SCALE
        powers = jnp.exp2(scores * SCORE_SCALE - top)
        total = jnp.sum(powers, axis=0, keepdims=True)
        mixed = dot_nn(value_t[head * HD : (head + 1) * HD], powers.astype(BF))
        outs.append(mixed / total)
        lse_ref[0, 0, head : head + 1, :] = top + jnp.log2(total)
    out_ref[...] = jnp.concatenate(outs, axis=0).T.astype(BF)


def backward_block(keys, limit, qkv_ref, grad_ref, lse_ref, out_ref):
    queries = qkv_ref[0]
    key_part = qkv_ref[1, :keys]
    value_part = qkv_ref[2, :keys]
    grads = grad_ref[...]
    key_t = key_part.T
    low = lane_half((keys, PAIR))
    live = live_rows(keys, limit)
    scaling = HD ** (-0.5)
    query_grads, key_grads, value_grads = [], [], []
    for head in range(2):
        scores = dot_nt(pick_half(key_part, low, head), queries)
        logits = scores * SCORE_SCALE - lse_ref[0, 0, head : head + 1, :]
        weights = jnp.exp2(jnp.where(live, logits, -1e30))
        value_grads.append(dot_nn(weights.astype(BF), grads))
        weight_grad = dot_nt(pick_half(value_part, low, head), grads)
        delta = jnp.sum(weight_grad * weights, axis=0, keepdims=True)
        score_grad = (weights * (weight_grad - delta)).astype(BF)
        key_grads.append(dot_nn(score_grad, queries))
        query_grads.append(dot_nn(key_t[head * HD : (head + 1) * HD], score_grad))
    out_ref[0] = (jnp.concatenate(query_grads, axis=0) * scaling).T.astype(BF)
    out_ref[1, :keys] = (jnp.where(low, key_grads[0], key_grads[1]) * scaling).astype(BF)
    out_ref[2, :keys] = jnp.where(low, value_grads[0], value_grads[1]).astype(BF)
    if keys < MAXLEN:
        out_ref[1, keys:] = jnp.zeros((MAXLEN - keys, PAIR), BF)
        out_ref[2, keys:] = jnp.zeros((MAXLEN - keys, PAIR), BF)


def by_blocks(block, limits_ref, *refs):
    limit = limits_ref[pl.program_id(0)]
    for blocks in range(1, MAXLEN // BLEN + 1):
        low_edge, high_edge = (blocks - 1) * BLEN, blocks * BLEN

        @pl.when((limit > low_edge) & (limit <= high_edge))
        def _():
            block(high_edge, limit, *refs)


def heads_forward(qkv, limits):
    count = qkv.shape[1]
    seqs = count // MAXLEN
    return pl.pallas_call(
        partial(by_blocks, forward_block),
        grid_spec=pltpu.PrefetchScalarGridSpec(
            num_scalar_prefetch=1,
            grid=(seqs, PAIRS),
            in_specs=[pl.BlockSpec((3, MAXLEN, PAIR), lambda s, p, _: (0, s, p))],
            out_specs=[
                pl.BlockSpec((MAXLEN, PAIR), lambda s, p, _: (s, p)),
                pl.BlockSpec((1, 1, 2, MAXLEN), lambda s, p, _: (s, p, 0, 0)),
            ],
        ),
        out_shape=[
            jax.ShapeDtypeStruct((count, D), BF),
            jax.ShapeDtypeStruct((seqs, PAIRS, 2, MAXLEN), F32),
        ],
        compiler_params=params(),
        cost_estimate=pl.CostEstimate(
            flops=16 * seqs * H * MAXLEN * MAXLEN * HD,
            bytes_accessed=8 * count * D,
            transcendentals=seqs * H * MAXLEN * MAXLEN,
        ),
        name="heads_forward",
    )(limits, qkv)


def heads_backward(qkv, grads, lse, limits):
    count = qkv.shape[1]
    seqs = count // MAXLEN
    return pl.pallas_call(
        partial(by_blocks, backward_block),
        grid_spec=pltpu.PrefetchScalarGridSpec(
            num_scalar_prefetch=1,
            grid=(seqs, PAIRS),
            in_specs=[
                pl.BlockSpec((3, MAXLEN, PAIR), lambda s, p, _: (0, s, p)),
                pl.BlockSpec((MAXLEN, PAIR), lambda s, p, _: (s, p)),
                pl.BlockSpec((1, 1, 2, MAXLEN), lambda s, p, _: (s, p, 0, 0)),
            ],
            out_specs=pl.BlockSpec((3, MAXLEN, PAIR), lambda s, p, _: (0, s, p)),
        ),
        out_shape=jax.ShapeDtypeStruct((3, count, D), BF),
        compiler_params=params(),
        cost_estimate=pl.CostEstimate(
            flops=40 * seqs * H * MAXLEN * MAXLEN * HD,
            bytes_accessed=14 * count * D,
            transcendentals=seqs * H * MAXLEN * MAXLEN,
        ),
        name="heads_backward",
    )(limits, qkv, grads, lse)


def normal_parts(hidden):
    size = jnp.abs(hidden)
    power = jnp.exp2(hidden * hidden * (-0.5 * LOG2E))
    t = 1.0 / (1.0 + 0.23164190 * size)
    series = t * (
        0.127414796
        + t * (-0.142248368 + t * (0.7107068705 + t * (-0.7265760135 + t * 0.5307027145)))
    )
    tail = series * power
    phi = jnp.where(hidden < 0.0, tail, 1.0 - tail)
    return phi, power


def row_mean(matrix):
    return jnp.mean(matrix, axis=1, keepdims=True)


def norm_rows(hidden):
    center = hidden - row_mean(hidden)
    scale = lax.rsqrt(row_mean(center * center) + EPSILON)
    return center * scale, scale


def norm_back(upstream, unit, scale, gain):
    inner = upstream * gain
    return scale * (inner - row_mean(inner) - unit * row_mean(inner * unit))


def fold_rows(matrix):
    rows, columns = matrix.shape
    return jnp.sum(matrix.reshape(rows // 8, 8, columns), axis=0)


BIAS_ROWS = ("b_query", "zero", "b_value", "b_output", "gain_attn", "shift_attn", "b_outer", "gain_ffn", "shift_ffn")


def ffn_kernel(
    tok_ref, att_ref, cot_ref, wo_ref, wi_ref, wout_ref, vec_ref, bi_ref,
    out_ref, nl_ref, act_ref, bg_ref, hg_ref, fl_ref, gf_ref, ag_ref, sums_ref, bisum_ref,
    slope_ref,
):
    vec = lambda name: vec_ref[BIAS_ROWS.index(name) : BIAS_ROWS.index(name) + 1, :]

    @pl.when(pl.program_id(0) == 0)
    def _():
        sums_ref[...] = jnp.zeros_like(sums_ref)
        bisum_ref[...] = jnp.zeros_like(bisum_ref)

    first = tok_ref[...].astype(F32) + dot_nn(att_ref[...], wo_ref[...]) + vec("b_output")
    unit_one, scale_one = norm_rows(first)
    normed = unit_one * vec("gain_attn") + vec("shift_attn")
    nl = normed.astype(BF)
    nl_ref[...] = nl
    second = normed + vec("b_outer")
    for c in range(CHUNKS):
        cols = slice(c * D, (c + 1) * D)
        hidden = dot_nn(nl, wi_ref[:, cols]) + bi_ref[:, cols]
        phi, power = normal_parts(hidden)
        active = (hidden * phi).astype(BF)
        slope_ref[:, cols] = phi + hidden * power * DENSITY
        act_ref[:, cols] = active
        second = second + dot_nn(active, wout_ref[cols, :])
    unit_two, scale_two = norm_rows(second)
    out_ref[...] = (unit_two * vec("gain_ffn") + vec("shift_ffn")).astype(BF)
    cot = cot_ref[...].astype(F32)
    sums_ref[0] += fold_rows(cot * unit_two)
    sums_ref[1] += fold_rows(cot)
    grad_second = norm_back(cot, unit_two, scale_two, vec("gain_ffn"))
    bg = grad_second.astype(BF)
    bg_ref[...] = bg
    sums_ref[2] += fold_rows(bg.astype(F32))
    grad_normed = grad_second
    for c in range(CHUNKS):
        cols = slice(c * D, (c + 1) * D)
        hg = (dot_nt(bg, wout_ref[cols, :]) * slope_ref[:, cols]).astype(BF)
        hg_ref[:, cols] = hg
        bisum_ref[:, cols] += fold_rows(hg.astype(F32))
        grad_normed = grad_normed + dot_nt(hg, wi_ref[:, cols])
    sums_ref[3] += fold_rows(grad_normed * unit_one)
    sums_ref[4] += fold_rows(grad_normed)
    grad_first = norm_back(grad_normed, unit_one, scale_one, vec("gain_attn"))
    gf_ref[...] = grad_first
    fl = grad_first.astype(BF)
    fl_ref[...] = fl
    sums_ref[5] += fold_rows(fl.astype(F32))
    ag_ref[...] = dot_nt(fl, wo_ref[...]).astype(BF)


def feed_forward(tokens, attended, cotangent, w_o, w_i, w_out, vecs, b_inner, rows=256):
    count = tokens.shape[0]
    narrow = pl.BlockSpec((rows, D), lambda i: (i, 0))
    wide = pl.BlockSpec((rows, FF), lambda i: (i, 0))
    shape = jax.ShapeDtypeStruct
    return pl.pallas_call(
        ffn_kernel,
        grid=(count // rows,),
        in_specs=[narrow, narrow, narrow, whole((D, D)), whole((D, FF)), whole((FF, D)), whole((16, D)), whole((1, FF))],
        out_specs=[narrow, narrow, wide, narrow, wide, narrow, narrow, narrow, whole((6, 8, D)), whole((8, FF))],
        out_shape=[
            shape((count, D), BF), shape((count, D), BF), shape((count, FF), BF), shape((count, D), BF),
            shape((count, FF), BF), shape((count, D), BF), shape((count, D), F32), shape((count, D), BF),
            shape((6, 8, D), F32), shape((8, FF), F32),
        ],
        scratch_shapes=[pltpu.VMEM((rows, FF), F32)],
        compiler_params=params(),
        cost_estimate=pl.CostEstimate(
            flops=2 * count * D * (4 * FF + 2 * D),
            bytes_accessed=count * (12 * D + 4 * FF + 4 * D) + 4 * D * FF + 2 * D * D,
            transcendentals=2 * count * FF,
        ),
        name="feed_forward",
    )(tokens, attended, cotangent, w_o, w_i, w_out, vecs, b_inner)


def outer_kernel(a_ref, b_ref, out_ref):
    out_ref[...] = dot_tn(a_ref[...], b_ref[...])


def weight_grad(left, right, rows=384, name="weight_grad"):
    count, height = left.shape
    columns = right.shape[1]
    return pl.pallas_call(
        outer_kernel,
        grid=(height // rows,),
        in_specs=[pl.BlockSpec((count, rows), lambda i: (0, i)), whole((count, columns))],
        out_specs=pl.BlockSpec((rows, columns), lambda i: (i, 0)),
        out_shape=jax.ShapeDtypeStruct((height, columns), F32),
        compiler_params=params(),
        cost_estimate=pl.CostEstimate(
            flops=2 * count * height * columns,
            bytes_accessed=2 * count * (height + columns) + 4 * height * columns,
            transcendentals=0,
        ),
        name=name,
    )(left, right)


def outer3_kernel(a_ref, b_ref, out_ref, sum_ref):
    out_ref[0] = dot_tn(a_ref[...], b_ref[0])
    sum_ref[0] = fold_rows(b_ref[0].astype(F32))


def qkv_weight_grad(tokens, grads):
    count = tokens.shape[0]
    return pl.pallas_call(
        outer3_kernel,
        grid=(3,),
        in_specs=[whole((count, D)), pl.BlockSpec((1, count, D), lambda i: (i, 0, 0))],
        out_specs=[pl.BlockSpec((1, D, D), lambda i: (i, 0, 0)), pl.BlockSpec((1, 8, D), lambda i: (i, 0, 0))],
        out_shape=[jax.ShapeDtypeStruct((3, D, D), F32), jax.ShapeDtypeStruct((3, 8, D), F32)],
        compiler_params=params(),
        cost_estimate=pl.CostEstimate(
            flops=6 * count * D * D, bytes_accessed=8 * count * D + 12 * D * D, transcendentals=0
        ),
        name="qkv_weight_grad",
    )(tokens, grads)


def tokens_kernel(gf_ref, g_ref, w_ref, out_ref):
    total = gf_ref[...]
    for part in range(3):
        total = total + dot_nt(g_ref[part], w_ref[:, part * D : (part + 1) * D])
    out_ref[...] = total.astype(BF)


def tokens_grad(grad_first, grads, w_qkv, rows=256):
    count = grad_first.shape[0]
    return pl.pallas_call(
        tokens_kernel,
        grid=(count // rows,),
        in_specs=[
            pl.BlockSpec((rows, D), lambda i: (i, 0)),
            pl.BlockSpec((3, rows, D), lambda i: (0, i, 0)),
            whole((D, 3 * D)),
        ],
        out_specs=pl.BlockSpec((rows, D), lambda i: (i, 0)),
        out_shape=jax.ShapeDtypeStruct((count, D), BF),
        compiler_params=params(),
        cost_estimate=pl.CostEstimate(
            flops=6 * count * D * D, bytes_accessed=12 * count * D + 6 * D * D, transcendentals=0
        ),
        name="tokens_grad",
    )(grad_first, grads, w_qkv)


def flip(value, axis, bit, size):
    return lax.ppermute(value, axis, [(i, i ^ (1 << bit)) for i in range(size)])


def bits_of(size):
    return size.bit_length() - 1


def reduce_rows(matrix, sizes):
    wide_bits, narrow_bits = bits_of(sizes["wide"]), bits_of(sizes["narrow"])
    index = {axis: lax.axis_index(axis) for axis in sizes}
    rows, columns = matrix.shape
    half = columns // 2
    own = rows // (sizes["wide"] * sizes["narrow"])
    side = index["narrow"] & 1
    give = lax.dynamic_slice_in_dim(matrix, (1 - side) * half, half, 1).astype(BF)
    keep = lax.dynamic_slice_in_dim(matrix, side * half, half, 1)
    total = keep + flip(give, "narrow", 0, sizes["narrow"]).astype(F32)
    slots = [("wide", b) for b in reversed(range(wide_bits))]
    slots += [("narrow", b) for b in reversed(range(1, narrow_bits))]
    total = total.reshape([2] * len(slots) + [2 * own, half])
    near = [("narrow", b) for b in range(1, narrow_bits)]
    far = [("wide", b) for b in range(1, wide_bits)]
    orders = (near + [("wide", 0)] + far, [("wide", 0)] + near + far[::-1])
    width = half // len(orders)
    done = []
    state = [(total[..., i * width : (i + 1) * width], list(slots)) for i in range(len(orders))]
    for step in range(len(slots)):
        for i, order in enumerate(orders):
            value, left = state[i]
            axis, bit = order[step]
            place = left.index((axis, bit))
            mine = (index[axis] >> bit) & 1
            give = lax.dynamic_index_in_dim(value, 1 - mine, place, keepdims=False).astype(BF)
            keep = lax.dynamic_index_in_dim(value, mine, place, keepdims=False)
            value = keep + flip(give, axis, bit, sizes[axis]).astype(F32)
            state[i] = (value, left[:place] + left[place + 1 :])
    total = jnp.concatenate([value for value, _ in state], axis=1)
    give = lax.dynamic_slice_in_dim(total, (1 - side) * own, own, 0)
    keep = lax.dynamic_slice_in_dim(total, side * own, own, 0)
    got = flip(give, "narrow", 0, sizes["narrow"])
    return jnp.where(
        side == 0, jnp.concatenate([keep, got], axis=1), jnp.concatenate([got, keep], axis=1)
    )


def pack_sums(vectors):
    block = jnp.stack(vectors, axis=1)
    return jnp.pad(block, ((0, 0), (0, -block.shape[1] % 256)))


def body(sizes, tokens, cotangent, lengths, buckets, w_query, w_key, w_value, w_output, b_query, b_value,
         b_output, gain_attn, shift_attn, w_inner, b_inner, w_outer, b_outer, gain_ffn, shift_ffn):
    devices = sizes["wide"] * sizes["narrow"]
    own = D // devices
    both = ("wide", "narrow")
    small = jnp.stack(
        [b_query, jnp.zeros_like(b_query), b_value, b_output, gain_attn, shift_attn, b_outer, gain_ffn, shift_ffn],
        axis=1,
    )
    small = jnp.concatenate([small, b_inner.reshape(own, CHUNKS)], axis=1)
    small = jnp.pad(small, ((0, 0), (0, 128 - small.shape[1])))
    outer_blocks = w_outer.reshape(CHUNKS, own, D)
    packed = jnp.concatenate(
        [w_query, w_key, w_value, w_output, w_inner] + [outer_blocks[c] for c in range(CHUNKS)] + [small], axis=1
    )
    full = lax.all_gather(packed, both, axis=0, tiled=True)
    w_qkv = full[:, : 3 * D]
    w_o = full[:, 3 * D : 4 * D]
    w_i = full[:, 4 * D : 8 * D]
    w_out = full[:, 8 * D : 12 * D].reshape(devices, own, CHUNKS, D).transpose(0, 2, 1, 3).reshape(FF, D)
    vectors = full[:, 12 * D :].astype(F32)
    vecs = vectors[:, :16].T
    bi = vectors[:, 9 : 9 + CHUNKS].reshape(1, FF)

    factor = jnp.where(buckets[0] == 0, 1, jnp.where(buckets[0] == 1, 2, 4)).astype(jnp.int32)
    limits = jnp.minimum(lengths, BLEN * factor).astype(jnp.int32)

    qkv = project_qkv(tokens, w_qkv, vecs[:8])
    attended, lse = heads_forward(qkv, limits)
    layer_out, normed_low, active, branch, hidden_grad, first_low, grad_first, attended_grad, sums, bi_sums = (
        feed_forward(tokens, attended, cotangent, w_o, w_i, w_out, vecs, bi)
    )
    outer_grad = weight_grad(active, branch, name="outer_grad")
    inner_grad = weight_grad(normed_low, hidden_grad, name="inner_grad")
    output_grad = weight_grad(attended, first_low, name="output_grad")
    sums = jnp.sum(sums, axis=1)
    bi_sums = jnp.sum(bi_sums, axis=0).reshape(D, CHUNKS)
    outer_rows = outer_grad.reshape(devices, CHUNKS, own, D).transpose(0, 2, 1, 3).reshape(D, FF)
    ffn_sums = jnp.concatenate([sums.T, bi_sums], axis=1)
    ffn_sums = jnp.pad(ffn_sums, ((0, 0), (0, 512 - ffn_sums.shape[1])))
    ffn_own = reduce_rows(jnp.concatenate([inner_grad, outer_rows, ffn_sums], axis=1), sizes)

    grads = heads_backward(qkv, attended_grad, lse, limits)
    qkv_grad, qkv_sums = qkv_weight_grad(tokens, grads)
    qkv_sums = jnp.sum(qkv_sums, axis=1).T
    qkv_sums = jnp.pad(qkv_sums, ((0, 0), (0, 512 - qkv_sums.shape[1])))
    attn_own = reduce_rows(
        jnp.concatenate([qkv_grad[0], qkv_grad[1], qkv_grad[2], output_grad, qkv_sums], axis=1), sizes
    )
    grad_tokens = tokens_grad(grad_first, grads, w_qkv)

    sums_own = ffn_own[:, 2 * FF :]
    attn_sums = attn_own[:, 4 * D :]
    return (
        layer_out,
        grad_tokens,
        attn_own[:, :D],
        attn_own[:, D : 2 * D],
        attn_own[:, 2 * D : 3 * D],
        attn_own[:, 3 * D : 4 * D],
        attn_sums[:, 0],
        attn_sums[:, 2],
        sums_own[:, 5],
        sums_own[:, 3],
        sums_own[:, 4],
        ffn_own[:, :FF],
        sums_own[:, 6 : 6 + CHUNKS].reshape(own * CHUNKS),
        ffn_own[:, FF : 2 * FF].reshape(own, CHUNKS, D).transpose(1, 0, 2).reshape(CHUNKS * own, D),
        sums_own[:, 2],
        sums_own[:, 0],
        sums_own[:, 1],
    )


def solution(mesh):
    rows, vector = P(("wide", "narrow"), None), P(("wide", "narrow"))
    sizes = {axis: mesh.shape[axis] for axis in ("wide", "narrow")}
    return jax.shard_map(
        partial(body, sizes),
        mesh=mesh,
        in_specs=(rows, rows, vector, vector) + (rows,) * 4 + (vector,) * 5
        + (rows, vector, rows, vector, vector, vector),
        out_specs=(rows,) * 6 + (vector,) * 5 + (rows, vector, rows, vector, vector, vector),
        check_vma=False,
    )
```

```python
from functools import partial

import jax
import jax.numpy as jnp
from jax import lax
from jax.experimental import pallas as pl
from jax.experimental.pallas import tpu as pltpu
from jax.sharding import PartitionSpec as P

D = 768
H = 12
HD = 64
FF = 3072
BLEN = 128
MAXLEN = 512
SEQ_DEV = 2
PAIR = 2 * HD
PAIRS = H // 2
CHUNKS = FF // D

EPSILON = 1e-12
DENSITY = 0.3989422804014327
LOG2E = 1.4426950408889634
SCORE_SCALE = LOG2E * HD ** (-0.5)
VMEM = 60 * 1024 * 1024
BF = jnp.bfloat16
F32 = jnp.float32


def params(**kw):
    return pltpu.CompilerParams(vmem_limit_bytes=VMEM, **kw)


def dot_nn(a, b):
    return lax.dot_general(a, b, (((1,), (0,)), ((), ())), preferred_element_type=F32)


def dot_nt(a, b):
    return lax.dot_general(a, b, (((1,), (1,)), ((), ())), preferred_element_type=F32)


def dot_tn(a, b):
    return lax.dot_general(a, b, (((0,), (0,)), ((), ())), preferred_element_type=F32)


def whole(shape):
    return pl.BlockSpec(shape, lambda *_: (0,) * len(shape), pipeline_mode=pl.Buffered(1))


def columns_of(block, width):
    return pl.BlockSpec((D, width), lambda *_: (0, block), pipeline_mode=pl.Buffered(1))


def qkv_kernel(x_ref, w_ref, b_ref, out_ref):
    x = x_ref[...]
    for part in range(3):
        rows = dot_nn(x, w_ref[:, part * D : (part + 1) * D])
        out_ref[part] = (rows + b_ref[part : part + 1, :]).astype(BF)


def project_qkv(tokens, w_qkv, biases, rows=256):
    count = tokens.shape[0]
    return pl.pallas_call(
        qkv_kernel,
        grid=(count // rows,),
        in_specs=[
            pl.BlockSpec((rows, D), lambda i: (i, 0)),
            whole((D, 3 * D)),
            whole((16, D)),
        ],
        out_specs=pl.BlockSpec((3, rows, D), lambda i: (0, i, 0)),
        out_shape=jax.ShapeDtypeStruct((3, count, D), BF),
        compiler_params=params(),
        cost_estimate=pl.CostEstimate(
            flops=2 * count * D * 3 * D, bytes_accessed=8 * count * D + 6 * D * D, transcendentals=0
        ),
        name="project_qkv",
    )(tokens, w_qkv, biases)


def lane_half(shape):
    return lax.broadcasted_iota(jnp.int32, shape, 1) < HD


def live_rows(keys, limit):
    return lax.broadcasted_iota(jnp.int32, (keys, 1), 0) < limit


def pick_half(matrix, low, head):
    zero = jnp.zeros_like(matrix)
    return jnp.where(low, matrix, zero) if head == 0 else jnp.where(low, zero, matrix)


def forward_block(keys, limit, qkv_ref, out_ref, lse_ref):
    queries = qkv_ref[0]
    key_part = qkv_ref[1, :keys]
    value_t = qkv_ref[2, :keys].T
    low = lane_half((keys, PAIR))
    live = live_rows(keys, limit)
    outs = []
    for head in range(2):
        scores = dot_nt(pick_half(key_part, low, head), queries)
        scores = jnp.where(live, scores, -1e30)
        top = jnp.max(scores, axis=0, keepdims=True) * SCORE_SCALE
        powers = jnp.exp2(scores * SCORE_SCALE - top)
        total = jnp.sum(powers, axis=0, keepdims=True)
        mixed = dot_nn(value_t[head * HD : (head + 1) * HD], powers.astype(BF))
        outs.append(mixed / total)
        lse_ref[0, 0, head : head + 1, :] = top + jnp.log2(total)
    out_ref[...] = jnp.concatenate(outs, axis=0).T.astype(BF)


def backward_block(keys, limit, qkv_ref, grad_ref, lse_ref, out_ref):
    queries = qkv_ref[0]
    key_part = qkv_ref[1, :keys]
    value_part = qkv_ref[2, :keys]
    grads = grad_ref[...]
    key_t = key_part.T
    low = lane_half((keys, PAIR))
    live = live_rows(keys, limit)
    scaling = HD ** (-0.5)
    query_grads, key_grads, value_grads = [], [], []
    for head in range(2):
        scores = dot_nt(pick_half(key_part, low, head), queries)
        logits = scores * SCORE_SCALE - lse_ref[0, 0, head : head + 1, :]
        weights = jnp.exp2(jnp.where(live, logits, -1e30))
        value_grads.append(dot_nn(weights.astype(BF), grads))
        weight_grad = dot_nt(pick_half(value_part, low, head), grads)
        delta = jnp.sum(weight_grad * weights, axis=0, keepdims=True)
        score_grad = (weights * (weight_grad - delta)).astype(BF)
        key_grads.append(dot_nn(score_grad, queries))
        query_grads.append(dot_nn(key_t[head * HD : (head + 1) * HD], score_grad))
    out_ref[0] = (jnp.concatenate(query_grads, axis=0) * scaling).T.astype(BF)
    out_ref[1, :keys] = (jnp.where(low, key_grads[0], key_grads[1]) * scaling).astype(BF)
    out_ref[2, :keys] = jnp.where(low, value_grads[0], value_grads[1]).astype(BF)
    if keys < MAXLEN:
        out_ref[1, keys:] = jnp.zeros((MAXLEN - keys, PAIR), BF)
        out_ref[2, keys:] = jnp.zeros((MAXLEN - keys, PAIR), BF)


def by_blocks(block, limits_ref, *refs):
    limit = limits_ref[pl.program_id(0)]
    for blocks in range(1, MAXLEN // BLEN + 1):
        low_edge, high_edge = (blocks - 1) * BLEN, blocks * BLEN

        @pl.when((limit > low_edge) & (limit <= high_edge))
        def _():
            block(high_edge, limit, *refs)


def heads_forward(qkv, limits):
    count = qkv.shape[1]
    seqs = count // MAXLEN
    return pl.pallas_call(
        partial(by_blocks, forward_block),
        grid_spec=pltpu.PrefetchScalarGridSpec(
            num_scalar_prefetch=1,
            grid=(seqs, PAIRS),
            in_specs=[pl.BlockSpec((3, MAXLEN, PAIR), lambda s, p, _: (0, s, p))],
            out_specs=[
                pl.BlockSpec((MAXLEN, PAIR), lambda s, p, _: (s, p)),
                pl.BlockSpec((1, 1, 2, MAXLEN), lambda s, p, _: (s, p, 0, 0)),
            ],
        ),
        out_shape=[
            jax.ShapeDtypeStruct((count, D), BF),
            jax.ShapeDtypeStruct((seqs, PAIRS, 2, MAXLEN), F32),
        ],
        compiler_params=params(),
        cost_estimate=pl.CostEstimate(
            flops=16 * seqs * H * MAXLEN * MAXLEN * HD,
            bytes_accessed=8 * count * D,
            transcendentals=seqs * H * MAXLEN * MAXLEN,
        ),
        name="heads_forward",
    )(limits, qkv)


def heads_backward(qkv, grads, lse, limits):
    count = qkv.shape[1]
    seqs = count // MAXLEN
    return pl.pallas_call(
        partial(by_blocks, backward_block),
        grid_spec=pltpu.PrefetchScalarGridSpec(
            num_scalar_prefetch=1,
            grid=(seqs, PAIRS),
            in_specs=[
                pl.BlockSpec((3, MAXLEN, PAIR), lambda s, p, _: (0, s, p)),
                pl.BlockSpec((MAXLEN, PAIR), lambda s, p, _: (s, p)),
                pl.BlockSpec((1, 1, 2, MAXLEN), lambda s, p, _: (s, p, 0, 0)),
            ],
            out_specs=pl.BlockSpec((3, MAXLEN, PAIR), lambda s, p, _: (0, s, p)),
        ),
        out_shape=jax.ShapeDtypeStruct((3, count, D), BF),
        compiler_params=params(),
        cost_estimate=pl.CostEstimate(
            flops=40 * seqs * H * MAXLEN * MAXLEN * HD,
            bytes_accessed=14 * count * D,
            transcendentals=seqs * H * MAXLEN * MAXLEN,
        ),
        name="heads_backward",
    )(limits, qkv, grads, lse)


def normal_parts(hidden):
    size = jnp.abs(hidden)
    power = jnp.exp2(hidden * hidden * (-0.5 * LOG2E))
    t = 1.0 / (1.0 + 0.23164190 * size)
    series = t * (
        0.127414796
        + t * (-0.142248368 + t * (0.7107068705 + t * (-0.7265760135 + t * 0.5307027145)))
    )
    tail = series * power
    phi = jnp.where(hidden < 0.0, tail, 1.0 - tail)
    return phi, power


def row_mean(matrix):
    return jnp.mean(matrix, axis=1, keepdims=True)


def norm_rows(hidden):
    center = hidden - row_mean(hidden)
    scale = lax.rsqrt(row_mean(center * center) + EPSILON)
    return center * scale, scale


def norm_back(upstream, unit, scale, gain):
    inner = upstream * gain
    return scale * (inner - row_mean(inner) - unit * row_mean(inner * unit))


def fold_rows(matrix):
    rows, columns = matrix.shape
    return jnp.sum(matrix.reshape(rows // 8, 8, columns), axis=0)


BIAS_ROWS = ("b_query", "zero", "b_value", "b_output", "gain_attn", "shift_attn", "b_outer", "gain_ffn", "shift_ffn", "b_inner")


def ffn_kernel(
    tok_ref, att_ref, cot_ref, wi_ref, wout_ref, wo_ref, vec_ref,
    out_ref, nl_ref, act_ref, bg_ref, hg_ref, fl_ref, gf_ref, ag_ref, sums_ref, bisum_ref,
    slope_ref,
):
    vec = lambda name: vec_ref[BIAS_ROWS.index(name) : BIAS_ROWS.index(name) + 1, :]

    @pl.when(pl.program_id(0) == 0)
    def _():
        sums_ref[...] = jnp.zeros_like(sums_ref)
        bisum_ref[...] = jnp.zeros_like(bisum_ref)

    first = tok_ref[...].astype(F32) + dot_nn(att_ref[...], wo_ref[...]) + vec("b_output")
    unit_one, scale_one = norm_rows(first)
    normed = unit_one * vec("gain_attn") + vec("shift_attn")
    nl = normed.astype(BF)
    nl_ref[...] = nl
    second = normed + vec("b_outer")
    for c in range(CHUNKS):
        cols = slice(c * D, (c + 1) * D)
        hidden = dot_nn(nl, wi_ref[:, cols]) + vec_ref[BIAS_ROWS.index("b_inner") + c : BIAS_ROWS.index("b_inner") + c + 1, :]
        phi, power = normal_parts(hidden)
        active = (hidden * phi).astype(BF)
        slope_ref[:, cols] = phi + hidden * power * DENSITY
        act_ref[:, cols] = active
        second = second + dot_nn(active, wout_ref[:, cols])
    unit_two, scale_two = norm_rows(second)
    out_ref[...] = (unit_two * vec("gain_ffn") + vec("shift_ffn")).astype(BF)
    cot = cot_ref[...].astype(F32)
    sums_ref[0] += fold_rows(cot * unit_two)
    sums_ref[1] += fold_rows(cot)
    grad_second = norm_back(cot, unit_two, scale_two, vec("gain_ffn"))
    bg = grad_second.astype(BF)
    bg_ref[...] = bg
    sums_ref[2] += fold_rows(bg.astype(F32))
    grad_normed = grad_second
    for c in range(CHUNKS):
        cols = slice(c * D, (c + 1) * D)
        hg = (dot_nt(bg, wout_ref[:, cols]) * slope_ref[:, cols]).astype(BF)
        hg_ref[:, cols] = hg
        bisum_ref[:, cols] += fold_rows(hg.astype(F32))
        grad_normed = grad_normed + dot_nt(hg, wi_ref[:, cols])
    sums_ref[3] += fold_rows(grad_normed * unit_one)
    sums_ref[4] += fold_rows(grad_normed)
    grad_first = norm_back(grad_normed, unit_one, scale_one, vec("gain_attn"))
    gf_ref[...] = grad_first
    fl = grad_first.astype(BF)
    fl_ref[...] = fl
    sums_ref[5] += fold_rows(fl.astype(F32))
    ag_ref[...] = dot_nt(fl, wo_ref[...]).astype(BF)


def feed_forward(tokens, attended, cotangent, weights, vecs, rows=256):
    count = tokens.shape[0]
    narrow = pl.BlockSpec((rows, D), lambda i: (i, 0))
    wide = pl.BlockSpec((rows, FF), lambda i: (i, 0))
    shape = jax.ShapeDtypeStruct
    return pl.pallas_call(
        ffn_kernel,
        grid=(count // rows,),
        in_specs=[
            narrow, narrow, narrow,
            columns_of(0, FF), columns_of(1, FF), columns_of(2 * CHUNKS, D),
            whole((16, D)),
        ],
        out_specs=[narrow, narrow, wide, narrow, wide, narrow, narrow, narrow, whole((6, 8, D)), whole((8, FF))],
        out_shape=[
            shape((count, D), BF), shape((count, D), BF), shape((count, FF), BF), shape((count, D), BF),
            shape((count, FF), BF), shape((count, D), BF), shape((count, D), F32), shape((count, D), BF),
            shape((6, 8, D), F32), shape((8, FF), F32),
        ],
        scratch_shapes=[pltpu.VMEM((rows, FF), F32)],
        compiler_params=params(),
        cost_estimate=pl.CostEstimate(
            flops=2 * count * D * (4 * FF + 2 * D),
            bytes_accessed=count * (12 * D + 4 * FF + 4 * D) + 4 * D * FF + 2 * D * D,
            transcendentals=2 * count * FF,
        ),
        name="feed_forward",
    )(tokens, attended, cotangent, weights, weights, weights, vecs)


def outer_kernel(a_ref, b_ref, out_ref):
    out_ref[...] = dot_tn(a_ref[...], b_ref[...]).astype(BF)


def outer_weight_grad(active, branch, rows=384):
    count = active.shape[0]
    split = D // rows
    return pl.pallas_call(
        outer_kernel,
        grid=(CHUNKS, split),
        in_specs=[pl.BlockSpec((count, rows), lambda c, m: (0, c * split + m)), whole((count, D))],
        out_specs=pl.BlockSpec((rows, D), lambda c, m: (m, c)),
        out_shape=jax.ShapeDtypeStruct((D, FF), BF),
        compiler_params=params(),
        cost_estimate=pl.CostEstimate(
            flops=2 * count * FF * D, bytes_accessed=2 * count * (FF + D) + 2 * FF * D, transcendentals=0
        ),
        name="outer_weight_grad",
    )(active, branch)


def inner_kernel(a_ref, b_ref, out_ref, turned_ref):
    @pl.when(pl.program_id(0) == 0)
    def _():
        turned_ref[...] = a_ref[...].T

    out_ref[...] = dot_nn(turned_ref[...], b_ref[...])


def inner_weight_grad(normed, hidden_grad, columns=768):
    count = normed.shape[0]
    return pl.pallas_call(
        inner_kernel,
        grid=(FF // columns,),
        in_specs=[whole((count, D)), pl.BlockSpec((count, columns), lambda i: (0, i))],
        out_specs=pl.BlockSpec((D, columns), lambda i: (0, i)),
        out_shape=jax.ShapeDtypeStruct((D, FF), F32),
        scratch_shapes=[pltpu.VMEM((D, count), BF)],
        compiler_params=params(),
        cost_estimate=pl.CostEstimate(
            flops=2 * count * FF * D, bytes_accessed=2 * count * (FF + D) + 4 * FF * D, transcendentals=0
        ),
        name="inner_weight_grad",
    )(normed, hidden_grad)


SUMS = 128


def attn_weights_kernel(tok_ref, att_ref, g_ref, gcols_ref, fl_ref, sums_ref, out_ref):
    count = tok_ref.shape[0]
    turned = tok_ref[...].T
    for part in range(3):
        out_ref[:, part * D : (part + 1) * D] = dot_nn(turned, g_ref[part])
    out_ref[:, 3 * D : 4 * D] = dot_tn(att_ref[...], fl_ref[...])
    place = lax.broadcasted_iota(jnp.int32, (count, SUMS), 1)
    sums = sums_ref[...]
    for part, column in ((0, 10), (2, 11)):
        sums = sums + dot_tn(gcols_ref[part], (place == column).astype(BF))
    out_ref[:, 4 * D :] = sums


def attn_weight_grads(tokens, attended, grads, first_low, sums, rows=384):
    count = tokens.shape[0]
    narrow = pl.BlockSpec((count, rows), lambda i: (0, i))
    return pl.pallas_call(
        attn_weights_kernel,
        grid=(D // rows,),
        in_specs=[
            narrow, narrow, whole((3, count, D)), pl.BlockSpec((3, count, rows), lambda i: (0, 0, i)),
            whole((count, D)), pl.BlockSpec((rows, SUMS), lambda i: (i, 0)),
        ],
        out_specs=pl.BlockSpec((rows, 4 * D + SUMS), lambda i: (i, 0)),
        out_shape=jax.ShapeDtypeStruct((D, 4 * D + SUMS), F32),
        compiler_params=params(),
        cost_estimate=pl.CostEstimate(
            flops=8 * count * D * D, bytes_accessed=18 * count * D + 16 * D * D, transcendentals=0
        ),
        name="attn_weight_grads",
    )(tokens, attended, grads, grads, first_low, sums)


def tokens_kernel(gf_ref, g_ref, w_ref, out_ref):
    total = gf_ref[...]
    for part in range(3):
        total = total + dot_nt(g_ref[part], w_ref[:, part * D : (part + 1) * D])
    out_ref[...] = total.astype(BF)


def tokens_grad(grad_first, grads, w_qkv, rows=256):
    count = grad_first.shape[0]
    return pl.pallas_call(
        tokens_kernel,
        grid=(count // rows,),
        in_specs=[
            pl.BlockSpec((rows, D), lambda i: (i, 0)),
            pl.BlockSpec((3, rows, D), lambda i: (0, i, 0)),
            whole((D, 3 * D)),
        ],
        out_specs=pl.BlockSpec((rows, D), lambda i: (i, 0)),
        out_shape=jax.ShapeDtypeStruct((count, D), BF),
        compiler_params=params(),
        cost_estimate=pl.CostEstimate(
            flops=6 * count * D * D, bytes_accessed=12 * count * D + 6 * D * D, transcendentals=0
        ),
        name="tokens_grad",
    )(grad_first, grads, w_qkv)


AXES = ("hi", "lo", "far", "near")
CHIPS = AXES[:3]


def swap_near(value):
    return lax.ppermute(value, "near", [(0, 1), (1, 0)])


def exchange(value):
    return lax.all_to_all(value, CHIPS, 0, 0, tiled=True)


def gather_rows(block, sizes):
    own, columns = block.shape
    chips = sizes["hi"] * sizes["lo"] * sizes["far"]
    mine = exchange(jnp.broadcast_to(block[None], (chips, own, columns)))
    other = swap_near(mine)
    place = lax.broadcasted_iota(jnp.int32, (chips, 2, own, columns), 1)
    full = jnp.where(place == lax.axis_index("near"), mine[:, None], other[:, None])
    return lax.optimization_barrier(full).reshape(chips * 2 * own, columns)


def scatter_rows(matrix, sizes):
    rows, columns = matrix.shape
    chips = sizes["hi"] * sizes["lo"] * sizes["far"]
    own = rows // (2 * chips)
    side = lax.axis_index("near")
    parts = matrix.reshape(chips, 2, own, columns)
    give = lax.dynamic_index_in_dim(parts, 1 - side, 1, keepdims=False).astype(BF)
    keep = lax.dynamic_index_in_dim(parts, side, 1, keepdims=False)
    pair = (keep + swap_near(give).astype(F32)).astype(BF)
    return pair, lambda: jnp.sum(exchange(pair).astype(F32), axis=0)


def body(sizes, tokens, cotangent, lengths, buckets, w_query, w_key, w_value, w_output, b_query, b_value,
         b_output, gain_attn, shift_attn, w_inner, b_inner, w_outer, b_outer, gain_ffn, shift_ffn):
    own = w_query.shape[0]
    devices = D // own
    inner_turned = w_inner.reshape(own, devices, CHUNKS, own).transpose(0, 2, 1, 3).reshape(own, FF)
    outer_blocks = w_outer.reshape(CHUNKS, own, D)
    ffn_pack = jnp.concatenate([inner_turned] + [outer_blocks[c] for c in range(CHUNKS)] + [w_output], axis=1)
    ffn_weights = lax.all_gather(ffn_pack, AXES, axis=0, tiled=True)

    small = jnp.stack(
        [b_query, jnp.zeros_like(b_query), b_value, b_output, gain_attn, shift_attn, b_outer, gain_ffn, shift_ffn],
        axis=1,
    )
    small = jnp.concatenate([small, b_inner.reshape(CHUNKS, own).T], axis=1)
    small = jnp.pad(small, ((0, 0), (0, 128 - small.shape[1])))
    attn_weights = gather_rows(jnp.concatenate([w_query, w_key, w_value, small], axis=1), sizes)
    vecs = attn_weights[:, 3 * D : 3 * D + 16].astype(F32).T

    factor = jnp.where(buckets[0] == 0, 1, jnp.where(buckets[0] == 1, 2, 4)).astype(jnp.int32)
    limits = jnp.minimum(lengths, BLEN * factor).astype(jnp.int32)

    qkv = project_qkv(tokens, attn_weights, vecs)
    attended, lse = heads_forward(qkv, limits)
    layer_out, normed_low, active, branch, hidden_grad, first_low, grad_first, attended_grad, sums, bi_sums = (
        feed_forward(tokens, attended, cotangent, ffn_weights, vecs)
    )
    outer_grad = outer_weight_grad(active, branch)
    outer_own = lax.psum_scatter(outer_grad, AXES, scatter_dimension=0, tiled=True)
    normed_low, _ = lax.optimization_barrier((normed_low, outer_grad))
    inner_grad = inner_weight_grad(normed_low, hidden_grad)
    inner_pair, inner_finish = scatter_rows(inner_grad, sizes)
    sums = jnp.concatenate([jnp.sum(sums, axis=1), jnp.sum(bi_sums, axis=0).reshape(CHUNKS, D)], axis=0)
    sums = jnp.pad(sums, ((0, SUMS - sums.shape[0]), (0, 0))).T

    attended_grad, _ = lax.optimization_barrier((attended_grad, inner_pair))
    grads = heads_backward(qkv, attended_grad, lse, limits)
    _, attn_finish = scatter_rows(attn_weight_grads(tokens, attended, grads, first_low, sums), sizes)
    grad_tokens = tokens_grad(grad_first, grads, attn_weights)
    inner_own = inner_finish()
    attn_own = attn_finish()

    sums_own = attn_own[:, 4 * D :]
    return (
        layer_out,
        grad_tokens,
        attn_own[:, :D],
        attn_own[:, D : 2 * D],
        attn_own[:, 2 * D : 3 * D],
        attn_own[:, 3 * D : 4 * D],
        sums_own[:, 10],
        sums_own[:, 11],
        sums_own[:, 5],
        sums_own[:, 3],
        sums_own[:, 4],
        inner_own.reshape(own, CHUNKS, devices, own).transpose(0, 2, 1, 3).reshape(own, FF),
        sums_own[:, 6 : 6 + CHUNKS].T.reshape(CHUNKS * own),
        outer_own.astype(F32).reshape(own, CHUNKS, D).transpose(1, 0, 2).reshape(CHUNKS * own, D),
        sums_own[:, 2],
        sums_own[:, 0],
        sums_own[:, 1],
    )


def solution(mesh):
    wide, narrow = mesh.shape["wide"], mesh.shape["narrow"]
    sizes = {"hi": wide // 2, "lo": 2, "far": narrow // 2, "near": 2}
    split = jax.sharding.Mesh(mesh.devices.reshape([sizes[axis] for axis in AXES]), AXES)
    rows, vector = P(AXES, None), P(AXES)
    return jax.shard_map(
        partial(body, sizes),
        mesh=split,
        in_specs=(rows, rows, vector, vector) + (rows,) * 4 + (vector,) * 5
        + (rows, vector, rows, vector, vector, vector),
        out_specs=(rows,) * 6 + (vector,) * 5 + (rows, vector, rows, vector, vector, vector),
        check_vma=False,
    )
```

```python
from functools import partial

import jax
import jax.numpy as jnp
from jax import lax
from jax.experimental import pallas as pl
from jax.experimental.pallas import tpu as pltpu
from jax.sharding import PartitionSpec as P

D = 768
H = 12
HD = 64
FF = 3072
BLEN = 128
MAXLEN = 512
SEQ_DEV = 2
PAIR = 2 * HD
PAIRS = H // 2
CHUNKS = FF // D

EPSILON = 1e-12
DENSITY = 0.3989422804014327
LOG2E = 1.4426950408889634
SCORE_SCALE = LOG2E * HD ** (-0.5)
VMEM = 60 * 1024 * 1024
BF = jnp.bfloat16
F32 = jnp.float32


def cost(megaflops):
    return pl.CostEstimate(flops=int(megaflops * 1e6 * COST_SCALE), bytes_accessed=1, transcendentals=0)


COST_SCALE = 1.0


def params(**kw):
    return pltpu.CompilerParams(vmem_limit_bytes=VMEM, **kw)


def dot_nn(a, b):
    return lax.dot_general(a, b, (((1,), (0,)), ((), ())), preferred_element_type=F32)


def dot_nt(a, b):
    return lax.dot_general(a, b, (((1,), (1,)), ((), ())), preferred_element_type=F32)


def dot_tn(a, b):
    return lax.dot_general(a, b, (((0,), (0,)), ((), ())), preferred_element_type=F32)


def whole(shape):
    return pl.BlockSpec(shape, lambda *_: (0,) * len(shape), pipeline_mode=pl.Buffered(1))


def columns_of(block, width):
    return pl.BlockSpec((D, width), lambda *_: (0, block), pipeline_mode=pl.Buffered(1))


def row_split(layout, rows, columns):
    own = layout[-1]
    if own % 8:
        return [jax.ShapeDtypeStruct((rows, columns), BF)]
    return [jax.ShapeDtypeStruct((rows // 2, columns), BF)] * 2


def store_split(layout, side, value, refs):
    if len(refs) == 1:
        refs[0][...] = value.astype(BF)
        return
    high, middle, own = layout
    parts = value.reshape(high, middle, 2, own, value.shape[1])
    lower, upper = parts[:, :, 0], parts[:, :, 1]
    for ref, part in zip(refs, (jnp.where(side == 0, upper, lower), jnp.where(side == 0, lower, upper))):
        ref[...] = jnp.transpose(part, (1, 0, 2, 3)).reshape(value.shape[0] // 2, value.shape[1]).astype(BF)


def split_rows(layout, side, outs):
    if len(outs) == 2:
        return outs
    high, middle, own = layout
    parts = outs[0].reshape(high, middle, 2, own, -1)
    halves = []
    for place in (1 - side, side):
        part = lax.dynamic_index_in_dim(parts, place, 2, keepdims=False)
        halves.append(part.transpose(1, 0, 2, 3).reshape(high * middle * own, -1))
    return halves


SUMS = 128
HALF = PAIRS // 2
HALF_D = HALF * PAIR


def lane_half(shape):
    return lax.broadcasted_iota(jnp.int32, shape, 1) < HD


def pick_half(matrix, low, head):
    zero = jnp.zeros_like(matrix)
    return jnp.where(low, matrix, zero) if head == 0 else jnp.where(low, zero, matrix)


def mask_last(scores, limit, fill):
    edge = scores.shape[0] - BLEN
    live = lax.broadcasted_iota(jnp.int32, (BLEN, 1), 0) + edge < limit
    last = jnp.where(live, scores[edge:], fill)
    return jnp.concatenate([scores[:edge], last], axis=0) if edge else last


def pair_columns(pair):
    return pl.ds(pl.multiple_of(pair * PAIR, PAIR), PAIR)


def forward_block(keys, limit, pair, qkv_ref, out_ref, lse_ref):
    columns = pair_columns(pair)
    queries = qkv_ref[0, :, columns]
    key_part = qkv_ref[1, :keys, columns]
    value_t = qkv_ref[2, :keys, columns].T
    low = lane_half((keys, PAIR))
    outs = []
    for head in range(2):
        scores = mask_last(dot_nt(pick_half(key_part, low, head), queries), limit, -1e30)
        top = jnp.max(scores, axis=0, keepdims=True) * SCORE_SCALE
        powers = jnp.exp2(scores * SCORE_SCALE - top)
        total = jnp.sum(powers, axis=0, keepdims=True)
        mixed = dot_nn(value_t[head * HD : (head + 1) * HD], powers.astype(BF))
        outs.append(mixed / total)
        lse_ref[0, pair, head : head + 1, :] = top + jnp.log2(total)
    out_ref[:, columns] = jnp.concatenate(outs, axis=0).T.astype(BF)


def backward_block(keys, limit, pair, first_pair, qkv_ref, grad_ref, lse_ref, out_ref):
    columns, here = pair_columns(first_pair + pair), pair_columns(pair)
    queries = qkv_ref[0, :, columns]
    key_part = qkv_ref[1, :keys, columns]
    value_part = qkv_ref[2, :keys, columns]
    grads = grad_ref[:, columns]
    key_t = key_part.T
    low = lane_half((keys, PAIR))
    scaling = HD ** (-0.5)
    query_grads, key_grads, value_grads = [], [], []
    for head in range(2):
        scores = dot_nt(pick_half(key_part, low, head), queries)
        logits = scores * SCORE_SCALE - lse_ref[0, first_pair + pair, head : head + 1, :]
        weights = jnp.exp2(mask_last(logits, limit, -1e30))
        value_grads.append(dot_nn(weights.astype(BF), grads))
        weight_grad = dot_nt(pick_half(value_part, low, head), grads)
        delta = jnp.sum(weight_grad * weights, axis=0, keepdims=True)
        score_grad = (weights * (weight_grad - delta)).astype(BF)
        key_grads.append(dot_nn(score_grad, queries))
        query_grads.append(dot_nn(key_t[head * HD : (head + 1) * HD], score_grad))
    out_ref[0, :, here] = (jnp.concatenate(query_grads, axis=0) * scaling).T.astype(BF)
    out_ref[1, :keys, here] = (jnp.where(low, key_grads[0], key_grads[1]) * scaling).astype(BF)
    out_ref[2, :keys, here] = jnp.where(low, value_grads[0], value_grads[1]).astype(BF)
    if keys < MAXLEN:
        out_ref[1, keys:, here] = jnp.zeros((MAXLEN - keys, PAIR), BF)
        out_ref[2, keys:, here] = jnp.zeros((MAXLEN - keys, PAIR), BF)


def by_blocks(limit, pairs, block, *refs):
    for blocks in range(1, MAXLEN // BLEN + 1):
        low_edge, high_edge = (blocks - 1) * BLEN, blocks * BLEN

        @pl.when((limit > low_edge) & (limit <= high_edge))
        def _():
            def one_pair(pair, carry):
                block(high_edge, limit, pair, *refs)
                return carry

            lax.fori_loop(0, pairs, one_pair, 0, unroll=2 if pairs % 2 == 0 else pairs)


def forward_kernel(limits_ref, x_ref, w_ref, bias_ref, qkv_ref, out_ref, lse_ref):
    x = x_ref[...]
    for part in range(3):
        rows = dot_nn(x, w_ref[:, part * D : (part + 1) * D])
        qkv_ref[part] = (rows + bias_ref[part : part + 1, :]).astype(BF)
    by_blocks(limits_ref[pl.program_id(0)], PAIRS, forward_block, qkv_ref, out_ref, lse_ref)


def heads_forward(tokens, weights, biases, limits):
    count = tokens.shape[0]
    seqs = count // MAXLEN
    return pl.pallas_call(
        forward_kernel,
        grid_spec=pltpu.PrefetchScalarGridSpec(
            num_scalar_prefetch=1,
            grid=(seqs,),
            in_specs=[pl.BlockSpec((MAXLEN, D), lambda s, _: (s, 0)), whole((D, 3 * D)), whole((16, D))],
            out_specs=[
                pl.BlockSpec((3, MAXLEN, D), lambda s, _: (0, s, 0)),
                pl.BlockSpec((MAXLEN, D), lambda s, _: (s, 0)),
                pl.BlockSpec((1, PAIRS, 2, MAXLEN), lambda s, _: (s, 0, 0, 0)),
            ],
        ),
        out_shape=[
            jax.ShapeDtypeStruct((3, count, D), BF),
            jax.ShapeDtypeStruct((count, D), BF),
            jax.ShapeDtypeStruct((seqs, PAIRS, 2, MAXLEN), F32),
        ],
        compiler_params=params(),
        cost_estimate=cost(6000),
        name="heads_forward",
    )(limits, tokens, weights, biases)


def backward_kernel(first_pair, layout, limits_ref, side_ref, qkv_ref, grad_ref, lse_ref, tok_ref, sums_ref, out_ref,
                    *refs):
    split_refs, dw_ref = refs[:-1], refs[-1]
    seq = pl.program_id(0)
    by_blocks(limits_ref[seq], HALF, backward_block, first_pair, qkv_ref, grad_ref, lse_ref, out_ref)
    turned = tok_ref[...].T
    place = lax.broadcasted_iota(jnp.int32, (MAXLEN, SUMS), 1)
    head_rows = slice(first_pair * PAIR, first_pair * PAIR + HALF_D)

    def products():
        for part in range(3):
            yield slice(None), slice(part * HALF_D, (part + 1) * HALF_D), dot_nn(turned, out_ref[part])
        for part, column in ((0, 10), (2, 11)):
            yield head_rows, slice(3 * HALF_D, None), dot_tn(out_ref[part], (place == column).astype(BF))

    @pl.when(seq == 0)
    def _():
        dw_ref[:, 3 * HALF_D :] = sums_ref[...]
        for index, (rows, columns, value) in enumerate(products()):
            dw_ref[rows, columns] = value if index < 3 else dw_ref[rows, columns] + value

    @pl.when(seq > 0)
    def _():
        for rows, columns, value in products():
            dw_ref[rows, columns] += value

    @pl.when(seq == pl.num_programs(0) - 1)
    def _():
        store_split(layout, side_ref[0], dw_ref[...], split_refs)


def heads_backward(half, layout, side, qkv, grads, lse, limits, tokens, sums):
    count = qkv.shape[1]
    seqs = count // MAXLEN
    columns = 3 * HALF_D + SUMS
    weights = row_split(layout, D, columns)
    out = pl.pallas_call(
        partial(backward_kernel, half * HALF, layout),
        grid_spec=pltpu.PrefetchScalarGridSpec(
            num_scalar_prefetch=2,
            grid=(seqs,),
            in_specs=[
                pl.BlockSpec((3, MAXLEN, D), lambda s, *_: (0, s, 0)),
                pl.BlockSpec((MAXLEN, D), lambda s, *_: (s, 0)),
                pl.BlockSpec((1, PAIRS, 2, MAXLEN), lambda s, *_: (s, 0, 0, 0)),
                pl.BlockSpec((MAXLEN, D), lambda s, *_: (s, 0)),
                whole((D, SUMS)),
            ],
            out_specs=[pl.BlockSpec((3, MAXLEN, HALF_D), lambda s, *_: (0, s, 0))]
            + [whole(array.shape) for array in weights],
            scratch_shapes=[pltpu.VMEM((D, columns), F32)],
        ),
        out_shape=[jax.ShapeDtypeStruct((3, count, HALF_D), BF)] + weights,
        compiler_params=params(),
        cost_estimate=cost(9000),
        name="heads_backward",
    )(limits, side, qkv, grads, lse, tokens, sums)
    return out[0], out[1:]


def normal_parts(hidden):
    size = jnp.abs(hidden)
    power = jnp.exp2(hidden * hidden * (-0.5 * LOG2E))
    t = 1.0 / (1.0 + 0.23164190 * size)
    series = t * (
        0.127414796
        + t * (-0.142248368 + t * (0.7107068705 + t * (-0.7265760135 + t * 0.5307027145)))
    )
    tail = series * power
    phi = jnp.where(hidden < 0.0, tail, 1.0 - tail)
    return phi, power


def row_mean(matrix):
    return jnp.mean(matrix, axis=1, keepdims=True)


def norm_rows(hidden):
    center = hidden - row_mean(hidden)
    scale = lax.rsqrt(row_mean(center * center) + EPSILON)
    return center * scale, scale


def norm_back(upstream, unit, scale, gain):
    inner = upstream * gain
    return scale * (inner - row_mean(inner) - unit * row_mean(inner * unit))


def fold_rows(matrix):
    rows, columns = matrix.shape
    return jnp.sum(matrix.reshape(rows // 8, 8, columns), axis=0)


BIAS_ROWS = ("b_query", "zero", "b_value", "b_output", "gain_attn", "shift_attn", "b_outer", "gain_ffn", "shift_ffn", "b_inner")


def load_weights(weights_ref, held_ref, sems):
    def block(c):
        columns = slice(c * D, (c + 1) * D)
        return pltpu.make_async_copy(weights_ref.at[:, columns], held_ref.at[:, columns], sems.at[c])

    return [block(c) for c in range(2 * CHUNKS + 1)]


def ffn_forward_step(wait, tok_ref, att_ref, cot_ref, vec_ref, out_ref, nl_ref, slope_ref, bg_ref, gs_ref,
                     unit_ref, scale_ref, sums_ref, held_ref, act_ref, allbg_ref):
    vec = lambda name, c=0: vec_ref[BIAS_ROWS.index(name) + c : BIAS_ROWS.index(name) + c + 1, :]
    block = lambda c: slice(c * D, (c + 1) * D)
    count = tok_ref.shape[0]
    rows = pl.ds(pl.multiple_of(pl.program_id(0) * count, count), count)
    wait(2 * CHUNKS)
    first = tok_ref[...].astype(F32) + dot_nn(att_ref[...], held_ref[:, block(2 * CHUNKS)]) + vec("b_output")
    unit_one, scale_one = norm_rows(first)
    unit_ref[...] = unit_one
    scale_ref[...] = jnp.broadcast_to(scale_one, scale_ref.shape)
    normed = unit_one * vec("gain_attn") + vec("shift_attn")
    nl = normed.astype(BF)
    nl_ref[...] = nl
    second = normed + vec("b_outer")
    for c in range(CHUNKS):
        wait(c)
        hidden = dot_nn(nl, held_ref[:, block(c)]) + vec("b_inner", c)
        phi, power = normal_parts(hidden)
        active = (hidden * phi).astype(BF)
        slope_ref[:, block(c)] = (phi + hidden * power * DENSITY).astype(slope_ref.dtype)
        act_ref[rows, block(c)] = active
        wait(CHUNKS + c)
        second = second + dot_nn(active, held_ref[:, block(CHUNKS + c)])
    unit_two, scale_two = norm_rows(second)
    out_ref[...] = (unit_two * vec("gain_ffn") + vec("shift_ffn")).astype(BF)
    cot = cot_ref[...].astype(F32)
    sums_ref[0] += fold_rows(cot * unit_two)
    sums_ref[1] += fold_rows(cot)
    grad_second = norm_back(cot, unit_two, scale_two, vec("gain_ffn"))
    gs_ref[...] = grad_second
    bg = grad_second.astype(BF)
    bg_ref[...] = bg
    allbg_ref[rows, :] = bg
    sums_ref[2] += fold_rows(bg.astype(F32))


def ffn_forward_kernel(blocks, layout, side_ref, tok_ref, att_ref, cot_ref, weights_ref, vec_ref, out_ref, nl_ref,
                       slope_ref, bg_ref, gs_ref, unit_ref, scale_ref, sums_ref, *rest):
    split_refs, (held_ref, act_ref, allbg_ref, sems) = rest[:-4], rest[-4:]
    step = pl.program_id(0)
    refs = (tok_ref, att_ref, cot_ref, vec_ref, out_ref, nl_ref, slope_ref, bg_ref, gs_ref, unit_ref, scale_ref,
            sums_ref, held_ref, act_ref, allbg_ref)

    @pl.when(step == 0)
    def _():
        copies = load_weights(weights_ref, held_ref, sems)
        copies[2 * CHUNKS].start()
        for c in range(CHUNKS):
            copies[c].start()
            copies[CHUNKS + c].start()
        sums_ref[...] = jnp.zeros_like(sums_ref)
        ffn_forward_step(lambda c: copies[c].wait(), *refs)

    @pl.when((step > 0) & (step < blocks))
    def _():
        ffn_forward_step(lambda c: None, *refs)

    @pl.when(step >= blocks)
    def _():
        columns = pl.ds(pl.multiple_of((step - blocks) * D, D), D)
        store_split(layout, side_ref[0], dot_tn(act_ref[:, columns], allbg_ref[...]), split_refs)


SLOPE = F32


def ffn_forward(layout, side, tokens, attended, cotangent, weights, vecs, rows=256):
    count = tokens.shape[0]
    blocks = count // rows
    at = lambda i: jnp.minimum(i, blocks - 1)
    narrow = pl.BlockSpec((rows, D), lambda i, _: (at(i), 0))
    shape = jax.ShapeDtypeStruct
    split = row_split(layout, D, FF)
    out = pl.pallas_call(
        partial(ffn_forward_kernel, blocks, layout),
        grid_spec=pltpu.PrefetchScalarGridSpec(
            num_scalar_prefetch=1,
            grid=(blocks + CHUNKS,),
            in_specs=[narrow, narrow, narrow, pl.BlockSpec(memory_space=pl.ANY), whole((16, D))],
            out_specs=[
                narrow, narrow, pl.BlockSpec((rows, FF), lambda i, _: (at(i), 0)), narrow, narrow, narrow,
                pl.BlockSpec((rows, 128), lambda i, _: (at(i), 0)), whole((3, 8, D)),
            ]
            + [pl.BlockSpec((part.shape[0], D), lambda i, _: (0, jnp.maximum(i - blocks, 0))) for part in split],
            scratch_shapes=[
                pltpu.VMEM((D, 2 * FF + D), BF), pltpu.VMEM((count, FF), BF), pltpu.VMEM((count, D), BF),
                pltpu.SemaphoreType.DMA((2 * CHUNKS + 1,)),
            ],
        ),
        out_shape=[
            shape((count, D), BF), shape((count, D), BF), shape((count, FF), SLOPE), shape((count, D), BF),
            shape((count, D), F32), shape((count, D), F32), shape((count, 128), F32), shape((3, 8, D), F32),
        ]
        + split,
        compiler_params=params(),
        cost_estimate=cost(16000),
        name="ffn_forward",
    )(side, tokens, attended, cotangent, weights, vecs)
    return out[:8], out[8:]


def ffn_backward_step(wait, bg_ref, slope_ref, gs_ref, unit_ref, scale_ref, vec_ref, gf_ref, ag_ref, sums_ref,
                      bisum_ref, held_ref, hg_ref, fl_ref):
    vec = lambda name: vec_ref[BIAS_ROWS.index(name) : BIAS_ROWS.index(name) + 1, :]
    block = lambda c: slice(c * D, (c + 1) * D)
    count = bg_ref.shape[0]
    rows = pl.ds(pl.multiple_of(pl.program_id(0) * count, count), count)
    bg = bg_ref[...]
    grad_normed = gs_ref[...]
    for c in range(CHUNKS):
        wait(CHUNKS + c)
        hg = (dot_nt(bg, held_ref[:, block(CHUNKS + c)]) * slope_ref[:, block(c)].astype(F32)).astype(BF)
        hg_ref[rows, block(c)] = hg
        bisum_ref[:, block(c)] += fold_rows(hg.astype(F32))
        wait(c)
        grad_normed = grad_normed + dot_nt(hg, held_ref[:, block(c)])
    unit_one = unit_ref[...]
    sums_ref[0] += fold_rows(grad_normed * unit_one)
    sums_ref[1] += fold_rows(grad_normed)
    grad_first = norm_back(grad_normed, unit_one, scale_ref[:, :1], vec("gain_attn"))
    gf_ref[...] = grad_first
    fl = grad_first.astype(BF)
    fl_ref[rows, :] = fl
    sums_ref[2] += fold_rows(fl.astype(F32))
    wait(2 * CHUNKS)
    ag_ref[...] = dot_nt(fl, held_ref[:, block(2 * CHUNKS)]).astype(BF)


def ffn_backward_kernel(blocks, layout, side_ref, bg_ref, slope_ref, gs_ref, unit_ref, scale_ref, nl_ref, att_ref,
                        weights_ref, vec_ref, gf_ref, ag_ref, sums_ref, bisum_ref, *rest):
    split_refs, (held_ref, hg_ref, fl_ref, turned_ref, sems) = rest[:-5], rest[-5:]
    step = pl.program_id(0)
    refs = (bg_ref, slope_ref, gs_ref, unit_ref, scale_ref, vec_ref, gf_ref, ag_ref, sums_ref, bisum_ref, held_ref,
            hg_ref, fl_ref)

    @pl.when(step == 0)
    def _():
        copies = load_weights(weights_ref, held_ref, sems)
        for c in range(CHUNKS):
            copies[CHUNKS + c].start()
            copies[c].start()
        copies[2 * CHUNKS].start()
        sums_ref[...] = jnp.zeros_like(sums_ref)
        bisum_ref[...] = jnp.zeros_like(bisum_ref)
        turned_ref[...] = nl_ref[...].T
        ffn_backward_step(lambda c: copies[c].wait(), *refs)

    @pl.when((step > 0) & (step < blocks))
    def _():
        ffn_backward_step(lambda c: None, *refs)

    @pl.when((step >= blocks) & (step < blocks + CHUNKS))
    def _():
        columns = pl.ds(pl.multiple_of((step - blocks) * D, D), D)
        store_split(layout, side_ref[0], dot_nn(turned_ref[...], hg_ref[:, columns]), split_refs)

    @pl.when(step == blocks + CHUNKS)
    def _():
        store_split(layout, side_ref[0], dot_tn(att_ref[...], fl_ref[...]), split_refs)


def ffn_backward(layout, side, branch, slope, grad_second, unit_one, scale_one, normed, attended, weights, vecs,
                 rows=256):
    count = branch.shape[0]
    blocks = count // rows
    at = lambda i: jnp.minimum(i, blocks - 1)
    narrow = pl.BlockSpec((rows, D), lambda i, _: (at(i), 0))
    shape = jax.ShapeDtypeStruct
    split = row_split(layout, D, FF + D)
    out = pl.pallas_call(
        partial(ffn_backward_kernel, blocks, layout),
        grid_spec=pltpu.PrefetchScalarGridSpec(
            num_scalar_prefetch=1,
            grid=(blocks + CHUNKS + 1,),
            in_specs=[
                narrow, pl.BlockSpec((rows, FF), lambda i, _: (at(i), 0)), narrow, narrow,
                pl.BlockSpec((rows, 128), lambda i, _: (at(i), 0)), whole((count, D)), whole((count, D)),
                pl.BlockSpec(memory_space=pl.ANY), whole((16, D)),
            ],
            out_specs=[narrow, narrow, whole((3, 8, D)), whole((8, FF))]
            + [pl.BlockSpec((part.shape[0], D), lambda i, _: (0, jnp.maximum(i - blocks, 0))) for part in split],
            scratch_shapes=[
                pltpu.VMEM((D, 2 * FF + D), BF), pltpu.VMEM((count, FF), BF), pltpu.VMEM((count, D), BF),
                pltpu.VMEM((D, count), BF), pltpu.SemaphoreType.DMA((2 * CHUNKS + 1,)),
            ],
        ),
        out_shape=[
            shape((count, D), F32), shape((count, D), BF), shape((3, 8, D), F32), shape((8, FF), F32),
        ]
        + split,
        compiler_params=params(),
        cost_estimate=cost(17000),
        name="ffn_backward",
    )(side, branch, slope, grad_second, unit_one, scale_one, normed, attended, weights, vecs)
    return out[:4], out[4:]


def tokens_kernel(gf_ref, low_ref, high_ref, w_ref, _, out_ref):
    total = gf_ref[...]
    for part in range(3):
        grads = jnp.concatenate([low_ref[part], high_ref[part]], axis=1)
        total = total + dot_nt(grads, w_ref[:, part * D : (part + 1) * D])
    out_ref[...] = total.astype(BF)


def tokens_grad(grad_first, low_grads, high_grads, weights, earlier, rows=256):
    count = grad_first.shape[0]
    grads = pl.BlockSpec((3, rows, HALF_D), lambda i: (0, i, 0))
    return pl.pallas_call(
        tokens_kernel,
        grid=(count // rows,),
        in_specs=[
            pl.BlockSpec((rows, D), lambda i: (i, 0)), grads, grads, whole((D, 3 * D)),
            pl.BlockSpec(memory_space=pl.ANY),
        ],
        out_specs=pl.BlockSpec((rows, D), lambda i: (i, 0)),
        out_shape=jax.ShapeDtypeStruct((count, D), BF),
        compiler_params=params(),
        cost_estimate=cost(3600),
        name="tokens_grad",
    )(grad_first, low_grads, high_grads, weights, earlier)


AXES = ("hi", "lo", "far", "near")
CHIPS = AXES[:3]
MIDDLE = AXES[1:3]


def swap_near(value):
    return lax.ppermute(value, "near", [(0, 1), (1, 0)])


def exchange(value, axes):
    return lax.all_to_all(value, axes, 0, 0, tiled=True)


def gather_rows(block, sizes):
    own, columns = block.shape
    chips = sizes["hi"] * sizes["lo"] * sizes["far"]
    mine = exchange(jnp.broadcast_to(block[None], (chips, own, columns)), CHIPS)
    other = swap_near(mine)
    place = lax.broadcasted_iota(jnp.int32, (chips, 2, own, columns), 1)
    full = jnp.where(place == lax.axis_index("near"), mine[:, None], other[:, None])
    return lax.optimization_barrier(full).reshape(chips * 2 * own, columns)


def pair_sums(layout, side, outs):
    give, keep = split_rows(layout, side, outs)
    return (keep.astype(F32) + swap_near(give).astype(F32)).astype(BF)


def scatter(pair, axes):
    return lax.psum_scatter(pair, axes, scatter_dimension=0, tiled=True)


def to_plane(layout, pair):
    return exchange(pair.reshape(layout[1], -1, pair.shape[1]), MIDDLE)


def to_owner(layout, plane):
    return exchange(plane.reshape(layout[0], layout[2], -1), "hi")


def tied(value, other):
    return value + 0 * other[(0,) * other.ndim].astype(value.dtype)


def total(received):
    sums = received[0].astype(F32)
    for part in range(1, received.shape[0]):
        sums = sums + received[part].astype(F32)
    return sums


def after(value, *others):
    return lax.optimization_barrier((value,) + others)[0]


def body(sizes, tokens, cotangent, lengths, buckets, w_query, w_key, w_value, w_output, b_query, b_value,
         b_output, gain_attn, shift_attn, w_inner, b_inner, w_outer, b_outer, gain_ffn, shift_ffn):
    own = w_query.shape[0]
    devices = D // own
    inner_turned = w_inner.reshape(own, devices, CHUNKS, own).transpose(0, 2, 1, 3).reshape(own, FF)
    outer_blocks = w_outer.reshape(CHUNKS, own, D)
    ffn_pack = jnp.concatenate([inner_turned] + [outer_blocks[c] for c in range(CHUNKS)] + [w_output], axis=1)
    ffn_weights = lax.all_gather(ffn_pack, AXES, axis=0, tiled=True)

    small = jnp.stack(
        [b_query, jnp.zeros_like(b_query), b_value, b_output, gain_attn, shift_attn, b_outer, gain_ffn, shift_ffn],
        axis=1,
    )
    small = jnp.concatenate([small, b_inner.reshape(CHUNKS, own).T], axis=1)
    small = jnp.pad(small, ((0, 0), (0, 128 - small.shape[1])))
    attn_weights = gather_rows(jnp.concatenate([w_query, w_key, w_value, small], axis=1), sizes)
    vecs = attn_weights[:, 3 * D : 3 * D + 16].astype(F32).T

    factor = jnp.where(buckets[0] == 0, 1, jnp.where(buckets[0] == 1, 2, 4)).astype(jnp.int32)
    limits = jnp.minimum(lengths, BLEN * factor).astype(jnp.int32)

    qkv, attended, lse = heads_forward(tokens, attn_weights, vecs, limits)
    layout = (sizes["hi"], sizes["lo"] * sizes["far"], own)
    near = lax.axis_index("near")
    side = near.astype(jnp.int32).reshape(1)
    (layer_out, normed_low, slope, branch, grad_second, unit_one, scale_one, sums_two), outer_grad = ffn_forward(
        layout, side, tokens, attended, cotangent, ffn_weights, vecs
    )
    outer_pair = pair_sums(layout, near, outer_grad)
    outer_got = to_plane(layout, outer_pair)
    (grad_first, attended_grad, sums_one, sums_inner), inner_grad = ffn_backward(
        layout, side, after(branch, outer_pair), slope, grad_second, unit_one, scale_one, normed_low, attended,
        ffn_weights, vecs
    )
    outer_got = after(outer_got, inner_grad[0])
    inner_pair = pair_sums(layout, near, [after(part, outer_got) for part in inner_grad])
    inner_plane = scatter(inner_pair, MIDDLE)
    outer_got = to_owner(layout, total(outer_got).astype(BF))
    sums = jnp.concatenate(
        [jnp.sum(sums_two, axis=1), jnp.sum(sums_one, axis=1), jnp.sum(sums_inner, axis=0).reshape(CHUNKS, D)], axis=0
    )
    sums = jnp.pad(sums, ((0, SUMS - sums.shape[0]), (0, 0))).T

    attended_grad = after(attended_grad, inner_pair)
    low_grads, low_grad = heads_backward(0, layout, side, qkv, attended_grad, lse, limits, tokens, sums)
    outer_got = after(outer_got, low_grad[0])
    low_pair = pair_sums(layout, near, [after(part, outer_got) for part in low_grad])
    low_got = to_plane(layout, low_pair)
    high_grads, high_grad = heads_backward(
        1, layout, side, qkv, after(attended_grad, low_pair), lse, limits, tokens, jnp.zeros_like(sums)
    )
    low_got = after(low_got, high_grad[0])
    inner_own = scatter(tied(inner_plane, high_grads), "hi").astype(F32)
    high_pair = pair_sums(layout, near, [after(part, low_got) for part in high_grad])
    high_got = to_plane(layout, high_pair)
    grad_tokens = tokens_grad(after(grad_first, high_pair), low_grads, high_grads, attn_weights, inner_plane)
    high_got = after(high_got, grad_tokens)
    attn_plane = jnp.concatenate([tied(total(low_got), inner_own).astype(BF), total(high_got).astype(BF)], axis=1)
    attn_own = total(to_owner(layout, attn_plane))
    outer_own = total(outer_got)
    low_own, high_own = jnp.split(attn_own, 2, axis=1)

    sums_own = low_own[:, 3 * HALF_D :] + high_own[:, 3 * HALF_D :]
    heads = lambda part: jnp.concatenate(
        [own_half[:, part * HALF_D : (part + 1) * HALF_D] for own_half in (low_own, high_own)], axis=1
    )
    return (
        layer_out,
        grad_tokens,
        heads(0),
        heads(1),
        heads(2),
        inner_own[:, FF:],
        sums_own[:, 10],
        sums_own[:, 11],
        sums_own[:, 5],
        sums_own[:, 3],
        sums_own[:, 4],
        inner_own[:, :FF].reshape(own, CHUNKS, devices, own).transpose(0, 2, 1, 3).reshape(own, FF),
        sums_own[:, 6 : 6 + CHUNKS].T.reshape(CHUNKS * own),
        outer_own.reshape(own, CHUNKS, D).transpose(1, 0, 2).reshape(CHUNKS * own, D),
        sums_own[:, 2],
        sums_own[:, 0],
        sums_own[:, 1],
    )


def solution(mesh):
    wide, narrow = mesh.shape["wide"], mesh.shape["narrow"]
    sizes = {"hi": wide // 2, "lo": 2, "far": narrow // 2, "near": 2}
    split = jax.sharding.Mesh(mesh.devices.reshape([sizes[axis] for axis in AXES]), AXES)
    rows, vector = P(AXES, None), P(AXES)
    return jax.shard_map(
        partial(body, sizes),
        mesh=split,
        in_specs=(rows, rows, vector, vector) + (rows,) * 4 + (vector,) * 5
        + (rows, vector, rows, vector, vector, vector),
        out_specs=(rows,) * 6 + (vector,) * 5 + (rows, vector, rows, vector, vector, vector),
        check_vma=False,
    )
```

```python
from functools import partial

import jax
import jax.numpy as jnp
from jax import lax
from jax.experimental import pallas as pl
from jax.experimental.pallas import tpu as pltpu
from jax.sharding import PartitionSpec as P

D = 768
H = 12
HD = 64
FF = 3072
BLEN = 128
MAXLEN = 512
SEQ_DEV = 2
PAIR = 2 * HD
PAIRS = H // 2
CHUNKS = FF // D

EPSILON = 1e-12
DENSITY = 0.3989422804014327
HALF_ROOT = 0.7071067811865476
LOG2E = 1.4426950408889634
SCORE_SCALE = LOG2E * HD ** (-0.5)
VMEM = 60 * 1024 * 1024
BF = jnp.bfloat16
F32 = jnp.float32


def cost(megaflops):
    return pl.CostEstimate(flops=int(megaflops * 1e6 * COST_SCALE), bytes_accessed=1, transcendentals=0)


COST_SCALE = 1.0


def params(**kw):
    return pltpu.CompilerParams(vmem_limit_bytes=VMEM, **kw)


def dot_nn(a, b):
    return lax.dot_general(a, b, (((1,), (0,)), ((), ())), preferred_element_type=F32)


def dot_nt(a, b):
    return lax.dot_general(a, b, (((1,), (1,)), ((), ())), preferred_element_type=F32)


def dot_tn(a, b):
    return lax.dot_general(a, b, (((0,), (0,)), ((), ())), preferred_element_type=F32)


def whole(shape):
    return pl.BlockSpec(shape, lambda *_: (0,) * len(shape), pipeline_mode=pl.Buffered(1))


def columns_of(block, width):
    return pl.BlockSpec((D, width), lambda *_: (0, block), pipeline_mode=pl.Buffered(1))


def row_split(layout, rows, columns):
    own = layout[-1]
    if own % 8:
        return [jax.ShapeDtypeStruct((rows, columns), BF)]
    return [jax.ShapeDtypeStruct((rows // 2, columns), BF)] * 2


def store_split(layout, side, value, refs):
    if len(refs) == 1:
        refs[0][...] = value.astype(BF)
        return
    high, middle, own = layout
    parts = value.reshape(high, middle, 2, own, value.shape[1])
    lower, upper = parts[:, :, 0], parts[:, :, 1]
    for ref, part in zip(refs, (jnp.where(side == 0, upper, lower), jnp.where(side == 0, lower, upper))):
        ref[...] = jnp.transpose(part, (1, 0, 2, 3)).reshape(value.shape[0] // 2, value.shape[1]).astype(BF)


def split_rows(layout, side, outs):
    if len(outs) == 2:
        return outs
    high, middle, own = layout
    parts = outs[0].reshape(high, middle, 2, own, -1)
    halves = []
    for place in (1 - side, side):
        part = lax.dynamic_index_in_dim(parts, place, 2, keepdims=False)
        halves.append(part.transpose(1, 0, 2, 3).reshape(high * middle * own, -1))
    return halves


SUMS = 128
HALF = PAIRS // 2
HALF_D = HALF * PAIR


def lane_half(shape):
    return lax.broadcasted_iota(jnp.int32, shape, 1) < HD


def pick_half(matrix, low, head):
    zero = jnp.zeros_like(matrix)
    return jnp.where(low, matrix, zero) if head == 0 else jnp.where(low, zero, matrix)


def mask_last(scores, limit, fill):
    edge = scores.shape[0] - BLEN
    live = lax.broadcasted_iota(jnp.int32, (BLEN, 1), 0) + edge < limit
    last = jnp.where(live, scores[edge:], fill)
    return jnp.concatenate([scores[:edge], last], axis=0) if edge else last


def pair_columns(pair):
    return pl.ds(pl.multiple_of(pair * PAIR, PAIR), PAIR)


def forward_block(keys, limit, pair, qkv_ref, out_ref, lse_ref):
    columns = pair_columns(pair)
    queries = qkv_ref[0, :, columns]
    key_part = qkv_ref[1, :keys, columns]
    value_t = qkv_ref[2, :keys, columns].T
    low = lane_half((keys, PAIR))
    outs = []
    for head in range(2):
        scores = mask_last(dot_nt(pick_half(key_part, low, head), queries), limit, -1e30)
        top = jnp.max(scores, axis=0, keepdims=True) * SCORE_SCALE
        powers = jnp.exp2(scores * SCORE_SCALE - top)
        total = jnp.sum(powers, axis=0, keepdims=True)
        mixed = dot_nn(value_t[head * HD : (head + 1) * HD], powers.astype(BF))
        outs.append(mixed / total)
        lse_ref[0, pair, head : head + 1, :] = top + jnp.log2(total)
    out_ref[:, columns] = jnp.concatenate(outs, axis=0).T.astype(BF)


def backward_block(keys, limit, pair, first_pair, qkv_ref, grad_ref, lse_ref, out_ref):
    columns = here = pair_columns(pair)
    queries = qkv_ref[0, :, columns]
    key_part = qkv_ref[1, :keys, columns]
    value_part = qkv_ref[2, :keys, columns]
    grads = grad_ref[:, columns]
    key_t = key_part.T
    low = lane_half((keys, PAIR))
    scaling = HD ** (-0.5)
    query_grads, key_grads, value_grads = [], [], []
    for head in range(2):
        scores = dot_nt(pick_half(key_part, low, head), queries)
        logits = scores * SCORE_SCALE - lse_ref[0, first_pair + pair, head : head + 1, :]
        weights = jnp.exp2(mask_last(logits, limit, -1e30))
        value_grads.append(dot_nn(weights.astype(BF), grads))
        weight_grad = dot_nt(pick_half(value_part, low, head), grads)
        delta = jnp.sum(weight_grad * weights, axis=0, keepdims=True)
        score_grad = (weights * (weight_grad - delta)).astype(BF)
        key_grads.append(dot_nn(score_grad, queries))
        query_grads.append(dot_nn(key_t[head * HD : (head + 1) * HD], score_grad))
    out_ref[0, :, here] = (jnp.concatenate(query_grads, axis=0) * scaling).T.astype(BF)
    out_ref[1, :keys, here] = (jnp.where(low, key_grads[0], key_grads[1]) * scaling).astype(BF)
    out_ref[2, :keys, here] = jnp.where(low, value_grads[0], value_grads[1]).astype(BF)
    if keys < MAXLEN:
        out_ref[1, keys:, here] = jnp.zeros((MAXLEN - keys, PAIR), BF)
        out_ref[2, keys:, here] = jnp.zeros((MAXLEN - keys, PAIR), BF)


def by_blocks(limit, pairs, block, *refs):
    for blocks in range(1, MAXLEN // BLEN + 1):
        low_edge, high_edge = (blocks - 1) * BLEN, blocks * BLEN

        @pl.when((limit > low_edge) & (limit <= high_edge))
        def _():
            def one_pair(pair, carry):
                block(high_edge, limit, pair, *refs)
                return carry

            lax.fori_loop(0, pairs, one_pair, 0, unroll=2 if pairs % 2 == 0 else pairs)


def forward_kernel(limits_ref, x_ref, w_ref, bias_ref, qkv_ref, out_ref, lse_ref):
    x = x_ref[...]
    for part in range(3):
        rows = dot_nn(x, w_ref[:, part * D : (part + 1) * D])
        qkv_ref[part] = (rows + bias_ref[part : part + 1, :]).astype(BF)
    by_blocks(limits_ref[pl.program_id(0)], PAIRS, forward_block, qkv_ref, out_ref, lse_ref)


def heads_forward(tokens, weights, biases, limits):
    count = tokens.shape[0]
    seqs = count // MAXLEN
    return pl.pallas_call(
        forward_kernel,
        grid_spec=pltpu.PrefetchScalarGridSpec(
            num_scalar_prefetch=1,
            grid=(seqs,),
            in_specs=[pl.BlockSpec((MAXLEN, D), lambda s, _: (s, 0)), whole((D, 3 * D)), whole((16, D))],
            out_specs=[
                pl.BlockSpec((3, MAXLEN, D), lambda s, _: (0, s, 0)),
                pl.BlockSpec((MAXLEN, D), lambda s, _: (s, 0)),
                pl.BlockSpec((1, PAIRS, 2, MAXLEN), lambda s, _: (s, 0, 0, 0)),
            ],
        ),
        out_shape=[
            jax.ShapeDtypeStruct((3, count, D), BF),
            jax.ShapeDtypeStruct((count, D), BF),
            jax.ShapeDtypeStruct((seqs, PAIRS, 2, MAXLEN), F32),
        ],
        compiler_params=params(),
        cost_estimate=cost(6000),
        name="heads_forward",
    )(limits, tokens, weights, biases)


def sums_block(two_ref, one_ref, inner_ref):
    rows = [jnp.sum(ref[k], axis=0, keepdims=True) for ref in (two_ref, one_ref) for k in range(3)]
    inner = jnp.sum(inner_ref[...], axis=0, keepdims=True)
    rows += [inner[:, c * D : (c + 1) * D] for c in range(CHUNKS)]
    return jnp.concatenate(rows + [jnp.zeros((SUMS - len(rows), D), F32)], axis=0).T


def store_columns(layout, side, value, refs, start):
    columns = slice(start, start + value.shape[1])
    store_split(layout, side, value, [ref.at[:, columns] for ref in refs])


def backward_kernel(half, layout, limits_ref, side_ref, qkv_ref, grad_ref, lse_ref, tok_ref, *refs):
    sum_refs, refs = (refs[:3], refs[3:]) if half == 0 else ((), refs)
    out_ref, mark_ref, split_refs, held_ref = refs[0], refs[1], refs[2:-1], refs[-1]
    seq = pl.program_id(0)
    by_blocks(limits_ref[seq], HALF, backward_block, half * HALF, qkv_ref, grad_ref, lse_ref, out_ref)
    rows = pl.ds(pl.multiple_of(seq * MAXLEN, MAXLEN), MAXLEN)
    held_ref[:, rows, :] = out_ref[...]

    @pl.when(seq == pl.num_programs(0) - 1)
    def _():
        count = tok_ref.shape[0]
        turned = tok_ref[...].T
        for part in range(3):
            store_columns(layout, side_ref[0], dot_nn(turned, held_ref[part]), split_refs, part * HALF_D)
        place = lax.broadcasted_iota(jnp.int32, (count, SUMS), 1)
        own = sum(
            dot_tn(held_ref[part], (place == column).astype(BF)) for part, column in ((0, 10), (2, 11))
        )
        rest = jnp.zeros((HALF_D, SUMS), F32)
        sums = jnp.concatenate([own, rest] if half == 0 else [rest, own], axis=0)
        if sum_refs:
            sums = sums + sums_block(*sum_refs)
        store_columns(layout, side_ref[0], sums, split_refs, 3 * HALF_D)
        mark_ref[...] = jnp.zeros_like(mark_ref)


def heads_backward(half, layout, side, qkv, grads, lse, limits, tokens, sums=()):
    count = qkv.shape[1]
    seqs = count // MAXLEN
    columns = 3 * HALF_D + SUMS
    weights = row_split(layout, D, columns)
    mark = jax.ShapeDtypeStruct((16, 128), BF)
    out = pl.pallas_call(
        partial(backward_kernel, half, layout),
        grid_spec=pltpu.PrefetchScalarGridSpec(
            num_scalar_prefetch=2,
            grid=(seqs,),
            in_specs=[
                pl.BlockSpec((3, MAXLEN, HALF_D), lambda s, *_: (0, s, half)),
                pl.BlockSpec((MAXLEN, HALF_D), lambda s, *_: (s, half)),
                pl.BlockSpec((1, PAIRS, 2, MAXLEN), lambda s, *_: (s, 0, 0, 0)),
                whole((count, D)),
            ]
            + [whole(array.shape) for array in sums],
            out_specs=[pl.BlockSpec((3, MAXLEN, HALF_D), lambda s, *_: (0, s, 0))]
            + [whole(array.shape) for array in [mark] + weights],
            scratch_shapes=[pltpu.VMEM((3, count, HALF_D), BF)],
        ),
        out_shape=[jax.ShapeDtypeStruct((3, count, HALF_D), BF), mark] + weights,
        compiler_params=params(),
        cost_estimate=cost(9000),
        name="heads_backward",
    )(limits, side, qkv, grads, lse, tokens, *sums)
    return out[0], out[1], out[2:]


def normal_parts(hidden):
    return 0.5 + 0.5 * lax.erf(hidden * HALF_ROOT), jnp.exp2(hidden * hidden * (-0.5 * LOG2E))


def row_mean(matrix):
    return jnp.mean(matrix, axis=1, keepdims=True)


def norm_rows(hidden):
    center = hidden - row_mean(hidden)
    scale = lax.rsqrt(row_mean(center * center) + EPSILON)
    return center * scale, scale


def norm_back(upstream, unit, scale, gain):
    inner = upstream * gain
    return scale * (inner - row_mean(inner) - unit * row_mean(inner * unit))


def fold_rows(matrix):
    rows, columns = matrix.shape
    return jnp.sum(matrix.reshape(rows // 8, 8, columns), axis=0)


BIAS_ROWS = ("b_query", "zero", "b_value", "b_output", "gain_attn", "shift_attn", "b_outer", "gain_ffn", "shift_ffn", "b_inner")


def load_weights(weights_ref, held_ref, sems):
    def block(c):
        columns = slice(c * D, (c + 1) * D)
        return pltpu.make_async_copy(weights_ref.at[:, columns], held_ref.at[:, columns], sems.at[c])

    return [block(c) for c in range(2 * CHUNKS + 1)]


def ffn_forward_step(wait, tok_ref, att_ref, cot_ref, vec_ref, out_ref, nl_ref, slope_ref, bg_ref, gs_ref,
                     unit_ref, scale_ref, sums_ref, held_ref, act_ref, allbg_ref):
    vec = lambda name, c=0: vec_ref[BIAS_ROWS.index(name) + c : BIAS_ROWS.index(name) + c + 1, :]
    block = lambda c: slice(c * D, (c + 1) * D)
    count = tok_ref.shape[0]
    rows = pl.ds(pl.multiple_of(pl.program_id(0) * count, count), count)
    wait(2 * CHUNKS)
    first = tok_ref[...].astype(F32) + dot_nn(att_ref[...], held_ref[:, block(2 * CHUNKS)]) + vec("b_output")
    unit_one, scale_one = norm_rows(first)
    unit_ref[...] = unit_one
    scale_ref[...] = jnp.broadcast_to(scale_one, scale_ref.shape)
    normed = unit_one * vec("gain_attn") + vec("shift_attn")
    nl = normed.astype(BF)
    nl_ref[...] = nl
    second = normed + vec("b_outer")
    for c in range(CHUNKS):
        wait(c)
        hidden = dot_nn(nl, held_ref[:, block(c)]) + vec("b_inner", c)
        phi, power = normal_parts(hidden)
        active = (hidden * phi).astype(BF)
        slope_ref[:, block(c)] = (phi + hidden * power * DENSITY).astype(slope_ref.dtype)
        act_ref[rows, block(c)] = active
        wait(CHUNKS + c)
        second = second + dot_nn(active, held_ref[:, block(CHUNKS + c)])
    unit_two, scale_two = norm_rows(second)
    out_ref[...] = (unit_two * vec("gain_ffn") + vec("shift_ffn")).astype(BF)
    cot = cot_ref[...].astype(F32)
    sums_ref[0] += fold_rows(cot * unit_two)
    sums_ref[1] += fold_rows(cot)
    grad_second = norm_back(cot, unit_two, scale_two, vec("gain_ffn"))
    gs_ref[...] = grad_second
    bg = grad_second.astype(BF)
    bg_ref[...] = bg
    allbg_ref[rows, :] = bg
    sums_ref[2] += fold_rows(bg.astype(F32))


def ffn_forward_kernel(blocks, layout, side_ref, tok_ref, att_ref, cot_ref, weights_ref, vec_ref, out_ref, nl_ref,
                       slope_ref, bg_ref, gs_ref, unit_ref, scale_ref, sums_ref, *rest):
    split_refs, (held_ref, act_ref, allbg_ref, sems) = rest[:-4], rest[-4:]
    step = pl.program_id(0)
    refs = (tok_ref, att_ref, cot_ref, vec_ref, out_ref, nl_ref, slope_ref, bg_ref, gs_ref, unit_ref, scale_ref,
            sums_ref, held_ref, act_ref, allbg_ref)

    @pl.when(step == 0)
    def _():
        copies = load_weights(weights_ref, held_ref, sems)
        copies[2 * CHUNKS].start()
        for c in range(CHUNKS):
            copies[c].start()
            copies[CHUNKS + c].start()
        sums_ref[...] = jnp.zeros_like(sums_ref)
        ffn_forward_step(lambda c: copies[c].wait(), *refs)

    @pl.when((step > 0) & (step < blocks))
    def _():
        ffn_forward_step(lambda c: None, *refs)

    @pl.when(step >= blocks)
    def _():
        columns = pl.ds(pl.multiple_of((step - blocks) * D, D), D)
        store_split(layout, side_ref[0], dot_tn(act_ref[:, columns], allbg_ref[...]), split_refs)


SLOPE = F32


def ffn_forward(layout, side, tokens, attended, cotangent, weights, vecs, rows=256):
    count = tokens.shape[0]
    blocks = count // rows
    at = lambda i: jnp.minimum(i, blocks - 1)
    narrow = pl.BlockSpec((rows, D), lambda i, _: (at(i), 0))
    shape = jax.ShapeDtypeStruct
    split = row_split(layout, D, FF)
    out = pl.pallas_call(
        partial(ffn_forward_kernel, blocks, layout),
        grid_spec=pltpu.PrefetchScalarGridSpec(
            num_scalar_prefetch=1,
            grid=(blocks + CHUNKS,),
            in_specs=[narrow, narrow, narrow, pl.BlockSpec(memory_space=pl.ANY), whole((16, D))],
            out_specs=[
                narrow, narrow, pl.BlockSpec((rows, FF), lambda i, _: (at(i), 0)), narrow, narrow, narrow,
                pl.BlockSpec((rows, 128), lambda i, _: (at(i), 0)), whole((3, 8, D)),
            ]
            + [pl.BlockSpec((part.shape[0], D), lambda i, _: (0, jnp.maximum(i - blocks, 0))) for part in split],
            scratch_shapes=[
                pltpu.VMEM((D, 2 * FF + D), BF), pltpu.VMEM((count, FF), BF), pltpu.VMEM((count, D), BF),
                pltpu.SemaphoreType.DMA((2 * CHUNKS + 1,)),
            ],
        ),
        out_shape=[
            shape((count, D), BF), shape((count, D), BF), shape((count, FF), SLOPE), shape((count, D), BF),
            shape((count, D), F32), shape((count, D), F32), shape((count, 128), F32), shape((3, 8, D), F32),
        ]
        + split,
        compiler_params=params(),
        cost_estimate=cost(16000),
        name="ffn_forward",
    )(side, tokens, attended, cotangent, weights, vecs)
    return out[:8], out[8:]


def ffn_backward_step(wait, bg_ref, slope_ref, gs_ref, unit_ref, scale_ref, vec_ref, gf_ref, ag_ref, sums_ref,
                      bisum_ref, held_ref, hg_ref, fl_ref):
    vec = lambda name: vec_ref[BIAS_ROWS.index(name) : BIAS_ROWS.index(name) + 1, :]
    block = lambda c: slice(c * D, (c + 1) * D)
    count = bg_ref.shape[0]
    rows = pl.ds(pl.multiple_of(pl.program_id(0) * count, count), count)
    bg = bg_ref[...]
    grad_normed = gs_ref[...]
    for c in range(CHUNKS):
        wait(CHUNKS + c)
        hg = (dot_nt(bg, held_ref[:, block(CHUNKS + c)]) * slope_ref[:, block(c)].astype(F32)).astype(BF)
        hg_ref[rows, block(c)] = hg
        bisum_ref[:, block(c)] += fold_rows(hg.astype(F32))
        wait(c)
        grad_normed = grad_normed + dot_nt(hg, held_ref[:, block(c)])
    unit_one = unit_ref[...]
    sums_ref[0] += fold_rows(grad_normed * unit_one)
    sums_ref[1] += fold_rows(grad_normed)
    grad_first = norm_back(grad_normed, unit_one, scale_ref[:, :1], vec("gain_attn"))
    gf_ref[...] = grad_first
    fl = grad_first.astype(BF)
    fl_ref[rows, :] = fl
    sums_ref[2] += fold_rows(fl.astype(F32))
    wait(2 * CHUNKS)
    ag_ref[...] = dot_nt(fl, held_ref[:, block(2 * CHUNKS)]).astype(BF)


def ffn_backward_kernel(blocks, layout, side_ref, bg_ref, slope_ref, gs_ref, unit_ref, scale_ref, nl_ref, att_ref,
                        weights_ref, vec_ref, gf_ref, ag_ref, sums_ref, bisum_ref, *rest):
    split_refs, (held_ref, hg_ref, fl_ref, turned_ref, left_ref, sems) = rest[:-6], rest[-6:]
    step = pl.program_id(0)
    refs = (bg_ref, slope_ref, gs_ref, unit_ref, scale_ref, vec_ref, gf_ref, ag_ref, sums_ref, bisum_ref, held_ref,
            hg_ref, fl_ref)

    def lefts():
        last = 2 * CHUNKS + 1
        return [
            pltpu.make_async_copy(ref, left_ref.at[k], sems.at[last + k]) for k, ref in enumerate((nl_ref, att_ref))
        ]

    @pl.when(step == 0)
    def _():
        copies = load_weights(weights_ref, held_ref, sems)
        for c in range(CHUNKS):
            copies[CHUNKS + c].start()
            copies[c].start()
        copies[2 * CHUNKS].start()
        sums_ref[...] = jnp.zeros_like(sums_ref)
        bisum_ref[...] = jnp.zeros_like(bisum_ref)
        ffn_backward_step(lambda c: copies[c].wait(), *refs)

    @pl.when((step > 0) & (step < blocks))
    def _():
        ffn_backward_step(lambda c: None, *refs)

    @pl.when(step == 1)
    def _():
        for copy in lefts():
            copy.start()

    @pl.when(step == blocks)
    def _():
        for copy in lefts():
            copy.wait()
        turned_ref[...] = left_ref[0].T

    @pl.when((step >= blocks) & (step < blocks + CHUNKS))
    def _():
        columns = pl.ds(pl.multiple_of((step - blocks) * D, D), D)
        store_split(layout, side_ref[0], dot_nn(turned_ref[...], hg_ref[:, columns]), split_refs)

    @pl.when(step == blocks + CHUNKS)
    def _():
        store_split(layout, side_ref[0], dot_tn(left_ref[1], fl_ref[...]), split_refs)


def ffn_backward(layout, side, branch, slope, grad_second, unit_one, scale_one, normed, attended, weights, vecs,
                 rows=256):
    count = branch.shape[0]
    blocks = count // rows
    at = lambda i: jnp.minimum(i, blocks - 1)
    narrow = pl.BlockSpec((rows, D), lambda i, _: (at(i), 0))
    shape = jax.ShapeDtypeStruct
    split = row_split(layout, D, FF + D)
    out = pl.pallas_call(
        partial(ffn_backward_kernel, blocks, layout),
        grid_spec=pltpu.PrefetchScalarGridSpec(
            num_scalar_prefetch=1,
            grid=(blocks + CHUNKS + 1,),
            in_specs=[
                narrow, pl.BlockSpec((rows, FF), lambda i, _: (at(i), 0)), narrow, narrow,
                pl.BlockSpec((rows, 128), lambda i, _: (at(i), 0)),
            ]
            + [pl.BlockSpec(memory_space=pl.ANY)] * 3
            + [whole((16, D))],
            out_specs=[narrow, narrow, whole((3, 8, D)), whole((8, FF))]
            + [pl.BlockSpec((part.shape[0], D), lambda i, _: (0, jnp.maximum(i - blocks, 0))) for part in split],
            scratch_shapes=[
                pltpu.VMEM((D, 2 * FF + D), BF), pltpu.VMEM((count, FF), BF), pltpu.VMEM((count, D), BF),
                pltpu.VMEM((D, count), BF), pltpu.VMEM((2, count, D), BF),
                pltpu.SemaphoreType.DMA((2 * CHUNKS + 3,)),
            ],
        ),
        out_shape=[
            shape((count, D), F32), shape((count, D), BF), shape((3, 8, D), F32), shape((8, FF), F32),
        ]
        + split,
        compiler_params=params(),
        cost_estimate=cost(17000),
        name="ffn_backward",
    )(side, branch, slope, grad_second, unit_one, scale_one, normed, attended, weights, vecs)
    return out[:4], out[4:]


def tokens_kernel(gf_ref, low_ref, high_ref, w_ref, _, out_ref):
    total = gf_ref[...]
    for part in range(3):
        grads = jnp.concatenate([low_ref[part], high_ref[part]], axis=1)
        total = total + dot_nt(grads, w_ref[:, part * D : (part + 1) * D])
    out_ref[...] = total.astype(BF)


def tokens_grad(grad_first, low_grads, high_grads, weights, earlier, rows=256):
    count = grad_first.shape[0]
    grads = pl.BlockSpec((3, rows, HALF_D), lambda i: (0, i, 0))
    return pl.pallas_call(
        tokens_kernel,
        grid=(count // rows,),
        in_specs=[
            pl.BlockSpec((rows, D), lambda i: (i, 0)), grads, grads, whole((D, 3 * D)),
            pl.BlockSpec(memory_space=pl.ANY),
        ],
        out_specs=pl.BlockSpec((rows, D), lambda i: (i, 0)),
        out_shape=jax.ShapeDtypeStruct((count, D), BF),
        compiler_params=params(),
        cost_estimate=cost(3600),
        name="tokens_grad",
    )(grad_first, low_grads, high_grads, weights, earlier)


AXES = ("hi", "lo", "far", "near")
CHIPS = AXES[:3]
MIDDLE = AXES[1:3]


def swap_near(value):
    return lax.ppermute(value, "near", [(0, 1), (1, 0)])


def exchange(value, axes):
    return lax.all_to_all(value, axes, 0, 0, tiled=True)


def spread(value, axes, count):
    return exchange(jnp.broadcast_to(value[None], (count,) + value.shape), axes)


def join_rows(layout, mine):
    other = swap_near(mine)
    high, middle, own = layout
    columns = mine.shape[-1]
    place = lax.broadcasted_iota(jnp.int32, (high, middle, 2, own, columns), 2)
    pick = lambda part: part.transpose(1, 0, 2, 3)[:, :, None]
    full = jnp.where(place == lax.axis_index("near"), pick(mine), pick(other))
    return lax.optimization_barrier(full).reshape(-1, columns)


def pair_sums(layout, side, outs):
    give, keep = split_rows(layout, side, outs)
    return (keep.astype(F32) + swap_near(give).astype(F32)).astype(BF)


def scatter(pair, axes):
    return lax.psum_scatter(pair, axes, scatter_dimension=0, tiled=True)


def to_plane(layout, pair):
    return exchange(pair.reshape(layout[1], -1, pair.shape[1]), MIDDLE)


def to_owner(layout, plane):
    return exchange(plane.reshape(layout[0], layout[2], -1), "hi")


def after(value, *others):
    return lax.optimization_barrier((value,) + others)[0]


def total(received, behind=None):
    sums = received[0].astype(F32)
    for part in range(1, received.shape[0]):
        sums = sums + received[part].astype(F32)
    if behind is not None:
        none = 0 * behind[:, : sums.shape[1]].astype(F32)
        sums = sums + jnp.pad(none, ((0, sums.shape[0] - none.shape[0]), (0, 0)))
    return sums


def body(sizes, tokens, cotangent, lengths, buckets, w_query, w_key, w_value, w_output, b_query, b_value,
         b_output, gain_attn, shift_attn, w_inner, b_inner, w_outer, b_outer, gain_ffn, shift_ffn):
    own = w_query.shape[0]
    devices = D // own
    inner_turned = w_inner.reshape(own, devices, CHUNKS, own).transpose(0, 2, 1, 3).reshape(own, FF)
    outer_blocks = w_outer.reshape(CHUNKS, own, D)
    ffn_pack = jnp.concatenate([inner_turned] + [outer_blocks[c] for c in range(CHUNKS)] + [w_output], axis=1)
    ffn_weights = lax.all_gather(ffn_pack, AXES, axis=0, tiled=True)

    small = jnp.stack(
        [b_query, jnp.zeros_like(b_query), b_value, b_output, gain_attn, shift_attn, b_outer, gain_ffn, shift_ffn],
        axis=1,
    )
    small = jnp.concatenate([small, b_inner.reshape(CHUNKS, own).T], axis=1)
    small = jnp.pad(small, ((0, 0), (0, 128 - small.shape[1])))
    layout = (sizes["hi"], sizes["lo"] * sizes["far"], own)
    attn_pack = jnp.concatenate([w_query, w_key, w_value, small], axis=1)
    attn_mine = spread(spread(attn_pack, "hi", layout[0]), MIDDLE, layout[1])
    attn_weights = join_rows(layout, attn_mine)
    vecs = attn_weights[:, 3 * D : 3 * D + 16].astype(F32).T

    factor = jnp.where(buckets[0] == 0, 1, jnp.where(buckets[0] == 1, 2, 4)).astype(jnp.int32)
    limits = jnp.minimum(lengths, BLEN * factor).astype(jnp.int32)

    qkv, attended, lse = heads_forward(tokens, attn_weights, vecs, limits)
    near = lax.axis_index("near")
    side = near.astype(jnp.int32).reshape(1)
    (layer_out, normed_low, slope, branch, grad_second, unit_one, scale_one, sums_two), outer_grad = ffn_forward(
        layout, side, tokens, attended, cotangent, ffn_weights, vecs
    )
    outer_pair = pair_sums(layout, near, outer_grad)
    outer_got = to_plane(layout, outer_pair)
    (grad_first, attended_grad, sums_one, sums_inner), inner_grad = ffn_backward(
        layout, side, after(branch, outer_pair), slope, grad_second, unit_one, scale_one, normed_low, attended,
        ffn_weights, vecs
    )
    outer_got = after(outer_got, inner_grad[0])
    inner_pair = pair_sums(layout, near, [after(part, outer_got) for part in inner_grad])
    inner_plane = scatter(inner_pair, MIDDLE)
    outer_got = to_owner(layout, total(outer_got).astype(BF))
    attended_grad = after(attended_grad, inner_pair)
    low_grads, _, low_grad = heads_backward(
        0, layout, side, qkv, attended_grad, lse, limits, tokens, (sums_two, sums_one, sums_inner)
    )
    outer_got = after(outer_got, low_grad[0])
    low_pair = pair_sums(layout, near, [after(part, outer_got) for part in low_grad])
    low_got = to_plane(layout, low_pair)
    high_grads, mark, high_grad = heads_backward(
        1, layout, side, qkv, after(attended_grad, low_pair), lse, limits, tokens
    )
    low_got = after(low_got, high_grad[0])
    inner_own = scatter(inner_plane.at[:16, :128].add(mark), "hi").astype(F32)
    high_pair = pair_sums(layout, near, [after(part, low_got) for part in high_grad])
    high_got = to_plane(layout, high_pair)
    grad_tokens = tokens_grad(after(grad_first, high_pair), low_grads, high_grads, attn_weights, inner_plane)
    high_got = after(high_got, grad_tokens)
    attn_plane = jnp.concatenate([total(low_got, inner_own).astype(BF), total(high_got).astype(BF)], axis=1)
    attn_own = total(to_owner(layout, attn_plane))
    outer_own = total(outer_got)
    low_own, high_own = jnp.split(attn_own, 2, axis=1)

    sums_own = low_own[:, 3 * HALF_D :] + high_own[:, 3 * HALF_D :]
    heads = lambda part: jnp.concatenate(
        [own_half[:, part * HALF_D : (part + 1) * HALF_D] for own_half in (low_own, high_own)], axis=1
    )
    return (
        layer_out,
        grad_tokens,
        heads(0),
        heads(1),
        heads(2),
        inner_own[:, FF:],
        sums_own[:, 10],
        sums_own[:, 11],
        sums_own[:, 5],
        sums_own[:, 3],
        sums_own[:, 4],
        inner_own[:, :FF].reshape(own, CHUNKS, devices, own).transpose(0, 2, 1, 3).reshape(own, FF),
        sums_own[:, 6 : 6 + CHUNKS].T.reshape(CHUNKS * own),
        outer_own.reshape(own, CHUNKS, D).transpose(1, 0, 2).reshape(CHUNKS * own, D),
        sums_own[:, 2],
        sums_own[:, 0],
        sums_own[:, 1],
    )


def solution(mesh):
    wide, narrow = mesh.shape["wide"], mesh.shape["narrow"]
    sizes = {"hi": wide // 2, "lo": 2, "far": narrow // 2, "near": 2}
    split = jax.sharding.Mesh(mesh.devices.reshape([sizes[axis] for axis in AXES]), AXES)
    rows, vector = P(AXES, None), P(AXES)
    return jax.shard_map(
        partial(body, sizes),
        mesh=split,
        in_specs=(rows, rows, vector, vector) + (rows,) * 4 + (vector,) * 5
        + (rows, vector, rows, vector, vector, vector),
        out_specs=(rows,) * 6 + (vector,) * 5 + (rows, vector, rows, vector, vector, vector),
        check_vma=False,
    )
```

```python
from functools import partial

import jax
import jax.numpy as jnp
from jax import lax
from jax.experimental import pallas as pl
from jax.experimental.pallas import tpu as pltpu
from jax.sharding import PartitionSpec as P

D = 768
H = 12
HD = 64
FF = 3072
BLEN = 128
MAXLEN = 512
SEQ_DEV = 2
PAIR = 2 * HD
PAIRS = H // 2
CHUNKS = FF // D

EPSILON = 1e-12
DENSITY = 0.3989422804014327
HALF_ROOT = 0.7071067811865476
LOG2E = 1.4426950408889634
SCORE_SCALE = LOG2E * HD ** (-0.5)
VMEM = 60 * 1024 * 1024
BF = jnp.bfloat16
F32 = jnp.float32


def cost(megaflops):
    return pl.CostEstimate(flops=int(megaflops * 1e6 * COST_SCALE), bytes_accessed=1, transcendentals=0)


COST_SCALE = 1.0


def params(**kw):
    return pltpu.CompilerParams(vmem_limit_bytes=VMEM, **kw)


def dot_nn(a, b):
    return lax.dot_general(a, b, (((1,), (0,)), ((), ())), preferred_element_type=F32)


def dot_nt(a, b):
    return lax.dot_general(a, b, (((1,), (1,)), ((), ())), preferred_element_type=F32)


def dot_tn(a, b):
    return lax.dot_general(a, b, (((0,), (0,)), ((), ())), preferred_element_type=F32)


def whole(shape):
    return pl.BlockSpec(shape, lambda *_: (0,) * len(shape), pipeline_mode=pl.Buffered(1))


def columns_of(block, width):
    return pl.BlockSpec((D, width), lambda *_: (0, block), pipeline_mode=pl.Buffered(1))


def row_split(layout, rows, columns):
    own = layout[-1]
    if own % 8:
        return [jax.ShapeDtypeStruct((rows, columns), BF)]
    return [jax.ShapeDtypeStruct((rows // 2, columns), BF)] * 2


def store_split(layout, side, value, refs):
    if len(refs) == 1:
        refs[0][...] = value.astype(BF)
        return
    high, middle, own = layout
    parts = value.reshape(high, middle, 2, own, value.shape[1])
    lower, upper = parts[:, :, 0], parts[:, :, 1]
    for ref, part in zip(refs, (jnp.where(side == 0, upper, lower), jnp.where(side == 0, lower, upper))):
        ref[...] = jnp.transpose(part, (1, 0, 2, 3)).reshape(value.shape[0] // 2, value.shape[1]).astype(BF)


def split_rows(layout, side, outs):
    if len(outs) == 2:
        return outs
    high, middle, own = layout
    parts = outs[0].reshape(high, middle, 2, own, -1)
    halves = []
    for place in (1 - side, side):
        part = lax.dynamic_index_in_dim(parts, place, 2, keepdims=False)
        halves.append(part.transpose(1, 0, 2, 3).reshape(high * middle * own, -1))
    return halves


def pack_kernel(inner_ref, outer_ref, output_ref, pack_ref):
    own = inner_ref.shape[0]
    inner, outer = inner_ref[...].astype(F32), outer_ref[...].astype(F32)
    for c in range(CHUNKS):
        starts = range(own * c, FF, CHUNKS * own)
        block = jnp.concatenate([inner[:, start : start + own] for start in starts], axis=1)
        pack_ref[:, c * D : (c + 1) * D] = block.astype(BF)
        pack_ref[:, FF + c * D : FF + (c + 1) * D] = outer[c * own : (c + 1) * own].astype(BF)
    pack_ref[:, 2 * FF :] = output_ref[...]


def ffn_pack(w_inner, w_outer, w_output):
    own = w_inner.shape[0]
    if own % 8:
        turned = w_inner.reshape(own, -1, CHUNKS, own).transpose(0, 2, 1, 3).reshape(own, FF)
        blocks = w_outer.reshape(CHUNKS, own, D)
        return jnp.concatenate([turned] + [blocks[c] for c in range(CHUNKS)] + [w_output], axis=1)
    return pl.pallas_call(
        pack_kernel,
        out_shape=jax.ShapeDtypeStruct((own, 2 * FF + D), BF),
        compiler_params=params(),
        name="ffn_pack",
    )(w_inner, w_outer, w_output)


SUMS = 128
HALF = PAIRS // 2
HALF_D = HALF * PAIR


def lane_half(shape):
    return lax.broadcasted_iota(jnp.int32, shape, 1) < HD


def pick_half(matrix, low, head):
    zero = jnp.zeros_like(matrix)
    return jnp.where(low, matrix, zero) if head == 0 else jnp.where(low, zero, matrix)


def mask_last(scores, limit, fill):
    edge = scores.shape[0] - BLEN
    live = lax.broadcasted_iota(jnp.int32, (BLEN, 1), 0) + edge < limit
    last = jnp.where(live, scores[edge:], fill)
    return jnp.concatenate([scores[:edge], last], axis=0) if edge else last


def pair_columns(pair):
    return pl.ds(pl.multiple_of(pair * PAIR, PAIR), PAIR)


def forward_block(keys, limit, pair, qkv_ref, out_ref, lse_ref):
    columns = pair_columns(pair)
    queries = qkv_ref[0, :, columns]
    key_part = qkv_ref[1, :keys, columns]
    value_t = qkv_ref[2, :keys, columns].T
    low = lane_half((keys, PAIR))
    outs = []
    for head in range(2):
        scores = mask_last(dot_nt(pick_half(key_part, low, head), queries), limit, -1e30)
        top = jnp.max(scores, axis=0, keepdims=True) * SCORE_SCALE
        powers = jnp.exp2(scores * SCORE_SCALE - top)
        total = jnp.sum(powers, axis=0, keepdims=True)
        mixed = dot_nn(value_t[head * HD : (head + 1) * HD], powers.astype(BF))
        outs.append(mixed / total)
        lse_ref[0, pair, head : head + 1, :] = top + jnp.log2(total)
    out_ref[:, columns] = jnp.concatenate(outs, axis=0).T.astype(BF)


def backward_block(keys, limit, pair, first_pair, qkv_ref, grad_ref, lse_ref, out_ref):
    columns = here = pair_columns(pair)
    queries = qkv_ref[0, :, columns]
    key_part = qkv_ref[1, :keys, columns]
    value_part = qkv_ref[2, :keys, columns]
    grads = grad_ref[:, columns]
    key_t = key_part.T
    low = lane_half((keys, PAIR))
    scaling = HD ** (-0.5)
    query_grads, key_grads, value_grads = [], [], []
    for head in range(2):
        scores = dot_nt(pick_half(key_part, low, head), queries)
        logits = scores * SCORE_SCALE - lse_ref[0, first_pair + pair, head : head + 1, :]
        weights = jnp.exp2(mask_last(logits, limit, -1e30))
        value_grads.append(dot_nn(weights.astype(BF), grads))
        weight_grad = dot_nt(pick_half(value_part, low, head), grads)
        delta = jnp.sum(weight_grad * weights, axis=0, keepdims=True)
        score_grad = (weights * (weight_grad - delta)).astype(BF)
        key_grads.append(dot_nn(score_grad, queries))
        query_grads.append(dot_nn(key_t[head * HD : (head + 1) * HD], score_grad))
    out_ref[0, :, here] = (jnp.concatenate(query_grads, axis=0) * scaling).T.astype(BF)
    out_ref[1, :keys, here] = (jnp.where(low, key_grads[0], key_grads[1]) * scaling).astype(BF)
    out_ref[2, :keys, here] = jnp.where(low, value_grads[0], value_grads[1]).astype(BF)
    if keys < MAXLEN:
        out_ref[1, keys:, here] = jnp.zeros((MAXLEN - keys, PAIR), BF)
        out_ref[2, keys:, here] = jnp.zeros((MAXLEN - keys, PAIR), BF)


def by_blocks(limit, pairs, block, *refs):
    for blocks in range(1, MAXLEN // BLEN + 1):
        low_edge, high_edge = (blocks - 1) * BLEN, blocks * BLEN

        @pl.when((limit > low_edge) & (limit <= high_edge))
        def _():
            def one_pair(pair, carry):
                block(high_edge, limit, pair, *refs)
                return carry

            lax.fori_loop(0, pairs, one_pair, 0, unroll=2 if pairs % 2 == 0 else pairs)


def forward_kernel(limits_ref, x_ref, w_ref, bias_ref, qkv_ref, out_ref, lse_ref):
    x = x_ref[...]
    for part in range(3):
        rows = dot_nn(x, w_ref[:, part * D : (part + 1) * D])
        qkv_ref[part] = (rows + bias_ref[part : part + 1, :]).astype(BF)
    by_blocks(limits_ref[pl.program_id(0)], PAIRS, forward_block, qkv_ref, out_ref, lse_ref)


def heads_forward(tokens, weights, biases, limits):
    count = tokens.shape[0]
    seqs = count // MAXLEN
    return pl.pallas_call(
        forward_kernel,
        grid_spec=pltpu.PrefetchScalarGridSpec(
            num_scalar_prefetch=1,
            grid=(seqs,),
            in_specs=[pl.BlockSpec((MAXLEN, D), lambda s, _: (s, 0)), whole((D, 3 * D)), whole((16, D))],
            out_specs=[
                pl.BlockSpec((3, MAXLEN, D), lambda s, _: (0, s, 0)),
                pl.BlockSpec((MAXLEN, D), lambda s, _: (s, 0)),
                pl.BlockSpec((1, PAIRS, 2, MAXLEN), lambda s, _: (s, 0, 0, 0)),
            ],
        ),
        out_shape=[
            jax.ShapeDtypeStruct((3, count, D), BF),
            jax.ShapeDtypeStruct((count, D), BF),
            jax.ShapeDtypeStruct((seqs, PAIRS, 2, MAXLEN), F32),
        ],
        compiler_params=params(),
        cost_estimate=cost(6000),
        name="heads_forward",
    )(limits, tokens, weights, biases)


def sums_block(two_ref, one_ref, inner_ref):
    rows = [jnp.sum(ref[k], axis=0, keepdims=True) for ref in (two_ref, one_ref) for k in range(3)]
    inner = jnp.sum(inner_ref[...], axis=0, keepdims=True)
    rows += [inner[:, c * D : (c + 1) * D] for c in range(CHUNKS)]
    return jnp.concatenate(rows + [jnp.zeros((SUMS - len(rows), D), F32)], axis=0).T


def store_columns(layout, side, value, refs, start):
    columns = slice(start, start + value.shape[1])
    store_split(layout, side, value, [ref.at[:, columns] for ref in refs])


def backward_kernel(half, layout, limits_ref, side_ref, qkv_ref, grad_ref, lse_ref, tok_ref, *refs):
    sums_in, refs = (refs[:3], refs[3:]) if half == 0 else (refs[:1], refs[1:])
    out_ref, last_ref, split_refs, held_ref = refs[0], refs[1], refs[2:-1], refs[-1]
    seq = pl.program_id(0)
    by_blocks(limits_ref[seq], HALF, backward_block, half * HALF, qkv_ref, grad_ref, lse_ref, out_ref)
    rows = pl.ds(pl.multiple_of(seq * MAXLEN, MAXLEN), MAXLEN)
    held_ref[:, rows, :] = out_ref[...]

    @pl.when(seq == pl.num_programs(0) - 1)
    def _():
        count = tok_ref.shape[0]
        turned = tok_ref[...].T
        for part in range(3):
            store_columns(layout, side_ref[0], dot_nn(turned, held_ref[part]), split_refs, part * HALF_D)
        place = lax.broadcasted_iota(jnp.int32, (count, SUMS), 1)
        own = sum(
            dot_tn(held_ref[part], (place == column).astype(BF)) for part, column in ((0, 10), (2, 11))
        )
        rest = jnp.zeros((HALF_D, SUMS), F32)
        sums = jnp.concatenate([own, rest] if half == 0 else [rest, own], axis=0)
        if half == 0:
            last_ref[...] = sums + sums_block(*sums_in)
        else:
            store_columns(layout, side_ref[0], sums + sums_in[0][...], split_refs, 3 * HALF_D)
            last_ref[...] = jnp.zeros_like(last_ref)


def heads_backward(half, layout, side, qkv, grads, lse, limits, tokens, sums):
    count = qkv.shape[1]
    seqs = count // MAXLEN
    weights = row_split(layout, D, 3 * HALF_D + half * SUMS)
    last = jax.ShapeDtypeStruct((16, 128), BF) if half else jax.ShapeDtypeStruct((D, SUMS), F32)
    out = pl.pallas_call(
        partial(backward_kernel, half, layout),
        grid_spec=pltpu.PrefetchScalarGridSpec(
            num_scalar_prefetch=2,
            grid=(seqs,),
            in_specs=[
                pl.BlockSpec((3, MAXLEN, HALF_D), lambda s, *_: (0, s, half)),
                pl.BlockSpec((MAXLEN, HALF_D), lambda s, *_: (s, half)),
                pl.BlockSpec((1, PAIRS, 2, MAXLEN), lambda s, *_: (s, 0, 0, 0)),
                whole((count, D)),
            ]
            + [whole(array.shape) for array in sums],
            out_specs=[pl.BlockSpec((3, MAXLEN, HALF_D), lambda s, *_: (0, s, 0))]
            + [whole(array.shape) for array in [last] + weights],
            scratch_shapes=[pltpu.VMEM((3, count, HALF_D), BF)],
        ),
        out_shape=[jax.ShapeDtypeStruct((3, count, HALF_D), BF), last] + weights,
        compiler_params=params(),
        cost_estimate=cost(9000),
        name="heads_backward",
    )(limits, side, qkv, grads, lse, tokens, *sums)
    return out[0], out[1], out[2:]


def normal_parts(hidden):
    return 0.5 + 0.5 * lax.erf(hidden * HALF_ROOT), jnp.exp2(hidden * hidden * (-0.5 * LOG2E))


def row_mean(matrix):
    return jnp.mean(matrix, axis=1, keepdims=True)


def norm_rows(hidden):
    center = hidden - row_mean(hidden)
    scale = lax.rsqrt(row_mean(center * center) + EPSILON)
    return center * scale, scale


def norm_back(upstream, unit, scale, gain):
    inner = upstream * gain
    return scale * (inner - row_mean(inner) - unit * row_mean(inner * unit))


def fold_rows(matrix):
    rows, columns = matrix.shape
    return jnp.sum(matrix.reshape(rows // 8, 8, columns), axis=0)


BIAS_ROWS = ("b_query", "zero", "b_value", "b_output", "gain_attn", "shift_attn", "b_outer", "gain_ffn", "shift_ffn", "b_inner")


def load_weights(weights_ref, held_ref, sems):
    def block(c):
        columns = slice(c * D, (c + 1) * D)
        return pltpu.make_async_copy(weights_ref.at[:, columns], held_ref.at[:, columns], sems.at[c])

    return [block(c) for c in range(2 * CHUNKS + 1)]


def ffn_forward_step(wait, tok_ref, att_ref, cot_ref, vec_ref, out_ref, nl_ref, slope_ref, bg_ref, gs_ref,
                     unit_ref, scale_ref, sums_ref, held_ref, act_ref, allbg_ref):
    vec = lambda name, c=0: vec_ref[BIAS_ROWS.index(name) + c : BIAS_ROWS.index(name) + c + 1, :]
    block = lambda c: slice(c * D, (c + 1) * D)
    count = tok_ref.shape[0]
    rows = pl.ds(pl.multiple_of(pl.program_id(0) * count, count), count)
    wait(2 * CHUNKS)
    first = tok_ref[...].astype(F32) + dot_nn(att_ref[...], held_ref[:, block(2 * CHUNKS)]) + vec("b_output")
    unit_one, scale_one = norm_rows(first)
    unit_ref[...] = unit_one
    scale_ref[...] = jnp.broadcast_to(scale_one, scale_ref.shape)
    normed = unit_one * vec("gain_attn") + vec("shift_attn")
    nl = normed.astype(BF)
    nl_ref[...] = nl
    second = normed + vec("b_outer")
    for c in range(CHUNKS):
        wait(c)
        hidden = dot_nn(nl, held_ref[:, block(c)]) + vec("b_inner", c)
        phi, power = normal_parts(hidden)
        active = (hidden * phi).astype(BF)
        slope_ref[:, block(c)] = (phi + hidden * power * DENSITY).astype(slope_ref.dtype)
        act_ref[rows, block(c)] = active
        wait(CHUNKS + c)
        second = second + dot_nn(active, held_ref[:, block(CHUNKS + c)])
    unit_two, scale_two = norm_rows(second)
    out_ref[...] = (unit_two * vec("gain_ffn") + vec("shift_ffn")).astype(BF)
    cot = cot_ref[...].astype(F32)
    sums_ref[0] += fold_rows(cot * unit_two)
    sums_ref[1] += fold_rows(cot)
    grad_second = norm_back(cot, unit_two, scale_two, vec("gain_ffn"))
    gs_ref[...] = grad_second
    bg = grad_second.astype(BF)
    bg_ref[...] = bg
    allbg_ref[rows, :] = bg
    sums_ref[2] += fold_rows(bg.astype(F32))


def ffn_forward_kernel(blocks, layout, side_ref, tok_ref, att_ref, cot_ref, weights_ref, vec_ref, out_ref, nl_ref,
                       slope_ref, bg_ref, gs_ref, unit_ref, scale_ref, sums_ref, *rest):
    split_refs, (held_ref, act_ref, allbg_ref, sems) = rest[:-4], rest[-4:]
    step = pl.program_id(0)
    refs = (tok_ref, att_ref, cot_ref, vec_ref, out_ref, nl_ref, slope_ref, bg_ref, gs_ref, unit_ref, scale_ref,
            sums_ref, held_ref, act_ref, allbg_ref)

    @pl.when(step == 0)
    def _():
        copies = load_weights(weights_ref, held_ref, sems)
        copies[2 * CHUNKS].start()
        for c in range(CHUNKS):
            copies[c].start()
            copies[CHUNKS + c].start()
        sums_ref[...] = jnp.zeros_like(sums_ref)
        ffn_forward_step(lambda c: copies[c].wait(), *refs)

    @pl.when((step > 0) & (step < blocks))
    def _():
        ffn_forward_step(lambda c: None, *refs)

    @pl.when(step >= blocks)
    def _():
        columns = pl.ds(pl.multiple_of((step - blocks) * D, D), D)
        store_split(layout, side_ref[0], dot_tn(act_ref[:, columns], allbg_ref[...]), split_refs)


SLOPE = F32


def ffn_forward(layout, side, tokens, attended, cotangent, weights, vecs, rows=256):
    count = tokens.shape[0]
    blocks = count // rows
    at = lambda i: jnp.minimum(i, blocks - 1)
    narrow = pl.BlockSpec((rows, D), lambda i, _: (at(i), 0))
    shape = jax.ShapeDtypeStruct
    split = row_split(layout, D, FF)
    out = pl.pallas_call(
        partial(ffn_forward_kernel, blocks, layout),
        grid_spec=pltpu.PrefetchScalarGridSpec(
            num_scalar_prefetch=1,
            grid=(blocks + CHUNKS,),
            in_specs=[narrow, narrow, narrow, pl.BlockSpec(memory_space=pl.ANY), whole((16, D))],
            out_specs=[
                narrow, narrow, pl.BlockSpec((rows, FF), lambda i, _: (at(i), 0)), narrow, narrow, narrow,
                pl.BlockSpec((rows, 128), lambda i, _: (at(i), 0)), whole((3, 8, D)),
            ]
            + [pl.BlockSpec((part.shape[0], D), lambda i, _: (0, jnp.maximum(i - blocks, 0))) for part in split],
            scratch_shapes=[
                pltpu.VMEM((D, 2 * FF + D), BF), pltpu.VMEM((count, FF), BF), pltpu.VMEM((count, D), BF),
                pltpu.SemaphoreType.DMA((2 * CHUNKS + 1,)),
            ],
        ),
        out_shape=[
            shape((count, D), BF), shape((count, D), BF), shape((count, FF), SLOPE), shape((count, D), BF),
            shape((count, D), F32), shape((count, D), F32), shape((count, 128), F32), shape((3, 8, D), F32),
        ]
        + split,
        compiler_params=params(),
        cost_estimate=cost(16000),
        name="ffn_forward",
    )(side, tokens, attended, cotangent, weights, vecs)
    return out[:8], out[8:]


def ffn_backward_step(wait, bg_ref, slope_ref, gs_ref, unit_ref, scale_ref, vec_ref, gf_ref, ag_ref, sums_ref,
                      bisum_ref, held_ref, hg_ref, fl_ref):
    vec = lambda name: vec_ref[BIAS_ROWS.index(name) : BIAS_ROWS.index(name) + 1, :]
    block = lambda c: slice(c * D, (c + 1) * D)
    count = bg_ref.shape[0]
    rows = pl.ds(pl.multiple_of(pl.program_id(0) * count, count), count)
    bg = bg_ref[...]
    grad_normed = gs_ref[...]
    for c in range(CHUNKS):
        wait(CHUNKS + c)
        hg = (dot_nt(bg, held_ref[:, block(CHUNKS + c)]) * slope_ref[:, block(c)].astype(F32)).astype(BF)
        hg_ref[rows, block(c)] = hg
        bisum_ref[:, block(c)] += fold_rows(hg.astype(F32))
        wait(c)
        grad_normed = grad_normed + dot_nt(hg, held_ref[:, block(c)])
    unit_one = unit_ref[...]
    sums_ref[0] += fold_rows(grad_normed * unit_one)
    sums_ref[1] += fold_rows(grad_normed)
    grad_first = norm_back(grad_normed, unit_one, scale_ref[:, :1], vec("gain_attn"))
    gf_ref[...] = grad_first
    fl = grad_first.astype(BF)
    fl_ref[rows, :] = fl
    sums_ref[2] += fold_rows(fl.astype(F32))
    wait(2 * CHUNKS)
    ag_ref[...] = dot_nt(fl, held_ref[:, block(2 * CHUNKS)]).astype(BF)


def ffn_backward_kernel(blocks, layout, side_ref, bg_ref, slope_ref, gs_ref, unit_ref, scale_ref, nl_ref, att_ref,
                        weights_ref, vec_ref, gf_ref, ag_ref, sums_ref, bisum_ref, *rest):
    split_refs, (held_ref, hg_ref, fl_ref, turned_ref, left_ref, sems) = rest[:-6], rest[-6:]
    step = pl.program_id(0)
    refs = (bg_ref, slope_ref, gs_ref, unit_ref, scale_ref, vec_ref, gf_ref, ag_ref, sums_ref, bisum_ref, held_ref,
            hg_ref, fl_ref)

    def lefts():
        last = 2 * CHUNKS + 1
        return [
            pltpu.make_async_copy(ref, left_ref.at[k], sems.at[last + k]) for k, ref in enumerate((nl_ref, att_ref))
        ]

    @pl.when(step == 0)
    def _():
        copies = load_weights(weights_ref, held_ref, sems)
        for c in range(CHUNKS):
            copies[CHUNKS + c].start()
            copies[c].start()
        copies[2 * CHUNKS].start()
        sums_ref[...] = jnp.zeros_like(sums_ref)
        bisum_ref[...] = jnp.zeros_like(bisum_ref)
        ffn_backward_step(lambda c: copies[c].wait(), *refs)

    @pl.when((step > 0) & (step < blocks))
    def _():
        ffn_backward_step(lambda c: None, *refs)

    @pl.when(step == 1)
    def _():
        for copy in lefts():
            copy.start()

    @pl.when(step == blocks)
    def _():
        for copy in lefts():
            copy.wait()
        turned_ref[...] = left_ref[0].T

    @pl.when((step >= blocks) & (step < blocks + CHUNKS))
    def _():
        columns = pl.ds(pl.multiple_of((step - blocks) * D, D), D)
        store_split(layout, side_ref[0], dot_nn(turned_ref[...], hg_ref[:, columns]), split_refs)

    @pl.when(step == blocks + CHUNKS)
    def _():
        store_split(layout, side_ref[0], dot_tn(left_ref[1], fl_ref[...]), split_refs)


def ffn_backward(layout, side, branch, slope, grad_second, unit_one, scale_one, normed, attended, weights, vecs,
                 rows=256):
    count = branch.shape[0]
    blocks = count // rows
    at = lambda i: jnp.minimum(i, blocks - 1)
    narrow = pl.BlockSpec((rows, D), lambda i, _: (at(i), 0))
    shape = jax.ShapeDtypeStruct
    split = row_split(layout, D, FF + D)
    out = pl.pallas_call(
        partial(ffn_backward_kernel, blocks, layout),
        grid_spec=pltpu.PrefetchScalarGridSpec(
            num_scalar_prefetch=1,
            grid=(blocks + CHUNKS + 1,),
            in_specs=[
                narrow, pl.BlockSpec((rows, FF), lambda i, _: (at(i), 0)), narrow, narrow,
                pl.BlockSpec((rows, 128), lambda i, _: (at(i), 0)),
            ]
            + [pl.BlockSpec(memory_space=pl.ANY)] * 3
            + [whole((16, D))],
            out_specs=[narrow, narrow, whole((3, 8, D)), whole((8, FF))]
            + [pl.BlockSpec((part.shape[0], D), lambda i, _: (0, jnp.maximum(i - blocks, 0))) for part in split],
            scratch_shapes=[
                pltpu.VMEM((D, 2 * FF + D), BF), pltpu.VMEM((count, FF), BF), pltpu.VMEM((count, D), BF),
                pltpu.VMEM((D, count), BF), pltpu.VMEM((2, count, D), BF),
                pltpu.SemaphoreType.DMA((2 * CHUNKS + 3,)),
            ],
        ),
        out_shape=[
            shape((count, D), F32), shape((count, D), BF), shape((3, 8, D), F32), shape((8, FF), F32),
        ]
        + split,
        compiler_params=params(),
        cost_estimate=cost(17000),
        name="ffn_backward",
    )(side, branch, slope, grad_second, unit_one, scale_one, normed, attended, weights, vecs)
    return out[:4], out[4:]


def tokens_kernel(gf_ref, low_ref, high_ref, w_ref, out_ref):
    total = gf_ref[...]
    for part in range(3):
        grads = jnp.concatenate([low_ref[part], high_ref[part]], axis=1)
        total = total + dot_nt(grads, w_ref[:, part * D : (part + 1) * D])
    out_ref[...] = total.astype(BF)


def tokens_grad(grad_first, low_grads, high_grads, weights, rows=256):
    count = grad_first.shape[0]
    grads = pl.BlockSpec((3, rows, HALF_D), lambda i: (0, i, 0))
    return pl.pallas_call(
        tokens_kernel,
        grid=(count // rows,),
        in_specs=[pl.BlockSpec((rows, D), lambda i: (i, 0)), grads, grads, whole((D, 3 * D))],
        out_specs=pl.BlockSpec((rows, D), lambda i: (i, 0)),
        out_shape=jax.ShapeDtypeStruct((count, D), BF),
        compiler_params=params(),
        cost_estimate=cost(3600),
        name="tokens_grad",
    )(grad_first, low_grads, high_grads, weights)


AXES = ("hi", "lo", "far", "near")
CHIPS = AXES[:3]
MIDDLE = AXES[1:3]


def swap_near(value):
    return lax.ppermute(value, "near", [(0, 1), (1, 0)])


def exchange(value, axes):
    return lax.all_to_all(value, axes, 0, 0, tiled=True)


def spread(value, axes, count):
    return exchange(jnp.broadcast_to(value[None], (count,) + value.shape), axes)


def join_rows(layout, mine):
    other = swap_near(mine)
    high, middle, own = layout
    columns = mine.shape[-1]
    place = lax.broadcasted_iota(jnp.int32, (high, middle, 2, own, columns), 2)
    pick = lambda part: part.transpose(1, 0, 2, 3)[:, :, None]
    full = jnp.where(place == lax.axis_index("near"), pick(mine), pick(other))
    return lax.optimization_barrier(full).reshape(-1, columns)


def pair_sums(layout, side, outs, behind=None):
    give, keep = split_rows(layout, side, outs)
    sums = keep.astype(F32) + swap_near(give).astype(F32)
    if behind is not None:
        none = 0 * behind[:8, :128].astype(F32)
        sums = sums + jnp.pad(none, ((0, sums.shape[0] - 8), (0, sums.shape[1] - 128)))
    return sums.astype(BF)


def scatter(pair, axes):
    return lax.psum_scatter(pair, axes, scatter_dimension=0, tiled=True)


def to_plane(layout, pair):
    return exchange(pair.reshape(layout[1], -1, pair.shape[1]), MIDDLE)


def to_owner(layout, plane):
    return exchange(plane.reshape(layout[0], layout[2], -1), "hi")


def after(value, *others):
    return lax.optimization_barrier((value,) + others)[0]


def total(received, behind=None):
    sums = received[0].astype(F32)
    for part in range(1, received.shape[0]):
        sums = sums + received[part].astype(F32)
    if behind is not None:
        none = 0 * behind[:, : sums.shape[1]].astype(F32)
        sums = sums + jnp.pad(none, ((0, sums.shape[0] - none.shape[0]), (0, 0)))
    return sums


SUM_COLUMNS = ((10, 1), (11, 1), (5, 1), (3, 1), (4, 1), (6, CHUNKS), (2, 1), (0, 1), (1, 1))


def finish_parts(sums):
    half = lambda start, part: sums[:, start + part * HALF_D : start + (part + 1) * HALF_D]
    weights = [(half(0, part), half(3 * HALF_D, part)) for part in range(3)]
    turned = sums[:, 6 * HALF_D :].T
    return weights, [turned[start : start + count] for start, count in SUM_COLUMNS]


def finish_kernel(got_ref, *out_refs):
    weights, vectors = finish_parts(total(got_ref))
    for ref, (low, high) in zip(out_refs, weights):
        ref[:, :HALF_D] = low
        ref[:, HALF_D:] = high
    for ref, vector in zip(out_refs[3:], vectors):
        ref[...] = vector


def finish(received):
    own = received.shape[1]
    if own % 8:
        weights, vectors = finish_parts(total(received))
        weights = [jnp.concatenate(pair, axis=1) for pair in weights]
    else:
        out = pl.pallas_call(
            finish_kernel,
            out_shape=[jax.ShapeDtypeStruct((own, D), F32)] * 3
            + [jax.ShapeDtypeStruct((count, own), F32) for _, count in SUM_COLUMNS],
            compiler_params=params(),
            name="finish",
        )(received)
        weights, vectors = out[:3], out[3:]
    return weights, [vector.reshape(-1) for vector in vectors]


def body(sizes, tokens, cotangent, lengths, buckets, w_query, w_key, w_value, w_output, b_query, b_value,
         b_output, gain_attn, shift_attn, w_inner, b_inner, w_outer, b_outer, gain_ffn, shift_ffn):
    own = w_query.shape[0]
    ffn_weights = lax.all_gather(ffn_pack(w_inner, w_outer, w_output), AXES, axis=0, tiled=True)

    small = jnp.stack(
        [b_query, jnp.zeros_like(b_query), b_value, b_output, gain_attn, shift_attn, b_outer, gain_ffn, shift_ffn],
        axis=1,
    )
    small = jnp.concatenate([small, b_inner.reshape(CHUNKS, own).T], axis=1)
    small = jnp.pad(small, ((0, 0), (0, 128 - small.shape[1])))
    layout = (sizes["hi"], sizes["lo"] * sizes["far"], own)
    attn_pack = jnp.concatenate([w_query, w_key, w_value, small], axis=1)
    attn_mine = spread(spread(attn_pack, "hi", layout[0]), MIDDLE, layout[1])
    attn_weights = join_rows(layout, attn_mine)
    vecs = attn_weights[:, 3 * D : 3 * D + 16].astype(F32).T

    factor = jnp.where(buckets[0] == 0, 1, jnp.where(buckets[0] == 1, 2, 4)).astype(jnp.int32)
    limits = jnp.minimum(lengths, BLEN * factor).astype(jnp.int32)

    qkv, attended, lse = heads_forward(tokens, attn_weights, vecs, limits)
    near = lax.axis_index("near")
    side = near.astype(jnp.int32).reshape(1)
    (layer_out, normed_low, slope, branch, grad_second, unit_one, scale_one, sums_two), outer_grad = ffn_forward(
        layout, side, tokens, attended, cotangent, ffn_weights, vecs
    )
    outer_pair = pair_sums(layout, near, outer_grad)
    outer_got = to_plane(layout, outer_pair)
    (grad_first, attended_grad, sums_one, sums_inner), inner_grad = ffn_backward(
        layout, side, after(branch, outer_pair), slope, grad_second, unit_one, scale_one, normed_low, attended,
        ffn_weights, vecs
    )
    outer_got = after(outer_got, inner_grad[0])
    outer_plane = total(outer_got).astype(BF)
    inner_pair = pair_sums(layout, near, [after(part, outer_got) for part in inner_grad], outer_plane)
    inner_plane = scatter(inner_pair, MIDDLE)
    outer_got = to_owner(layout, outer_plane)
    attended_grad = after(attended_grad, inner_pair)
    low_grads, sums, low_grad = heads_backward(
        0, layout, side, qkv, attended_grad, lse, limits, tokens, (sums_two, sums_one, sums_inner)
    )
    outer_got = after(outer_got, low_grad[0])
    low_pair = pair_sums(layout, near, [after(part, outer_got) for part in low_grad])
    low_got = to_plane(layout, low_pair)
    high_grads, mark, high_grad = heads_backward(
        1, layout, side, qkv, after(attended_grad, low_pair), lse, limits, tokens, (sums,)
    )
    low_got = after(low_got, high_grad[0])
    inner_own = scatter(inner_plane.at[:16, :128].add(mark), "hi").astype(F32)
    high_pair = pair_sums(layout, near, [after(part, low_got) for part in high_grad])
    high_got = to_plane(layout, high_pair)
    grad_tokens = tokens_grad(after(grad_first, high_pair), low_grads, high_grads, attn_weights)
    high_got = after(high_got, grad_tokens)
    attn_plane = jnp.concatenate([total(low_got, inner_own).astype(BF), total(high_got).astype(BF)], axis=1)
    w_grads, vectors = finish(to_owner(layout, attn_plane))
    outer_own = total(outer_got)
    devices = D // own
    return (
        layer_out,
        grad_tokens,
        *w_grads,
        inner_own[:, FF:],
        *vectors[:5],
        inner_own[:, :FF].reshape(own, CHUNKS, devices, own).transpose(0, 2, 1, 3).reshape(own, FF),
        vectors[5],
        outer_own.reshape(own, CHUNKS, D).transpose(1, 0, 2).reshape(CHUNKS * own, D),
        *vectors[6:],
    )


def solution(mesh):
    wide, narrow = mesh.shape["wide"], mesh.shape["narrow"]
    sizes = {"hi": wide // 2, "lo": 2, "far": narrow // 2, "near": 2}
    split = jax.sharding.Mesh(mesh.devices.reshape([sizes[axis] for axis in AXES]), AXES)
    rows, vector = P(AXES, None), P(AXES)
    return jax.shard_map(
        partial(body, sizes),
        mesh=split,
        in_specs=(rows, rows, vector, vector) + (rows,) * 4 + (vector,) * 5
        + (rows, vector, rows, vector, vector, vector),
        out_specs=(rows,) * 6 + (vector,) * 5 + (rows, vector, rows, vector, vector, vector),
        check_vma=False,
    )
```

```python
from functools import partial

import jax
import jax.numpy as jnp
from jax import lax
from jax.experimental import pallas as pl
from jax.experimental.pallas import tpu as pltpu
from jax.sharding import PartitionSpec as P

D = 768
H = 12
HD = 64
FF = 3072
BLEN = 128
MAXLEN = 512
SEQ_DEV = 2
PAIR = 2 * HD
PAIRS = H // 2
CHUNKS = FF // D

EPSILON = 1e-12
DENSITY = 0.3989422804014327
HALF_ROOT = 0.7071067811865476
LOG2E = 1.4426950408889634
SCORE_SCALE = LOG2E * HD ** (-0.5)
VMEM = 60 * 1024 * 1024
BF = jnp.bfloat16
F32 = jnp.float32


def cost(megaflops):
    return pl.CostEstimate(flops=int(megaflops * 1e6 * COST_SCALE), bytes_accessed=1, transcendentals=0)


COST_SCALE = 1.0


def params(**kw):
    return pltpu.CompilerParams(vmem_limit_bytes=VMEM, **kw)


def dot_nn(a, b):
    return lax.dot_general(a, b, (((1,), (0,)), ((), ())), preferred_element_type=F32)


def dot_nt(a, b):
    return lax.dot_general(a, b, (((1,), (1,)), ((), ())), preferred_element_type=F32)


def dot_tn(a, b):
    return lax.dot_general(a, b, (((0,), (0,)), ((), ())), preferred_element_type=F32)


def whole(shape):
    return pl.BlockSpec(shape, lambda *_: (0,) * len(shape), pipeline_mode=pl.Buffered(1))


def columns_of(block, width):
    return pl.BlockSpec((D, width), lambda *_: (0, block), pipeline_mode=pl.Buffered(1))


def row_split(layout, rows, columns):
    own = layout[-1]
    if own % 8:
        return [jax.ShapeDtypeStruct((rows, columns), BF)]
    return [jax.ShapeDtypeStruct((rows // 2, columns), BF)] * 2


def store_split(layout, side, value, refs):
    if len(refs) == 1:
        refs[0][...] = value.astype(BF)
        return
    high, middle, own = layout
    parts = value.reshape(high, middle, 2, own, value.shape[1])
    lower, upper = parts[:, :, 0], parts[:, :, 1]
    for ref, part in zip(refs, (jnp.where(side == 0, upper, lower), jnp.where(side == 0, lower, upper))):
        ref[...] = jnp.transpose(part, (1, 0, 2, 3)).reshape(value.shape[0] // 2, value.shape[1]).astype(BF)


def split_rows(layout, side, outs):
    if len(outs) == 2:
        return outs
    high, middle, own = layout
    parts = outs[0].reshape(high, middle, 2, own, -1)
    halves = []
    for place in (1 - side, side):
        part = lax.dynamic_index_in_dim(parts, place, 2, keepdims=False)
        halves.append(part.transpose(1, 0, 2, 3).reshape(high * middle * own, -1))
    return halves


def pack_kernel(inner_ref, outer_ref, output_ref, pack_ref):
    own = inner_ref.shape[0]
    inner, outer = inner_ref[...].astype(F32), outer_ref[...].astype(F32)
    for c in range(CHUNKS):
        starts = range(own * c, FF, CHUNKS * own)
        block = jnp.concatenate([inner[:, start : start + own] for start in starts], axis=1)
        pack_ref[:, c * D : (c + 1) * D] = block.astype(BF)
        pack_ref[:, FF + c * D : FF + (c + 1) * D] = outer[c * own : (c + 1) * own].astype(BF)
    pack_ref[:, 2 * FF :] = output_ref[...]


def ffn_pack(w_inner, w_outer, w_output):
    own = w_inner.shape[0]
    if own % 8:
        turned = w_inner.reshape(own, -1, CHUNKS, own).transpose(0, 2, 1, 3).reshape(own, FF)
        blocks = w_outer.reshape(CHUNKS, own, D)
        return jnp.concatenate([turned] + [blocks[c] for c in range(CHUNKS)] + [w_output], axis=1)
    return pl.pallas_call(
        pack_kernel,
        out_shape=jax.ShapeDtypeStruct((own, 2 * FF + D), BF),
        compiler_params=params(),
        name="ffn_pack",
    )(w_inner, w_outer, w_output)


SUMS = 128
HALF = PAIRS // 2
HALF_D = HALF * PAIR


def lane_half(shape):
    return lax.broadcasted_iota(jnp.int32, shape, 1) < HD


def pick_half(matrix, low, head):
    zero = jnp.zeros_like(matrix)
    return jnp.where(low, matrix, zero) if head == 0 else jnp.where(low, zero, matrix)


def mask_last(scores, limit, fill):
    edge = scores.shape[0] - BLEN
    live = lax.broadcasted_iota(jnp.int32, (BLEN, 1), 0) + edge < limit
    last = jnp.where(live, scores[edge:], fill)
    return jnp.concatenate([scores[:edge], last], axis=0) if edge else last


def pair_columns(pair):
    return pl.ds(pl.multiple_of(pair * PAIR, PAIR), PAIR)


def forward_block(keys, limit, pair, qkv_ref, out_ref, lse_ref):
    columns = pair_columns(pair)
    queries = qkv_ref[0, :, columns]
    key_part = qkv_ref[1, :keys, columns]
    value_t = qkv_ref[2, :keys, columns].T
    low = lane_half((keys, PAIR))
    outs = []
    for head in range(2):
        scores = mask_last(dot_nt(pick_half(key_part, low, head), queries), limit, -1e30)
        top = jnp.max(scores, axis=0, keepdims=True) * SCORE_SCALE
        powers = jnp.exp2(scores * SCORE_SCALE - top)
        total = jnp.sum(powers, axis=0, keepdims=True)
        mixed = dot_nn(value_t[head * HD : (head + 1) * HD], powers.astype(BF))
        outs.append(mixed / total)
        lse_ref[0, pair, head : head + 1, :] = top + jnp.log2(total)
    out_ref[:, columns] = jnp.concatenate(outs, axis=0).T.astype(BF)


def backward_block(keys, limit, pair, first_pair, qkv_ref, grad_ref, lse_ref, out_ref):
    columns = here = pair_columns(pair)
    queries = qkv_ref[0, :, columns]
    key_part = qkv_ref[1, :keys, columns]
    value_part = qkv_ref[2, :keys, columns]
    grads = grad_ref[:, columns]
    key_t = key_part.T
    low = lane_half((keys, PAIR))
    scaling = HD ** (-0.5)
    query_grads, key_grads, value_grads = [], [], []
    for head in range(2):
        scores = dot_nt(pick_half(key_part, low, head), queries)
        logits = scores * SCORE_SCALE - lse_ref[0, first_pair + pair, head : head + 1, :]
        weights = jnp.exp2(mask_last(logits, limit, -1e30))
        value_grads.append(dot_nn(weights.astype(BF), grads))
        weight_grad = dot_nt(pick_half(value_part, low, head), grads)
        delta = jnp.sum(weight_grad * weights, axis=0, keepdims=True)
        score_grad = (weights * (weight_grad - delta)).astype(BF)
        key_grads.append(dot_nn(score_grad, queries))
        query_grads.append(dot_nn(key_t[head * HD : (head + 1) * HD], score_grad))
    out_ref[0, :, here] = (jnp.concatenate(query_grads, axis=0) * scaling).T.astype(BF)
    out_ref[1, :keys, here] = (jnp.where(low, key_grads[0], key_grads[1]) * scaling).astype(BF)
    out_ref[2, :keys, here] = jnp.where(low, value_grads[0], value_grads[1]).astype(BF)
    if keys < MAXLEN:
        out_ref[1, keys:, here] = jnp.zeros((MAXLEN - keys, PAIR), BF)
        out_ref[2, keys:, here] = jnp.zeros((MAXLEN - keys, PAIR), BF)


def by_blocks(limit, pairs, block, *refs):
    for blocks in range(1, MAXLEN // BLEN + 1):
        low_edge, high_edge = (blocks - 1) * BLEN, blocks * BLEN

        @pl.when((limit > low_edge) & (limit <= high_edge))
        def _():
            def one_pair(pair, carry):
                block(high_edge, limit, pair, *refs)
                return carry

            lax.fori_loop(0, pairs, one_pair, 0, unroll=2 if pairs % 2 == 0 else pairs)


def forward_kernel(limits_ref, x_ref, w_ref, bias_ref, qkv_ref, out_ref, lse_ref):
    x = x_ref[...]
    for part in range(3):
        rows = dot_nn(x, w_ref[:, part * D : (part + 1) * D])
        qkv_ref[part] = (rows + bias_ref[part : part + 1, :]).astype(BF)
    by_blocks(limits_ref[pl.program_id(0)], PAIRS, forward_block, qkv_ref, out_ref, lse_ref)


def heads_forward(tokens, weights, biases, limits):
    count = tokens.shape[0]
    seqs = count // MAXLEN
    return pl.pallas_call(
        forward_kernel,
        grid_spec=pltpu.PrefetchScalarGridSpec(
            num_scalar_prefetch=1,
            grid=(seqs,),
            in_specs=[pl.BlockSpec((MAXLEN, D), lambda s, _: (s, 0)), whole((D, 3 * D)), whole((16, D))],
            out_specs=[
                pl.BlockSpec((3, MAXLEN, D), lambda s, _: (0, s, 0)),
                pl.BlockSpec((MAXLEN, D), lambda s, _: (s, 0)),
                pl.BlockSpec((1, PAIRS, 2, MAXLEN), lambda s, _: (s, 0, 0, 0)),
            ],
        ),
        out_shape=[
            jax.ShapeDtypeStruct((3, count, D), BF),
            jax.ShapeDtypeStruct((count, D), BF),
            jax.ShapeDtypeStruct((seqs, PAIRS, 2, MAXLEN), F32),
        ],
        compiler_params=params(),
        cost_estimate=cost(6000),
        name="heads_forward",
    )(limits, tokens, weights, biases)


def sums_block(two_ref, one_ref, inner_ref):
    rows = [jnp.sum(ref[k], axis=0, keepdims=True) for ref in (two_ref, one_ref) for k in range(3)]
    inner = jnp.sum(inner_ref[...], axis=0, keepdims=True)
    rows += [inner[:, c * D : (c + 1) * D] for c in range(CHUNKS)]
    return jnp.concatenate(rows + [jnp.zeros((SUMS - len(rows), D), F32)], axis=0).T


def store_columns(layout, side, value, refs, start):
    columns = slice(start, start + value.shape[1])
    store_split(layout, side, value, [ref.at[:, columns] for ref in refs])


def backward_kernel(half, layout, limits_ref, side_ref, qkv_ref, grad_ref, lse_ref, tok_ref, *refs):
    sums_in, refs = (refs[:3], refs[3:]) if half == 0 else (refs[:1], refs[1:])
    out_ref, last_ref, split_refs, (held_ref, rows_ref, sem) = refs[0], refs[1], refs[2:-3], refs[-3:]
    rows_copy = pltpu.make_async_copy(tok_ref, rows_ref, sem)
    seq = pl.program_id(0)

    @pl.when(seq == 0)
    def _():
        rows_copy.start()

    by_blocks(limits_ref[seq], HALF, backward_block, half * HALF, qkv_ref, grad_ref, lse_ref, out_ref)
    rows = pl.ds(pl.multiple_of(seq * MAXLEN, MAXLEN), MAXLEN)
    held_ref[:, rows, :] = out_ref[...]

    @pl.when(seq == pl.num_programs(0) - 1)
    def _():
        rows_copy.wait()
        turned = rows_ref[...].T
        for part in range(3):
            store_columns(layout, side_ref[0], dot_nn(turned, held_ref[part]), split_refs, part * HALF_D)
        own = [jnp.sum(fold_rows(held_ref[part].astype(F32)), axis=0, keepdims=True) for part in (0, 2)]
        blank = lambda count: jnp.zeros((count, HALF_D), F32)
        own = jnp.concatenate([blank(10)] + own + [blank(SUMS - 12)], axis=0).T
        rest = jnp.zeros((HALF_D, SUMS), F32)
        sums = jnp.concatenate([own, rest] if half == 0 else [rest, own], axis=0)
        if half == 0:
            last_ref[...] = sums + sums_block(*sums_in)
        else:
            store_columns(layout, side_ref[0], sums + sums_in[0][...], split_refs, 3 * HALF_D)
            last_ref[...] = jnp.zeros_like(last_ref)


def heads_backward(half, layout, side, qkv, grads, lse, limits, tokens, sums):
    count = qkv.shape[1]
    seqs = count // MAXLEN
    weights = row_split(layout, D, 3 * HALF_D + half * SUMS)
    last = jax.ShapeDtypeStruct((16, 128), BF) if half else jax.ShapeDtypeStruct((D, SUMS), F32)
    out = pl.pallas_call(
        partial(backward_kernel, half, layout),
        grid_spec=pltpu.PrefetchScalarGridSpec(
            num_scalar_prefetch=2,
            grid=(seqs,),
            in_specs=[
                pl.BlockSpec((3, MAXLEN, HALF_D), lambda s, *_: (0, s, half)),
                pl.BlockSpec((MAXLEN, HALF_D), lambda s, *_: (s, half)),
                pl.BlockSpec((1, PAIRS, 2, MAXLEN), lambda s, *_: (s, 0, 0, 0)),
                pl.BlockSpec(memory_space=pl.ANY),
            ]
            + [whole(array.shape) for array in sums],
            out_specs=[pl.BlockSpec((3, MAXLEN, HALF_D), lambda s, *_: (0, s, 0))]
            + [whole(array.shape) for array in [last] + weights],
            scratch_shapes=[
                pltpu.VMEM((3, count, HALF_D), BF), pltpu.VMEM((count, D), BF), pltpu.SemaphoreType.DMA,
            ],
        ),
        out_shape=[jax.ShapeDtypeStruct((3, count, HALF_D), BF), last] + weights,
        compiler_params=params(),
        cost_estimate=cost(9000),
        name="heads_backward",
    )(limits, side, qkv, grads, lse, tokens, *sums)
    return out[0], out[1], out[2:]


def normal_parts(hidden):
    return 0.5 + 0.5 * lax.erf(hidden * HALF_ROOT), jnp.exp2(hidden * hidden * (-0.5 * LOG2E))


def row_mean(matrix):
    return jnp.mean(matrix, axis=1, keepdims=True)


def norm_rows(hidden):
    center = hidden - row_mean(hidden)
    scale = lax.rsqrt(row_mean(center * center) + EPSILON)
    return center * scale, scale


def norm_back(upstream, unit, scale, gain):
    inner = upstream * gain
    return scale * (inner - row_mean(inner) - unit * row_mean(inner * unit))


def fold_rows(matrix):
    rows, columns = matrix.shape
    return jnp.sum(matrix.reshape(rows // 8, 8, columns), axis=0)


BIAS_ROWS = ("b_query", "zero", "b_value", "b_output", "gain_attn", "shift_attn", "b_outer", "gain_ffn", "shift_ffn", "b_inner")


def load_weights(weights_ref, held_ref, sems):
    def block(c):
        columns = slice(c * D, (c + 1) * D)
        return pltpu.make_async_copy(weights_ref.at[:, columns], held_ref.at[:, columns], sems.at[c])

    return [block(c) for c in range(2 * CHUNKS + 1)]


def ffn_forward_step(wait, tok_ref, att_ref, cot_ref, vec_ref, out_ref, nl_ref, slope_ref, bg_ref, gs_ref,
                     unit_ref, scale_ref, sums_ref, held_ref, act_ref, allbg_ref):
    vec = lambda name, c=0: vec_ref[BIAS_ROWS.index(name) + c : BIAS_ROWS.index(name) + c + 1, :]
    block = lambda c: slice(c * D, (c + 1) * D)
    count = tok_ref.shape[0]
    rows = pl.ds(pl.multiple_of(pl.program_id(0) * count, count), count)
    wait(2 * CHUNKS)
    first = tok_ref[...].astype(F32) + dot_nn(att_ref[...], held_ref[:, block(2 * CHUNKS)]) + vec("b_output")
    unit_one, scale_one = norm_rows(first)
    unit_ref[...] = unit_one
    scale_ref[...] = jnp.broadcast_to(scale_one, scale_ref.shape)
    normed = unit_one * vec("gain_attn") + vec("shift_attn")
    nl = normed.astype(BF)
    nl_ref[...] = nl
    second = normed + vec("b_outer")
    for c in range(CHUNKS):
        wait(c)
        hidden = dot_nn(nl, held_ref[:, block(c)]) + vec("b_inner", c)
        phi, power = normal_parts(hidden)
        active = (hidden * phi).astype(BF)
        slope_ref[:, block(c)] = (phi + hidden * power * DENSITY).astype(slope_ref.dtype)
        act_ref[rows, block(c)] = active
        wait(CHUNKS + c)
        second = second + dot_nn(active, held_ref[:, block(CHUNKS + c)])
    unit_two, scale_two = norm_rows(second)
    out_ref[...] = (unit_two * vec("gain_ffn") + vec("shift_ffn")).astype(BF)
    cot = cot_ref[...].astype(F32)
    sums_ref[0] += fold_rows(cot * unit_two)
    sums_ref[1] += fold_rows(cot)
    grad_second = norm_back(cot, unit_two, scale_two, vec("gain_ffn"))
    gs_ref[...] = grad_second
    bg = grad_second.astype(BF)
    bg_ref[...] = bg
    allbg_ref[rows, :] = bg
    sums_ref[2] += fold_rows(bg.astype(F32))


def ffn_forward_kernel(blocks, layout, side_ref, tok_ref, att_ref, cot_ref, weights_ref, vec_ref, out_ref, nl_ref,
                       slope_ref, bg_ref, gs_ref, unit_ref, scale_ref, sums_ref, *rest):
    split_refs, (held_ref, act_ref, allbg_ref, sems) = rest[:-4], rest[-4:]
    step = pl.program_id(0)
    refs = (tok_ref, att_ref, cot_ref, vec_ref, out_ref, nl_ref, slope_ref, bg_ref, gs_ref, unit_ref, scale_ref,
            sums_ref, held_ref, act_ref, allbg_ref)

    @pl.when(step == 0)
    def _():
        copies = load_weights(weights_ref, held_ref, sems)
        copies[2 * CHUNKS].start()
        for c in range(CHUNKS):
            copies[c].start()
            copies[CHUNKS + c].start()
        sums_ref[...] = jnp.zeros_like(sums_ref)
        ffn_forward_step(lambda c: copies[c].wait(), *refs)

    @pl.when((step > 0) & (step < blocks))
    def _():
        ffn_forward_step(lambda c: None, *refs)

    @pl.when(step >= blocks)
    def _():
        for k in range(2):
            columns = pl.ds(pl.multiple_of((step - blocks) * 2 * D + k * D, D), D)
            store_columns(layout, side_ref[0], dot_tn(act_ref[:, columns], allbg_ref[...]), split_refs, k * D)


SLOPE = F32


def ffn_forward(layout, side, tokens, attended, cotangent, weights, vecs, rows=256):
    count = tokens.shape[0]
    blocks = count // rows
    at = lambda i: jnp.minimum(i, blocks - 1)
    narrow = pl.BlockSpec((rows, D), lambda i, _: (at(i), 0))
    shape = jax.ShapeDtypeStruct
    split = row_split(layout, D, FF)
    out = pl.pallas_call(
        partial(ffn_forward_kernel, blocks, layout),
        grid_spec=pltpu.PrefetchScalarGridSpec(
            num_scalar_prefetch=1,
            grid=(blocks + CHUNKS // 2,),
            in_specs=[narrow, narrow, narrow, pl.BlockSpec(memory_space=pl.ANY), whole((16, D))],
            out_specs=[
                narrow, narrow, pl.BlockSpec((rows, FF), lambda i, _: (at(i), 0)), narrow, narrow, narrow,
                pl.BlockSpec((rows, 128), lambda i, _: (at(i), 0)), whole((3, 8, D)),
            ]
            + [pl.BlockSpec((part.shape[0], 2 * D), lambda i, _: (0, jnp.maximum(i - blocks, 0))) for part in split],
            scratch_shapes=[
                pltpu.VMEM((D, 2 * FF + D), BF), pltpu.VMEM((count, FF), BF), pltpu.VMEM((count, D), BF),
                pltpu.SemaphoreType.DMA((2 * CHUNKS + 1,)),
            ],
        ),
        out_shape=[
            shape((count, D), BF), shape((count, D), BF), shape((count, FF), SLOPE), shape((count, D), BF),
            shape((count, D), F32), shape((count, D), F32), shape((count, 128), F32), shape((3, 8, D), F32),
        ]
        + split,
        compiler_params=params(),
        cost_estimate=cost(16000),
        name="ffn_forward",
    )(side, tokens, attended, cotangent, weights, vecs)
    return out[:8], out[8:]


def ffn_backward_step(wait, bg_ref, slope_ref, gs_ref, unit_ref, scale_ref, vec_ref, gf_ref, ag_ref, sums_ref,
                      bisum_ref, held_ref, hg_ref, fl_ref):
    vec = lambda name: vec_ref[BIAS_ROWS.index(name) : BIAS_ROWS.index(name) + 1, :]
    block = lambda c: slice(c * D, (c + 1) * D)
    count = bg_ref.shape[0]
    rows = pl.ds(pl.multiple_of(pl.program_id(0) * count, count), count)
    bg = bg_ref[...]
    grad_normed = gs_ref[...]
    for c in range(CHUNKS):
        wait(CHUNKS + c)
        hg = (dot_nt(bg, held_ref[:, block(CHUNKS + c)]) * slope_ref[:, block(c)].astype(F32)).astype(BF)
        hg_ref[rows, block(c)] = hg
        bisum_ref[:, block(c)] += fold_rows(hg.astype(F32))
        wait(c)
        grad_normed = grad_normed + dot_nt(hg, held_ref[:, block(c)])
    unit_one = unit_ref[...]
    sums_ref[0] += fold_rows(grad_normed * unit_one)
    sums_ref[1] += fold_rows(grad_normed)
    grad_first = norm_back(grad_normed, unit_one, scale_ref[:, :1], vec("gain_attn"))
    gf_ref[...] = grad_first
    fl = grad_first.astype(BF)
    fl_ref[rows, :] = fl
    sums_ref[2] += fold_rows(fl.astype(F32))
    wait(2 * CHUNKS)
    ag_ref[...] = dot_nt(fl, held_ref[:, block(2 * CHUNKS)]).astype(BF)


def ffn_backward_kernel(blocks, layout, side_ref, bg_ref, slope_ref, gs_ref, unit_ref, scale_ref, nl_ref, att_ref,
                        weights_ref, vec_ref, gf_ref, ag_ref, sums_ref, bisum_ref, *rest):
    split_refs, (held_ref, hg_ref, fl_ref, turned_ref, left_ref, sems) = rest[:-6], rest[-6:]
    step = pl.program_id(0)
    refs = (bg_ref, slope_ref, gs_ref, unit_ref, scale_ref, vec_ref, gf_ref, ag_ref, sums_ref, bisum_ref, held_ref,
            hg_ref, fl_ref)

    def lefts():
        last = 2 * CHUNKS + 1
        return [
            pltpu.make_async_copy(ref, left_ref.at[k], sems.at[last + k]) for k, ref in enumerate((nl_ref, att_ref))
        ]

    @pl.when(step == 0)
    def _():
        copies = load_weights(weights_ref, held_ref, sems)
        for c in range(CHUNKS):
            copies[CHUNKS + c].start()
            copies[c].start()
        copies[2 * CHUNKS].start()
        sums_ref[...] = jnp.zeros_like(sums_ref)
        bisum_ref[...] = jnp.zeros_like(bisum_ref)
        ffn_backward_step(lambda c: copies[c].wait(), *refs)

    @pl.when((step > 0) & (step < blocks))
    def _():
        ffn_backward_step(lambda c: None, *refs)

    @pl.when(step == 1)
    def _():
        for copy in lefts():
            copy.start()

    @pl.when(step == blocks)
    def _():
        for copy in lefts():
            copy.wait()
        turned_ref[...] = left_ref[0].T

    @pl.when((step >= blocks) & (step < blocks + CHUNKS))
    def _():
        columns = pl.ds(pl.multiple_of((step - blocks) * D, D), D)
        store_split(layout, side_ref[0], dot_nn(turned_ref[...], hg_ref[:, columns]), split_refs)

    @pl.when(step == blocks + CHUNKS)
    def _():
        store_split(layout, side_ref[0], dot_tn(left_ref[1], fl_ref[...]), split_refs)


def ffn_backward(layout, side, branch, slope, grad_second, unit_one, scale_one, normed, attended, weights, vecs,
                 rows=256):
    count = branch.shape[0]
    blocks = count // rows
    at = lambda i: jnp.minimum(i, blocks - 1)
    narrow = pl.BlockSpec((rows, D), lambda i, _: (at(i), 0))
    shape = jax.ShapeDtypeStruct
    split = row_split(layout, D, FF + D)
    out = pl.pallas_call(
        partial(ffn_backward_kernel, blocks, layout),
        grid_spec=pltpu.PrefetchScalarGridSpec(
            num_scalar_prefetch=1,
            grid=(blocks + CHUNKS + 1,),
            in_specs=[
                narrow, pl.BlockSpec((rows, FF), lambda i, _: (at(i), 0)), narrow, narrow,
                pl.BlockSpec((rows, 128), lambda i, _: (at(i), 0)),
            ]
            + [pl.BlockSpec(memory_space=pl.ANY)] * 3
            + [whole((16, D))],
            out_specs=[narrow, narrow, whole((3, 8, D)), whole((8, FF))]
            + [pl.BlockSpec((part.shape[0], D), lambda i, _: (0, jnp.maximum(i - blocks, 0))) for part in split],
            scratch_shapes=[
                pltpu.VMEM((D, 2 * FF + D), BF), pltpu.VMEM((count, FF), BF), pltpu.VMEM((count, D), BF),
                pltpu.VMEM((D, count), BF), pltpu.VMEM((2, count, D), BF),
                pltpu.SemaphoreType.DMA((2 * CHUNKS + 3,)),
            ],
        ),
        out_shape=[
            shape((count, D), F32), shape((count, D), BF), shape((3, 8, D), F32), shape((8, FF), F32),
        ]
        + split,
        compiler_params=params(),
        cost_estimate=cost(17000),
        name="ffn_backward",
    )(side, branch, slope, grad_second, unit_one, scale_one, normed, attended, weights, vecs)
    return out[:4], out[4:]


def tokens_kernel(gf_ref, low_ref, high_ref, w_ref, out_ref):
    total = gf_ref[...]
    for part in range(3):
        grads = jnp.concatenate([low_ref[part], high_ref[part]], axis=1)
        total = total + dot_nt(grads, w_ref[:, part * D : (part + 1) * D])
    out_ref[...] = total.astype(BF)


def tokens_grad(grad_first, low_grads, high_grads, weights, rows=256):
    count = grad_first.shape[0]
    grads = pl.BlockSpec((3, rows, HALF_D), lambda i: (0, i, 0))
    return pl.pallas_call(
        tokens_kernel,
        grid=(count // rows,),
        in_specs=[pl.BlockSpec((rows, D), lambda i: (i, 0)), grads, grads, whole((D, 3 * D))],
        out_specs=pl.BlockSpec((rows, D), lambda i: (i, 0)),
        out_shape=jax.ShapeDtypeStruct((count, D), BF),
        compiler_params=params(),
        cost_estimate=cost(3600),
        name="tokens_grad",
    )(grad_first, low_grads, high_grads, weights)


AXES = ("hi", "lo", "far", "near")
CHIPS = AXES[:3]
MIDDLE = AXES[1:3]


def swap_near(value):
    return lax.ppermute(value, "near", [(0, 1), (1, 0)])


def exchange(value, axes):
    return lax.all_to_all(value, axes, 0, 0, tiled=True)


def spread(value, axes, count):
    return exchange(jnp.broadcast_to(value[None], (count,) + value.shape), axes)


def join_rows(layout, mine):
    other = swap_near(mine)
    high, middle, own = layout
    columns = mine.shape[-1]
    place = lax.broadcasted_iota(jnp.int32, (high, middle, 2, own, columns), 2)
    pick = lambda part: part.transpose(1, 0, 2, 3)[:, :, None]
    full = jnp.where(place == lax.axis_index("near"), pick(mine), pick(other))
    return lax.optimization_barrier(full).reshape(-1, columns)


def pair_sums(layout, side, outs, behind=None):
    give, keep = split_rows(layout, side, outs)
    sums = keep.astype(F32) + swap_near(give).astype(F32)
    if behind is not None:
        none = 0 * behind[:8, :128].astype(F32)
        sums = sums + jnp.pad(none, ((0, sums.shape[0] - 8), (0, sums.shape[1] - 128)))
    return sums.astype(BF)


def scatter(pair, axes):
    return lax.psum_scatter(pair, axes, scatter_dimension=0, tiled=True)


def to_plane(layout, pair):
    return exchange(pair.reshape(layout[1], -1, pair.shape[1]), MIDDLE)


def to_owner(layout, plane):
    return exchange(plane.reshape(layout[0], layout[2], -1), "hi")


def after(value, *others):
    return lax.optimization_barrier((value,) + others)[0]


def total(received, behind=None):
    sums = received[0].astype(F32)
    for part in range(1, received.shape[0]):
        sums = sums + received[part].astype(F32)
    if behind is not None:
        none = 0 * behind[:, : sums.shape[1]].astype(F32)
        sums = sums + jnp.pad(none, ((0, sums.shape[0] - none.shape[0]), (0, 0)))
    return sums


SUM_COLUMNS = ((10, 1), (11, 1), (5, 1), (3, 1), (4, 1), (6, CHUNKS), (2, 1), (0, 1), (1, 1))


def finish_parts(sums):
    half = lambda start, part: sums[:, start + part * HALF_D : start + (part + 1) * HALF_D]
    weights = [(half(0, part), half(3 * HALF_D, part)) for part in range(3)]
    turned = sums[:, 6 * HALF_D :].T
    return weights, [turned[start : start + count] for start, count in SUM_COLUMNS]


def finish_kernel(got_ref, *out_refs):
    weights, vectors = finish_parts(total(got_ref))
    for ref, (low, high) in zip(out_refs, weights):
        ref[:, :HALF_D] = low
        ref[:, HALF_D:] = high
    for ref, vector in zip(out_refs[3:], vectors):
        ref[...] = vector


def finish(received):
    own = received.shape[1]
    if own % 8:
        weights, vectors = finish_parts(total(received))
        weights = [jnp.concatenate(pair, axis=1) for pair in weights]
    else:
        out = pl.pallas_call(
            finish_kernel,
            out_shape=[jax.ShapeDtypeStruct((own, D), F32)] * 3
            + [jax.ShapeDtypeStruct((count, own), F32) for _, count in SUM_COLUMNS],
            compiler_params=params(),
            name="finish",
        )(received)
        weights, vectors = out[:3], out[3:]
    return weights, [vector.reshape(-1) for vector in vectors]


def body(sizes, tokens, cotangent, lengths, buckets, w_query, w_key, w_value, w_output, b_query, b_value,
         b_output, gain_attn, shift_attn, w_inner, b_inner, w_outer, b_outer, gain_ffn, shift_ffn):
    own = w_query.shape[0]
    ffn_weights = lax.all_gather(ffn_pack(w_inner, w_outer, w_output), AXES, axis=0, tiled=True)

    small = jnp.stack(
        [b_query, jnp.zeros_like(b_query), b_value, b_output, gain_attn, shift_attn, b_outer, gain_ffn, shift_ffn],
        axis=1,
    )
    small = jnp.concatenate([small, b_inner.reshape(CHUNKS, own).T], axis=1)
    small = jnp.pad(small, ((0, 0), (0, 128 - small.shape[1])))
    layout = (sizes["hi"], sizes["lo"] * sizes["far"], own)
    attn_pack = jnp.concatenate([w_query, w_key, w_value, small], axis=1)
    attn_mine = spread(spread(attn_pack, "hi", layout[0]), MIDDLE, layout[1])
    attn_weights = join_rows(layout, attn_mine)
    vecs = attn_weights[:, 3 * D : 3 * D + 16].astype(F32).T

    factor = jnp.where(buckets[0] == 0, 1, jnp.where(buckets[0] == 1, 2, 4)).astype(jnp.int32)
    limits = jnp.minimum(lengths, BLEN * factor).astype(jnp.int32)

    qkv, attended, lse = heads_forward(tokens, attn_weights, vecs, limits)
    near = lax.axis_index("near")
    side = near.astype(jnp.int32).reshape(1)
    (layer_out, normed_low, slope, branch, grad_second, unit_one, scale_one, sums_two), outer_grad = ffn_forward(
        layout, side, tokens, attended, cotangent, ffn_weights, vecs
    )
    outer_pair = pair_sums(layout, near, outer_grad)
    outer_got = to_plane(layout, outer_pair)
    (grad_first, attended_grad, sums_one, sums_inner), inner_grad = ffn_backward(
        layout, side, after(branch, outer_pair), slope, grad_second, unit_one, scale_one, normed_low, attended,
        ffn_weights, vecs
    )
    outer_got = after(outer_got, inner_grad[0])
    outer_plane = total(outer_got).astype(BF)
    inner_pair = pair_sums(layout, near, [after(part, outer_got) for part in inner_grad], outer_plane)
    inner_plane = scatter(inner_pair, MIDDLE)
    outer_got = to_owner(layout, outer_plane)
    attended_grad = after(attended_grad, inner_pair)
    low_grads, sums, low_grad = heads_backward(
        0, layout, side, qkv, attended_grad, lse, limits, tokens, (sums_two, sums_one, sums_inner)
    )
    outer_got = after(outer_got, low_grad[0])
    low_pair = pair_sums(layout, near, [after(part, outer_got) for part in low_grad])
    low_got = to_plane(layout, low_pair)
    high_grads, mark, high_grad = heads_backward(
        1, layout, side, qkv, after(attended_grad, low_pair), lse, limits, tokens, (sums,)
    )
    low_got = after(low_got, high_grad[0])
    inner_own = scatter(inner_plane.at[:16, :128].add(mark), "hi").astype(F32)
    high_pair = pair_sums(layout, near, [after(part, low_got) for part in high_grad])
    high_got = to_plane(layout, high_pair)
    grad_tokens = tokens_grad(after(grad_first, high_pair), low_grads, high_grads, attn_weights)
    high_got = after(high_got, grad_tokens)
    attn_plane = jnp.concatenate([total(low_got, inner_own).astype(BF), total(high_got).astype(BF)], axis=1)
    w_grads, vectors = finish(to_owner(layout, attn_plane))
    outer_own = total(outer_got)
    devices = D // own
    return (
        layer_out,
        grad_tokens,
        *w_grads,
        inner_own[:, FF:],
        *vectors[:5],
        inner_own[:, :FF].reshape(own, CHUNKS, devices, own).transpose(0, 2, 1, 3).reshape(own, FF),
        vectors[5],
        outer_own.reshape(own, CHUNKS, D).transpose(1, 0, 2).reshape(CHUNKS * own, D),
        *vectors[6:],
    )


def solution(mesh):
    wide, narrow = mesh.shape["wide"], mesh.shape["narrow"]
    sizes = {"hi": wide // 2, "lo": 2, "far": narrow // 2, "near": 2}
    split = jax.sharding.Mesh(mesh.devices.reshape([sizes[axis] for axis in AXES]), AXES)
    rows, vector = P(AXES, None), P(AXES)
    return jax.shard_map(
        partial(body, sizes),
        mesh=split,
        in_specs=(rows, rows, vector, vector) + (rows,) * 4 + (vector,) * 5
        + (rows, vector, rows, vector, vector, vector),
        out_specs=(rows,) * 6 + (vector,) * 5 + (rows, vector, rows, vector, vector, vector),
        check_vma=False,
    )
```

```python
from functools import partial

import jax
import jax.numpy as jnp
from jax import lax
from jax.experimental import pallas as pl
from jax.experimental.pallas import tpu as pltpu
from jax.sharding import PartitionSpec as P

D = 768
H = 12
HD = 64
FF = 3072
BLEN = 128
MAXLEN = 512
SEQ_DEV = 2
PAIR = 2 * HD
PAIRS = H // 2
CHUNKS = FF // D

EPSILON = 1e-12
DENSITY = 0.3989422804014327
HALF_ROOT = 0.7071067811865476
LOG2E = 1.4426950408889634
SCORE_SCALE = LOG2E * HD ** (-0.5)
VMEM = 60 * 1024 * 1024
BF = jnp.bfloat16
F32 = jnp.float32


def cost(megaflops):
    return pl.CostEstimate(flops=int(megaflops * 1e6 * COST_SCALE), bytes_accessed=1, transcendentals=0)


COST_SCALE = 1.0


def params(**kw):
    return pltpu.CompilerParams(vmem_limit_bytes=VMEM, **kw)


def dot_nn(a, b):
    return lax.dot_general(a, b, (((1,), (0,)), ((), ())), preferred_element_type=F32)


def dot_nt(a, b):
    return lax.dot_general(a, b, (((1,), (1,)), ((), ())), preferred_element_type=F32)


def dot_tn(a, b):
    return lax.dot_general(a, b, (((0,), (0,)), ((), ())), preferred_element_type=F32)


def whole(shape):
    return pl.BlockSpec(shape, lambda *_: (0,) * len(shape), pipeline_mode=pl.Buffered(1))


def columns_of(block, width):
    return pl.BlockSpec((D, width), lambda *_: (0, block), pipeline_mode=pl.Buffered(1))


def row_split(layout, rows, columns):
    own = layout[-1]
    if own % 8:
        return [jax.ShapeDtypeStruct((rows, columns), BF)]
    return [jax.ShapeDtypeStruct((rows // 2, columns), BF)] * 2


def store_split(layout, side, value, refs):
    if len(refs) == 1:
        refs[0][...] = value.astype(BF)
        return
    high, middle, own = layout
    parts = value.reshape(high, middle, 2, own, value.shape[1])
    lower, upper = parts[:, :, 0], parts[:, :, 1]
    for ref, part in zip(refs, (jnp.where(side == 0, upper, lower), jnp.where(side == 0, lower, upper))):
        ref[...] = jnp.transpose(part, (1, 0, 2, 3)).reshape(value.shape[0] // 2, value.shape[1]).astype(BF)


def split_rows(layout, side, outs):
    if len(outs) == 2:
        return outs
    high, middle, own = layout
    parts = outs[0].reshape(high, middle, 2, own, -1)
    halves = []
    for place in (1 - side, side):
        part = lax.dynamic_index_in_dim(parts, place, 2, keepdims=False)
        halves.append(part.transpose(1, 0, 2, 3).reshape(high * middle * own, -1))
    return halves


def pack_kernel(inner_ref, outer_ref, output_ref, pack_ref):
    own = inner_ref.shape[0]
    inner, outer = inner_ref[...].astype(F32), outer_ref[...].astype(F32)
    for c in range(CHUNKS):
        starts = range(own * c, FF, CHUNKS * own)
        block = jnp.concatenate([inner[:, start : start + own] for start in starts], axis=1)
        pack_ref[:, c * D : (c + 1) * D] = block.astype(BF)
        pack_ref[:, FF + c * D : FF + (c + 1) * D] = outer[c * own : (c + 1) * own].astype(BF)
    pack_ref[:, 2 * FF :] = output_ref[...]


def ffn_pack(w_inner, w_outer, w_output):
    own = w_inner.shape[0]
    if own % 8:
        turned = w_inner.reshape(own, -1, CHUNKS, own).transpose(0, 2, 1, 3).reshape(own, FF)
        blocks = w_outer.reshape(CHUNKS, own, D)
        return jnp.concatenate([turned] + [blocks[c] for c in range(CHUNKS)] + [w_output], axis=1)
    return pl.pallas_call(
        pack_kernel,
        out_shape=jax.ShapeDtypeStruct((own, 2 * FF + D), BF),
        compiler_params=params(),
        name="ffn_pack",
    )(w_inner, w_outer, w_output)


SUMS = 128
HALF = PAIRS // 2
HALF_D = HALF * PAIR


def lane_half(shape):
    return lax.broadcasted_iota(jnp.int32, shape, 1) < HD


def pick_half(matrix, low, head):
    zero = jnp.zeros_like(matrix)
    return jnp.where(low, matrix, zero) if head == 0 else jnp.where(low, zero, matrix)


def mask_last(scores, limit, fill):
    edge = scores.shape[0] - BLEN
    live = lax.broadcasted_iota(jnp.int32, (BLEN, 1), 0) + edge < limit
    last = jnp.where(live, scores[edge:], fill)
    return jnp.concatenate([scores[:edge], last], axis=0) if edge else last


def pair_columns(pair):
    return pl.ds(pl.multiple_of(pair * PAIR, PAIR), PAIR)


def forward_block(keys, limit, pair, qkv_ref, out_ref, lse_ref):
    columns = pair_columns(pair)
    queries = qkv_ref[0, :, columns]
    key_part = qkv_ref[1, :keys, columns]
    value_t = qkv_ref[2, :keys, columns].T
    low = lane_half((keys, PAIR))
    outs = []
    for head in range(2):
        scores = mask_last(dot_nt(pick_half(key_part, low, head), queries), limit, -1e30)
        top = jnp.max(scores, axis=0, keepdims=True) * SCORE_SCALE
        powers = jnp.exp2(scores * SCORE_SCALE - top)
        total = jnp.sum(powers, axis=0, keepdims=True)
        mixed = dot_nn(value_t[head * HD : (head + 1) * HD], powers.astype(BF))
        outs.append(mixed / total)
        lse_ref[0, pair, head : head + 1, :] = top + jnp.log2(total)
    out_ref[:, columns] = jnp.concatenate(outs, axis=0).T.astype(BF)


def backward_block(keys, limit, pair, first_pair, qkv_ref, grad_ref, lse_ref, out_ref):
    columns = here = pair_columns(pair)
    queries = qkv_ref[0, :, columns]
    key_part = qkv_ref[1, :keys, columns]
    value_part = qkv_ref[2, :keys, columns]
    grads = grad_ref[:, columns]
    key_t = key_part.T
    low = lane_half((keys, PAIR))
    scaling = HD ** (-0.5)
    query_grads, key_grads, value_grads = [], [], []
    for head in range(2):
        scores = dot_nt(pick_half(key_part, low, head), queries)
        logits = scores * SCORE_SCALE - lse_ref[0, first_pair + pair, head : head + 1, :]
        weights = jnp.exp2(mask_last(logits, limit, -1e30))
        value_grads.append(dot_nn(weights.astype(BF), grads))
        weight_grad = dot_nt(pick_half(value_part, low, head), grads)
        delta = jnp.sum(weight_grad * weights, axis=0, keepdims=True)
        score_grad = (weights * (weight_grad - delta)).astype(BF)
        key_grads.append(dot_nn(score_grad, queries))
        query_grads.append(dot_nn(key_t[head * HD : (head + 1) * HD], score_grad))
    out_ref[0, :, here] = (jnp.concatenate(query_grads, axis=0) * scaling).T.astype(BF)
    out_ref[1, :keys, here] = (jnp.where(low, key_grads[0], key_grads[1]) * scaling).astype(BF)
    out_ref[2, :keys, here] = jnp.where(low, value_grads[0], value_grads[1]).astype(BF)
    if keys < MAXLEN:
        out_ref[1, keys:, here] = jnp.zeros((MAXLEN - keys, PAIR), BF)
        out_ref[2, keys:, here] = jnp.zeros((MAXLEN - keys, PAIR), BF)


def by_blocks(limit, pairs, block, *refs):
    for blocks in range(1, MAXLEN // BLEN + 1):
        low_edge, high_edge = (blocks - 1) * BLEN, blocks * BLEN

        @pl.when((limit > low_edge) & (limit <= high_edge))
        def _():
            def one_pair(pair, carry):
                block(high_edge, limit, pair, *refs)
                return carry

            lax.fori_loop(0, pairs, one_pair, 0, unroll=2 if pairs % 2 == 0 else pairs)


def forward_kernel(limits_ref, x_ref, w_ref, bias_ref, qkv_ref, out_ref, lse_ref):
    x = x_ref[...]
    for part in range(3):
        rows = dot_nn(x, w_ref[:, part * D : (part + 1) * D])
        qkv_ref[part] = (rows + bias_ref[part : part + 1, :]).astype(BF)
    by_blocks(limits_ref[pl.program_id(0)], PAIRS, forward_block, qkv_ref, out_ref, lse_ref)


def heads_forward(tokens, weights, biases, limits):
    count = tokens.shape[0]
    seqs = count // MAXLEN
    return pl.pallas_call(
        forward_kernel,
        grid_spec=pltpu.PrefetchScalarGridSpec(
            num_scalar_prefetch=1,
            grid=(seqs,),
            in_specs=[pl.BlockSpec((MAXLEN, D), lambda s, _: (s, 0)), whole((D, 3 * D)), whole((16, D))],
            out_specs=[
                pl.BlockSpec((3, MAXLEN, D), lambda s, _: (0, s, 0)),
                pl.BlockSpec((MAXLEN, D), lambda s, _: (s, 0)),
                pl.BlockSpec((1, PAIRS, 2, MAXLEN), lambda s, _: (s, 0, 0, 0)),
            ],
        ),
        out_shape=[
            jax.ShapeDtypeStruct((3, count, D), BF),
            jax.ShapeDtypeStruct((count, D), BF),
            jax.ShapeDtypeStruct((seqs, PAIRS, 2, MAXLEN), F32),
        ],
        compiler_params=params(),
        cost_estimate=cost(6000),
        name="heads_forward",
    )(limits, tokens, weights, biases)


def sums_block(two_ref, one_ref, inner_ref):
    rows = [jnp.sum(ref[k], axis=0, keepdims=True) for ref in (two_ref, one_ref) for k in range(3)]
    inner = jnp.sum(inner_ref[...], axis=0, keepdims=True)
    rows += [inner[:, c * D : (c + 1) * D] for c in range(CHUNKS)]
    return jnp.concatenate(rows + [jnp.zeros((SUMS - len(rows), D), F32)], axis=0).T


def store_columns(layout, side, value, refs, start):
    columns = slice(start, start + value.shape[1])
    store_split(layout, side, value, [ref.at[:, columns] for ref in refs])


def backward_kernel(half, layout, limits_ref, side_ref, qkv_ref, grad_ref, lse_ref, tok_ref, *refs):
    sums_in, refs = (refs[:3], refs[3:]) if half == 0 else (refs[:1], refs[1:])
    out_ref, last_ref, split_refs, (held_ref, rows_ref, sem) = refs[0], refs[1], refs[2:-3], refs[-3:]
    rows_copy = pltpu.make_async_copy(tok_ref, rows_ref, sem)
    seq = pl.program_id(0)

    @pl.when(seq == 0)
    def _():
        rows_copy.start()

    by_blocks(limits_ref[seq], HALF, backward_block, half * HALF, qkv_ref, grad_ref, lse_ref, out_ref)
    rows = pl.ds(pl.multiple_of(seq * MAXLEN, MAXLEN), MAXLEN)
    held_ref[:, rows, :] = out_ref[...]

    @pl.when(seq == pl.num_programs(0) - 1)
    def _():
        rows_copy.wait()
        turned = rows_ref[...].T
        for part in range(3):
            store_columns(layout, side_ref[0], dot_nn(turned, held_ref[part]), split_refs, part * HALF_D)
        own = [jnp.sum(fold_rows(held_ref[part].astype(F32)), axis=0, keepdims=True) for part in (0, 2)]
        blank = lambda count: jnp.zeros((count, HALF_D), F32)
        own = jnp.concatenate([blank(10)] + own + [blank(SUMS - 12)], axis=0).T
        rest = jnp.zeros((HALF_D, SUMS), F32)
        sums = jnp.concatenate([own, rest] if half == 0 else [rest, own], axis=0)
        if half == 0:
            last_ref[...] = sums + sums_block(*sums_in)
        else:
            store_columns(layout, side_ref[0], sums + sums_in[0][...], split_refs, 3 * HALF_D)
            last_ref[...] = jnp.zeros_like(last_ref)


def heads_backward(half, layout, side, qkv, grads, lse, limits, tokens, sums):
    count = qkv.shape[1]
    seqs = count // MAXLEN
    weights = row_split(layout, D, 3 * HALF_D + half * SUMS)
    last = jax.ShapeDtypeStruct((16, 128), BF) if half else jax.ShapeDtypeStruct((D, SUMS), F32)
    out = pl.pallas_call(
        partial(backward_kernel, half, layout),
        grid_spec=pltpu.PrefetchScalarGridSpec(
            num_scalar_prefetch=2,
            grid=(seqs,),
            in_specs=[
                pl.BlockSpec((3, MAXLEN, HALF_D), lambda s, *_: (0, s, half)),
                pl.BlockSpec((MAXLEN, HALF_D), lambda s, *_: (s, half)),
                pl.BlockSpec((1, PAIRS, 2, MAXLEN), lambda s, *_: (s, 0, 0, 0)),
                pl.BlockSpec(memory_space=pl.ANY),
            ]
            + [whole(array.shape) for array in sums],
            out_specs=[pl.BlockSpec((3, MAXLEN, HALF_D), lambda s, *_: (0, s, 0))]
            + [whole(array.shape) for array in [last] + weights],
            scratch_shapes=[
                pltpu.VMEM((3, count, HALF_D), BF), pltpu.VMEM((count, D), BF), pltpu.SemaphoreType.DMA,
            ],
        ),
        out_shape=[jax.ShapeDtypeStruct((3, count, HALF_D), BF), last] + weights,
        compiler_params=params(),
        cost_estimate=cost(9000),
        name="heads_backward",
    )(limits, side, qkv, grads, lse, tokens, *sums)
    return out[0], out[1], out[2:]


def normal_parts(hidden):
    return 0.5 + 0.5 * lax.erf(hidden * HALF_ROOT), jnp.exp2(hidden * hidden * (-0.5 * LOG2E))


def row_mean(matrix):
    return jnp.mean(matrix, axis=1, keepdims=True)


def norm_rows(hidden):
    center = hidden - row_mean(hidden)
    scale = lax.rsqrt(row_mean(center * center) + EPSILON)
    return center * scale, scale


def norm_back(upstream, unit, scale, gain):
    inner = upstream * gain
    return scale * (inner - row_mean(inner) - unit * row_mean(inner * unit))


def fold_rows(matrix):
    rows, columns = matrix.shape
    return jnp.sum(matrix.reshape(rows // 8, 8, columns), axis=0)


BIAS_ROWS = ("b_query", "zero", "b_value", "b_output", "gain_attn", "shift_attn", "b_outer", "gain_ffn", "shift_ffn", "b_inner")


def load_weights(weights_ref, held_ref, sems):
    def block(c):
        columns = slice(c * D, (c + 1) * D)
        return pltpu.make_async_copy(weights_ref.at[:, columns], held_ref.at[:, columns], sems.at[c])

    return [block(c) for c in range(2 * CHUNKS + 1)]


def ffn_forward_step(wait, tok_ref, att_ref, cot_ref, vec_ref, out_ref, nl_ref, slope_ref, bg_ref, gs_ref,
                     unit_ref, scale_ref, sums_ref, held_ref, act_ref, allbg_ref):
    vec = lambda name, c=0: vec_ref[BIAS_ROWS.index(name) + c : BIAS_ROWS.index(name) + c + 1, :]
    block = lambda c: slice(c * D, (c + 1) * D)
    count = tok_ref.shape[0]
    rows = pl.ds(pl.multiple_of(pl.program_id(0) * count, count), count)
    wait(2 * CHUNKS)
    first = tok_ref[...].astype(F32) + dot_nn(att_ref[...], held_ref[:, block(2 * CHUNKS)]) + vec("b_output")
    unit_one, scale_one = norm_rows(first)
    unit_ref[...] = unit_one
    scale_ref[...] = jnp.broadcast_to(scale_one, scale_ref.shape)
    normed = unit_one * vec("gain_attn") + vec("shift_attn")
    nl = normed.astype(BF)
    nl_ref[...] = nl
    second = normed + vec("b_outer")
    for c in range(CHUNKS):
        wait(c)
        hidden = dot_nn(nl, held_ref[:, block(c)]) + vec("b_inner", c)
        phi, power = normal_parts(hidden)
        active = (hidden * phi).astype(BF)
        slope_ref[:, block(c)] = (phi + hidden * power * DENSITY).astype(slope_ref.dtype)
        act_ref[rows, block(c)] = active
        wait(CHUNKS + c)
        second = second + dot_nn(active, held_ref[:, block(CHUNKS + c)])
    unit_two, scale_two = norm_rows(second)
    out_ref[...] = (unit_two * vec("gain_ffn") + vec("shift_ffn")).astype(BF)
    cot = cot_ref[...].astype(F32)
    sums_ref[0] += fold_rows(cot * unit_two)
    sums_ref[1] += fold_rows(cot)
    grad_second = norm_back(cot, unit_two, scale_two, vec("gain_ffn"))
    gs_ref[...] = grad_second
    bg = grad_second.astype(BF)
    bg_ref[...] = bg
    allbg_ref[rows, :] = bg
    sums_ref[2] += fold_rows(bg.astype(F32))


def ffn_forward_kernel(blocks, layout, side_ref, tok_ref, att_ref, cot_ref, weights_ref, vec_ref, out_ref, nl_ref,
                       slope_ref, bg_ref, gs_ref, unit_ref, scale_ref, sums_ref, *rest):
    split_refs, (held_ref, act_ref, allbg_ref, sems) = rest[:-4], rest[-4:]
    step = pl.program_id(0)
    refs = (tok_ref, att_ref, cot_ref, vec_ref, out_ref, nl_ref, slope_ref, bg_ref, gs_ref, unit_ref, scale_ref,
            sums_ref, held_ref, act_ref, allbg_ref)

    @pl.when(step == 0)
    def _():
        copies = load_weights(weights_ref, held_ref, sems)
        copies[2 * CHUNKS].start()
        for c in range(CHUNKS):
            copies[c].start()
            copies[CHUNKS + c].start()
        sums_ref[...] = jnp.zeros_like(sums_ref)
        ffn_forward_step(lambda c: copies[c].wait(), *refs)

    @pl.when((step > 0) & (step < blocks))
    def _():
        ffn_forward_step(lambda c: None, *refs)

    @pl.when(step >= blocks)
    def _():
        for k in range(2):
            columns = pl.ds(pl.multiple_of((step - blocks) * 2 * D + k * D, D), D)
            store_columns(layout, side_ref[0], dot_tn(act_ref[:, columns], allbg_ref[...]), split_refs, k * D)


SLOPE = F32


def ffn_forward(layout, side, tokens, attended, cotangent, weights, vecs, rows=256):
    count = tokens.shape[0]
    blocks = count // rows
    at = lambda i: jnp.minimum(i, blocks - 1)
    narrow = pl.BlockSpec((rows, D), lambda i, _: (at(i), 0))
    shape = jax.ShapeDtypeStruct
    split = row_split(layout, D, FF)
    out = pl.pallas_call(
        partial(ffn_forward_kernel, blocks, layout),
        grid_spec=pltpu.PrefetchScalarGridSpec(
            num_scalar_prefetch=1,
            grid=(blocks + CHUNKS // 2,),
            in_specs=[narrow, narrow, narrow, pl.BlockSpec(memory_space=pl.ANY), whole((16, D))],
            out_specs=[
                narrow, narrow, pl.BlockSpec((rows, FF), lambda i, _: (at(i), 0)), narrow, narrow, narrow,
                pl.BlockSpec((rows, 128), lambda i, _: (at(i), 0)), whole((3, 8, D)),
            ]
            + [pl.BlockSpec((part.shape[0], 2 * D), lambda i, _: (0, jnp.maximum(i - blocks, 0))) for part in split],
            scratch_shapes=[
                pltpu.VMEM((D, 2 * FF + D), BF), pltpu.VMEM((count, FF), BF), pltpu.VMEM((count, D), BF),
                pltpu.SemaphoreType.DMA((2 * CHUNKS + 1,)),
            ],
        ),
        out_shape=[
            shape((count, D), BF), shape((count, D), BF), shape((count, FF), SLOPE), shape((count, D), BF),
            shape((count, D), F32), shape((count, D), F32), shape((count, 128), F32), shape((3, 8, D), F32),
        ]
        + split,
        compiler_params=params(),
        cost_estimate=cost(16000),
        name="ffn_forward",
    )(side, tokens, attended, cotangent, weights, vecs)
    return out[:8], out[8:]


def ffn_backward_step(wait, bg_ref, slope_ref, gs_ref, unit_ref, scale_ref, vec_ref, gf_ref, ag_ref, sums_ref,
                      bisum_ref, held_ref, hg_ref, fl_ref):
    vec = lambda name: vec_ref[BIAS_ROWS.index(name) : BIAS_ROWS.index(name) + 1, :]
    block = lambda c: slice(c * D, (c + 1) * D)
    count = bg_ref.shape[0]
    rows = pl.ds(pl.multiple_of(pl.program_id(0) * count, count), count)
    bg = bg_ref[...]
    grad_normed = gs_ref[...]
    for c in range(CHUNKS):
        wait(CHUNKS + c)
        hg = (dot_nt(bg, held_ref[:, block(CHUNKS + c)]) * slope_ref[:, block(c)].astype(F32)).astype(BF)
        hg_ref[rows, block(c)] = hg
        bisum_ref[:, block(c)] += fold_rows(hg.astype(F32))
        wait(c)
        grad_normed = grad_normed + dot_nt(hg, held_ref[:, block(c)])
    unit_one = unit_ref[...]
    sums_ref[0] += fold_rows(grad_normed * unit_one)
    sums_ref[1] += fold_rows(grad_normed)
    grad_first = norm_back(grad_normed, unit_one, scale_ref[:, :1], vec("gain_attn"))
    gf_ref[...] = grad_first
    fl = grad_first.astype(BF)
    fl_ref[rows, :] = fl
    sums_ref[2] += fold_rows(fl.astype(F32))
    wait(2 * CHUNKS)
    ag_ref[...] = dot_nt(fl, held_ref[:, block(2 * CHUNKS)]).astype(BF)


def ffn_backward_kernel(blocks, layout, side_ref, bg_ref, slope_ref, gs_ref, unit_ref, scale_ref, nl_ref, att_ref,
                        weights_ref, vec_ref, gf_ref, ag_ref, sums_ref, bisum_ref, *rest):
    split_refs, (held_ref, hg_ref, fl_ref, turned_ref, left_ref, sems) = rest[:-6], rest[-6:]
    step = pl.program_id(0)
    refs = (bg_ref, slope_ref, gs_ref, unit_ref, scale_ref, vec_ref, gf_ref, ag_ref, sums_ref, bisum_ref, held_ref,
            hg_ref, fl_ref)

    def lefts():
        last = 2 * CHUNKS + 1
        return [
            pltpu.make_async_copy(ref, left_ref.at[k], sems.at[last + k]) for k, ref in enumerate((nl_ref, att_ref))
        ]

    @pl.when(step == 0)
    def _():
        copies = load_weights(weights_ref, held_ref, sems)
        for c in range(CHUNKS):
            copies[CHUNKS + c].start()
            copies[c].start()
        copies[2 * CHUNKS].start()
        sums_ref[...] = jnp.zeros_like(sums_ref)
        bisum_ref[...] = jnp.zeros_like(bisum_ref)
        ffn_backward_step(lambda c: copies[c].wait(), *refs)

    @pl.when((step > 0) & (step < blocks))
    def _():
        ffn_backward_step(lambda c: None, *refs)

    @pl.when(step == 1)
    def _():
        for copy in lefts():
            copy.start()

    @pl.when(step == blocks)
    def _():
        for copy in lefts():
            copy.wait()
        turned_ref[...] = left_ref[0].T

    @pl.when((step >= blocks) & (step < blocks + CHUNKS))
    def _():
        columns = pl.ds(pl.multiple_of((step - blocks) * D, D), D)
        store_split(layout, side_ref[0], dot_nn(turned_ref[...], hg_ref[:, columns]), split_refs)

    @pl.when(step == blocks + CHUNKS)
    def _():
        store_split(layout, side_ref[0], dot_tn(left_ref[1], fl_ref[...]), split_refs)


def ffn_backward(layout, side, branch, slope, grad_second, unit_one, scale_one, normed, attended, weights, vecs,
                 rows=256):
    count = branch.shape[0]
    blocks = count // rows
    at = lambda i: jnp.minimum(i, blocks - 1)
    narrow = pl.BlockSpec((rows, D), lambda i, _: (at(i), 0))
    shape = jax.ShapeDtypeStruct
    split = row_split(layout, D, FF + D)
    out = pl.pallas_call(
        partial(ffn_backward_kernel, blocks, layout),
        grid_spec=pltpu.PrefetchScalarGridSpec(
            num_scalar_prefetch=1,
            grid=(blocks + CHUNKS + 1,),
            in_specs=[
                narrow, pl.BlockSpec((rows, FF), lambda i, _: (at(i), 0)), narrow, narrow,
                pl.BlockSpec((rows, 128), lambda i, _: (at(i), 0)),
            ]
            + [pl.BlockSpec(memory_space=pl.ANY)] * 3
            + [whole((16, D))],
            out_specs=[narrow, narrow, whole((3, 8, D)), whole((8, FF))]
            + [pl.BlockSpec((part.shape[0], D), lambda i, _: (0, jnp.maximum(i - blocks, 0))) for part in split],
            scratch_shapes=[
                pltpu.VMEM((D, 2 * FF + D), BF), pltpu.VMEM((count, FF), BF), pltpu.VMEM((count, D), BF),
                pltpu.VMEM((D, count), BF), pltpu.VMEM((2, count, D), BF),
                pltpu.SemaphoreType.DMA((2 * CHUNKS + 3,)),
            ],
        ),
        out_shape=[
            shape((count, D), F32), shape((count, D), BF), shape((3, 8, D), F32), shape((8, FF), F32),
        ]
        + split,
        compiler_params=params(),
        cost_estimate=cost(17000),
        name="ffn_backward",
    )(side, branch, slope, grad_second, unit_one, scale_one, normed, attended, weights, vecs)
    return out[:4], out[4:]


def tokens_kernel(gf_ref, low_ref, high_ref, w_ref, out_ref):
    total = gf_ref[...]
    for part in range(3):
        grads = jnp.concatenate([low_ref[part], high_ref[part]], axis=1)
        total = total + dot_nt(grads, w_ref[:, part * D : (part + 1) * D])
    out_ref[...] = total.astype(BF)


def tokens_grad(grad_first, low_grads, high_grads, weights, rows=256):
    count = grad_first.shape[0]
    grads = pl.BlockSpec((3, rows, HALF_D), lambda i: (0, i, 0))
    return pl.pallas_call(
        tokens_kernel,
        grid=(count // rows,),
        in_specs=[pl.BlockSpec((rows, D), lambda i: (i, 0)), grads, grads, whole((D, 3 * D))],
        out_specs=pl.BlockSpec((rows, D), lambda i: (i, 0)),
        out_shape=jax.ShapeDtypeStruct((count, D), BF),
        compiler_params=params(),
        cost_estimate=cost(3600),
        name="tokens_grad",
    )(grad_first, low_grads, high_grads, weights)


AXES = ("hi", "lo", "far", "near")
CHIPS = AXES[:3]
MIDDLE = AXES[1:3]


def swap_near(value):
    return lax.ppermute(value, "near", [(0, 1), (1, 0)])


def exchange(value, axes):
    return lax.all_to_all(value, axes, 0, 0, tiled=True)


def spread(value, axes, count):
    return exchange(jnp.broadcast_to(value[None], (count,) + value.shape), axes)


def join_rows(layout, mine):
    other = swap_near(mine)
    high, middle, own = layout
    columns = mine.shape[-1]
    place = lax.broadcasted_iota(jnp.int32, (high, middle, 2, own, columns), 2)
    pick = lambda part: part.transpose(1, 0, 2, 3)[:, :, None]
    full = jnp.where(place == lax.axis_index("near"), pick(mine), pick(other))
    return lax.optimization_barrier(full).reshape(-1, columns)


def pair_sums(layout, side, outs, behind=None):
    give, keep = split_rows(layout, side, outs)
    sums = keep.astype(F32) + swap_near(give).astype(F32)
    if behind is not None:
        none = 0 * behind[:8, :128].astype(F32)
        sums = sums + jnp.pad(none, ((0, sums.shape[0] - 8), (0, sums.shape[1] - 128)))
    return sums.astype(BF)


def scatter(pair, axes):
    return lax.psum_scatter(pair, axes, scatter_dimension=0, tiled=True)


def to_plane(layout, pair):
    return exchange(pair.reshape(layout[1], -1, pair.shape[1]), MIDDLE)


def to_owner(layout, plane):
    return exchange(plane.reshape(layout[0], layout[2], -1), "hi")


def after(value, *others):
    return lax.optimization_barrier((value,) + others)[0]


def total(received, behind=None):
    sums = received[0].astype(F32)
    for part in range(1, received.shape[0]):
        sums = sums + received[part].astype(F32)
    if behind is not None:
        none = 0 * behind[:, : sums.shape[1]].astype(F32)
        sums = sums + jnp.pad(none, ((0, sums.shape[0] - none.shape[0]), (0, 0)))
    return sums


SUM_COLUMNS = ((10, 1), (11, 1), (5, 1), (3, 1), (4, 1), (6, CHUNKS), (2, 1), (0, 1), (1, 1))


def finish_parts(sums):
    half = lambda start, part: sums[:, start + part * HALF_D : start + (part + 1) * HALF_D]
    weights = [(half(0, part), half(3 * HALF_D, part)) for part in range(3)]
    turned = sums[:, 6 * HALF_D :].T
    return weights, [turned[start : start + count] for start, count in SUM_COLUMNS]


def finish_kernel(got_ref, *out_refs):
    weights, vectors = finish_parts(total(got_ref))
    for ref, (low, high) in zip(out_refs, weights):
        ref[:, :HALF_D] = low
        ref[:, HALF_D:] = high
    for ref, vector in zip(out_refs[3:], vectors):
        ref[...] = jnp.concatenate([vector[row : row + 1] for row in range(vector.shape[0])], axis=1)


def finish(received):
    own = received.shape[1]
    if own % 8:
        weights, vectors = finish_parts(total(received))
        weights = [jnp.concatenate(pair, axis=1) for pair in weights]
    else:
        out = pl.pallas_call(
            finish_kernel,
            out_shape=[jax.ShapeDtypeStruct((own, D), F32)] * 3
            + [jax.ShapeDtypeStruct((1, count * own), F32) for _, count in SUM_COLUMNS],
            compiler_params=params(),
            name="finish",
        )(received)
        weights, vectors = out[:3], out[3:]
    return weights, [vector.reshape(-1) for vector in vectors]


def body(sizes, tokens, cotangent, lengths, buckets, w_query, w_key, w_value, w_output, b_query, b_value,
         b_output, gain_attn, shift_attn, w_inner, b_inner, w_outer, b_outer, gain_ffn, shift_ffn):
    own = w_query.shape[0]
    ffn_weights = lax.all_gather(ffn_pack(w_inner, w_outer, w_output), AXES, axis=0, tiled=True)

    small = jnp.stack(
        [b_query, jnp.zeros_like(b_query), b_value, b_output, gain_attn, shift_attn, b_outer, gain_ffn, shift_ffn],
        axis=1,
    )
    small = jnp.concatenate([small, b_inner.reshape(CHUNKS, own).T], axis=1)
    small = jnp.pad(small, ((0, 0), (0, 128 - small.shape[1])))
    layout = (sizes["hi"], sizes["lo"] * sizes["far"], own)
    attn_pack = jnp.concatenate([w_query, w_key, w_value, small], axis=1)
    attn_mine = spread(spread(attn_pack, "hi", layout[0]), MIDDLE, layout[1])
    attn_weights = join_rows(layout, attn_mine)
    vecs = attn_weights[:, 3 * D : 3 * D + 16].astype(F32).T

    factor = jnp.where(buckets[0] == 0, 1, jnp.where(buckets[0] == 1, 2, 4)).astype(jnp.int32)
    limits = jnp.minimum(lengths, BLEN * factor).astype(jnp.int32)

    qkv, attended, lse = heads_forward(tokens, attn_weights, vecs, limits)
    near = lax.axis_index("near")
    side = near.astype(jnp.int32).reshape(1)
    (layer_out, normed_low, slope, branch, grad_second, unit_one, scale_one, sums_two), outer_grad = ffn_forward(
        layout, side, tokens, attended, cotangent, ffn_weights, vecs
    )
    outer_pair = pair_sums(layout, near, outer_grad)
    outer_got = to_plane(layout, outer_pair)
    (grad_first, attended_grad, sums_one, sums_inner), inner_grad = ffn_backward(
        layout, side, after(branch, outer_pair), slope, grad_second, unit_one, scale_one, normed_low, attended,
        ffn_weights, vecs
    )
    outer_got = after(outer_got, inner_grad[0])
    outer_plane = total(outer_got).astype(BF)
    inner_pair = pair_sums(layout, near, [after(part, outer_got) for part in inner_grad], outer_plane)
    inner_plane = scatter(inner_pair, MIDDLE)
    outer_got = to_owner(layout, outer_plane)
    attended_grad = after(attended_grad, inner_pair)
    low_grads, sums, low_grad = heads_backward(
        0, layout, side, qkv, attended_grad, lse, limits, tokens, (sums_two, sums_one, sums_inner)
    )
    outer_got = after(outer_got, low_grad[0])
    low_pair = pair_sums(layout, near, [after(part, outer_got) for part in low_grad])
    low_got = to_plane(layout, low_pair)
    high_grads, mark, high_grad = heads_backward(
        1, layout, side, qkv, after(attended_grad, low_pair), lse, limits, tokens, (sums,)
    )
    low_got = after(low_got, high_grad[0])
    inner_own = scatter(inner_plane.at[:16, :128].add(mark), "hi").astype(F32)
    high_pair = pair_sums(layout, near, [after(part, low_got) for part in high_grad])
    high_got = to_plane(layout, high_pair)
    grad_tokens = tokens_grad(after(grad_first, high_pair), low_grads, high_grads, attn_weights)
    high_got = after(high_got, grad_tokens)
    attn_plane = jnp.concatenate([total(low_got, inner_own).astype(BF), total(high_got).astype(BF)], axis=1)
    w_grads, vectors = finish(to_owner(layout, attn_plane))
    outer_own = total(outer_got)
    devices = D // own
    return (
        layer_out,
        grad_tokens,
        *w_grads,
        inner_own[:, FF:],
        *vectors[:5],
        inner_own[:, :FF].reshape(own, CHUNKS, devices, own).transpose(0, 2, 1, 3).reshape(own, FF),
        vectors[5],
        outer_own.reshape(own, CHUNKS, D).transpose(1, 0, 2).reshape(CHUNKS * own, D),
        *vectors[6:],
    )


def solution(mesh):
    wide, narrow = mesh.shape["wide"], mesh.shape["narrow"]
    sizes = {"hi": wide // 2, "lo": 2, "far": narrow // 2, "near": 2}
    split = jax.sharding.Mesh(mesh.devices.reshape([sizes[axis] for axis in AXES]), AXES)
    rows, vector = P(AXES, None), P(AXES)
    return jax.shard_map(
        partial(body, sizes),
        mesh=split,
        in_specs=(rows, rows, vector, vector) + (rows,) * 4 + (vector,) * 5
        + (rows, vector, rows, vector, vector, vector),
        out_specs=(rows,) * 6 + (vector,) * 5 + (rows, vector, rows, vector, vector, vector),
        check_vma=False,
    )
```
